32 devices in a mesh: gx: 8 (over y, x, core), gy: 4 (over z).
Axes of the slice: x: 2, y: 2, z: 4, core: 2. Of those that a mesh axis runs over, the one named last changes fastest.
Arguments:
- residual_in: float32 [112, 56, 336], P('gx', 'gy'), may hold values from -8 to 8
Outputs:
- correction: float32 [112, 56, 336], P('gx', 'gy')
- coarse_correction: float32 [16, 8, 48], P('gx', 'gy')
The draws below stay inside these ranges and needn't reach their ends.
All inputs are finite; a program needn't handle non-finite values.
Results may differ from the reference program's by a relative error of at most 0.0003.
Values sent between devices are 32-bit elements; how exact they have to be, the bound alone decides.
A program may use at most 64 MiB of HBM per device.

```python
import math
import jax
import jax.numpy as jnp
import numpy as np
from jax import lax

SWEEPS = 2
NX = 112
NY = 56
NZ = 336


def draw_residual_in(key, part):
    key = jax.random.fold_in(key, 5)
    return jax.random.truncated_normal(key, -6.0, 6.0, (NX, NY, NZ), jnp.float32)


def setup_inputs(seed: int = 0) -> dict:
    streams_of = jax.random.split(jax.random.key(seed), 2)
    return {
        "residual_in": draw_residual_in(jax.random.fold_in(streams_of[1], 71), 0),
    }


spectral_radius_bound = lax.Precision.HIGHEST
theta_cheb = 1.125
delta_cheb = 0.875
start_points = [-0.8717401485096066, -0.5917001814331423, -0.2092992179024789, 0.2092992179024789, 0.5917001814331423, 0.8717401485096066]

def legendre_pair(value):
    before, now = (1.0, value)
    for order in range(1, 7):
        before, now = (now, ((2 * order + 1) * value * now - order * before) / (order + 1))
    return (now, before)

def lobatto_tables():
    point_list = [-1.0]
    for guess in start_points:
        place = guess
        for newton in range(4):
            seventh, sixth = legendre_pair(place)
            slope = 7.0 * (place * seventh - sixth) / (place * place - 1.0)
            curve = (2.0 * place * slope - 56.0 * seventh) / (1.0 - place * place)
            place = place - slope / curve
        point_list.append(place)
    point_list.append(1.0)
    sample_nodes_list = np.array(point_list)
    values = np.array([legendre_pair(place)[0] for place in point_list])
    weights = 2.0 / (56.0 * values * values)
    derivative = np.zeros((8, 8))
    for i in range(8):
        for j in range(8):
            if i != j:
                derivative[i, j] = values[i] / (values[j] * (sample_nodes_list[i] - sample_nodes_list[j]))
    derivative[0, 0] = -14.0
    derivative[7, 7] = 14.0
    stiffness = derivative.T @ (weights[:, None] * derivative)
    return (sample_nodes_list, weights, stiffness)

def assemble(elements, stiffness, weights):
    width = 7 * elements + 1
    assembled = np.zeros((width, width))
    masses = np.zeros(width)
    for e in range(elements):
        assembled[7 * e:7 * e + 8, 7 * e:7 * e + 8] += stiffness
        masses[7 * e:7 * e + 8] += weights
    return (assembled, masses)

def mass_vector(elements, weights):
    masses = np.tile(weights[:7], elements)
    masses[7::7] += weights[7]
    return masses

def jacobi_eigen(matrix):
    order = matrix.shape[0]
    work = [[float(matrix[i, j]) for j in range(order)] for i in range(order)]
    vectors = [[1.0 if i == j else 0.0 for j in range(order)] for i in range(order)]
    for sweep in range(12):
        for p in range(order):
            for q in range(p + 1, order):
                angle = 0.5 * math.atan2(2.0 * work[p][q], work[q][q] - work[p][p])
                cosine = math.cos(angle)
                sine = math.sin(angle)
                for k in range(order):
                    left, right = (work[k][p], work[k][q])
                    work[k][p] = cosine * left - sine * right
                    work[k][q] = sine * left + cosine * right
                for k in range(order):
                    left, right = (work[p][k], work[q][k])
                    work[p][k] = cosine * left - sine * right
                    work[q][k] = sine * left + cosine * right
                for k in range(order):
                    left, right = (vectors[k][p], vectors[k][q])
                    vectors[k][p] = cosine * left - sine * right
                    vectors[k][q] = sine * left + cosine * right
    return (np.array([work[i][i] for i in range(order)]), np.array(vectors))

def schwarz_basis():
    sample_nodes_list, weights, stiffness = lobatto_tables()
    assembled, masses = assemble(3, stiffness, weights)
    block_stiff = assembled[6:16, 6:16]
    inv_root = 1.0 / np.sqrt(masses[6:16])
    eigen_vals, eigen_vecs = jacobi_eigen(inv_root[:, None] * block_stiff * inv_root[None, :])
    return (inv_root[:, None] * eigen_vecs, eigen_vals)

def sine_table(vertex, modes_in, elements):
    operator_output = vertex[:, None] * modes_in[None, :] % (2 * elements)
    angles = jnp.pi * modes_in.astype(jnp.float32) / elements
    entries = jnp.sqrt(2.0 / elements) * jnp.sin(jnp.pi * operator_output.astype(jnp.float32) / elements)
    entries = entries / jnp.sqrt((4.0 + 2.0 * jnp.cos(angles)) / 3.0)[None, :]
    return jnp.where(modes_in[None, :] > 0, entries, 0.0)

def coarse_eigen(modes_in, elements):
    angles = jnp.pi * modes_in.astype(jnp.float32) / elements
    return jnp.where(modes_in > 0, 3.0 * (1.0 - jnp.cos(angles)) / (4.0 + 2.0 * jnp.cos(angles)), 1.0)

def stiff_along(nodal, axis, stiffness):
    moved = jnp.moveaxis(nodal, axis, 0)
    elements = moved.shape[0] // 7
    trailing = moved.shape[1:]
    blocks = moved.reshape((elements, 7) + trailing)
    next_nodes = jnp.concatenate([moved[7::7], jnp.zeros((1,) + trailing, moved.dtype)], axis=0)
    stacked = jnp.concatenate([blocks, next_nodes[:, None]], axis=1)
    operator_output = jnp.einsum('ij,ej...->ei...', stiffness, stacked, precision=spectral_radius_bound)
    result = operator_output[:, :7]
    result = result.at[1:, 0].add(operator_output[:-1, 7])
    return jnp.moveaxis(result.reshape(moved.shape), 0, axis)

def operate(nodal, interior, stiffness, mass_x, mass_y, mass_z):
    summed = stiff_along(nodal, 0, stiffness) * mass_y[None, :, None] * mass_z[None, None, :]
    summed = summed + mass_x[:, None, None] * stiff_along(nodal, 1, stiffness) * mass_z[None, None, :]
    summed = summed + (mass_x[:, None] * mass_y[None, :])[:, :, None] * stiff_along(nodal, 2, stiffness)
    return interior * summed

def schwarz(nodal, interior, eigen_basis, eigen_vals):
    nodes_x, nodes_y, nodes_z = nodal.shape
    cells_horizontal, elems_y, element_tally_along_height = (nodes_x // 7, nodes_y // 7, nodes_z // 7)
    padded = jnp.pad(nodal, ((1, 2), (1, 2), (1, 2)))
    take_y = np.arange(elems_y)[:, None] * 7 + np.arange(10)[None, :]
    take_z = np.arange(element_tally_along_height)[:, None] * 7 + np.arange(10)[None, :]
    denominator = eigen_vals[:, None, None, None, None] + eigen_vals[None, None, :, None, None] + eigen_vals[None, None, None, None, :]
    kept_rows = eigen_basis[1:8]

    def one_slab(slab):
        block = lax.dynamic_slice_in_dim(padded, 7 * slab, 10, 0)
        block = block[:, take_y][:, :, :, take_z]
        coeffs = jnp.einsum('ma,mpnqo->apnqo', eigen_basis, block, precision=spectral_radius_bound)
        coeffs = jnp.einsum('nb,apnqo->apbqo', eigen_basis, coeffs, precision=spectral_radius_bound)
        coeffs = jnp.einsum('oc,apbqo->apbqc', eigen_basis, coeffs, precision=spectral_radius_bound)
        coeffs = coeffs / denominator
        coeffs = jnp.einsum('ma,apbqc->mpbqc', kept_rows, coeffs, precision=spectral_radius_bound)
        coeffs = jnp.einsum('nb,mpbqc->mpnqc', kept_rows, coeffs, precision=spectral_radius_bound)
        coeffs = jnp.einsum('oc,mpnqc->mpnqo', kept_rows, coeffs, precision=spectral_radius_bound)
        return coeffs.reshape(7, nodes_y, nodes_z)
    slabs = lax.map(one_slab, jnp.arange(cells_horizontal, dtype=jnp.int32))
    return interior * slabs.reshape(nodes_x, nodes_y, nodes_z)

def restrict_along(nodal, axis, sample_nodes_list):
    moved = jnp.moveaxis(nodal, axis, 0)
    elements = moved.shape[0] // 7
    trailing = moved.shape[1:]
    blocks = moved.reshape((elements, 7) + trailing)
    weight_low = jnp.asarray((1.0 - sample_nodes_list[:7]) / 2.0, jnp.float32)
    weight_high = jnp.asarray((1.0 + sample_nodes_list[:7]) / 2.0, jnp.float32)
    from_low = jnp.einsum('m,em...->e...', weight_low, blocks, precision=spectral_radius_bound)
    from_high = jnp.einsum('m,em...->e...', weight_high, blocks, precision=spectral_radius_bound)
    empty_matrix_line = jnp.zeros((1,) + trailing, moved.dtype)
    result = jnp.concatenate([from_low, empty_matrix_line], axis=0) + jnp.concatenate([empty_matrix_line, from_high], axis=0)
    return jnp.moveaxis(result, 0, axis)

def prolong_along(coarse, axis, sample_nodes_list):
    moved = jnp.moveaxis(coarse, axis, 0)
    elements = moved.shape[0] - 1
    trailing = moved.shape[1:]
    shape_w = (1, 7) + (1,) * len(trailing)
    weight_low = jnp.asarray((1.0 - sample_nodes_list[:7]) / 2.0, jnp.float32).reshape(shape_w)
    weight_high = jnp.asarray((1.0 + sample_nodes_list[:7]) / 2.0, jnp.float32).reshape(shape_w)
    result = weight_low * moved[:-1][:, None] + weight_high * moved[1:][:, None]
    return jnp.moveaxis(result.reshape((7 * elements,) + trailing), 0, axis)

def reference(residual_in):
    sample_nodes_list, weights, stiffness_np = lobatto_tables()
    basis_np, vals_np = schwarz_basis()
    stiffness = jnp.asarray(stiffness_np, jnp.float32)
    eigen_basis = jnp.asarray(basis_np, jnp.float32)
    eigen_vals = jnp.asarray(vals_np, jnp.float32)
    nodes_x, nodes_y, nodes_z = residual_in.shape
    cells_horizontal, elems_y, element_tally_along_height = (nodes_x // 7, nodes_y // 7, nodes_z // 7)
    mass_x = jnp.asarray(mass_vector(cells_horizontal, weights), jnp.float32)
    mass_y = jnp.asarray(mass_vector(elems_y, weights), jnp.float32)
    mass_z = jnp.asarray(mass_vector(element_tally_along_height, weights), jnp.float32)
    interior = ((jnp.arange(nodes_x) > 0)[:, None, None] & (jnp.arange(nodes_y) > 0)[None, :, None] & (jnp.arange(nodes_z) > 0)[None, None, :]).astype(jnp.float32)
    source = interior * residual_in
    sigma_ratio = theta_cheb / delta_cheb
    rho_now = 1.0 / sigma_ratio
    direction = schwarz(source, interior, eigen_basis, eigen_vals) / theta_cheb
    approx = direction
    remain = source - operate(direction, interior, stiffness, mass_x, mass_y, mass_z)
    for step in range(1, SWEEPS):
        rho_next = 1.0 / (2.0 * sigma_ratio - rho_now)
        direction = rho_next * rho_now * direction + 2.0 * rho_next / delta_cheb * schwarz(remain, interior, eigen_basis, eigen_vals)
        approx = approx + direction
        remain = remain - operate(direction, interior, stiffness, mass_x, mass_y, mass_z)
        rho_now = rho_next
    coarse_residual_vector = restrict_along(restrict_along(restrict_along(remain, 0, sample_nodes_list), 1, sample_nodes_list), 2, sample_nodes_list)
    coarse_residual_vector = coarse_residual_vector[:, :, :element_tally_along_height]
    first_axis_table = sine_table(jnp.arange(cells_horizontal + 1), jnp.arange(cells_horizontal), cells_horizontal)
    table_y = sine_table(jnp.arange(elems_y + 1), jnp.arange(elems_y), elems_y)
    table_z = sine_table(jnp.arange(element_tally_along_height), jnp.arange(element_tally_along_height), element_tally_along_height)
    mode_eigenvalues = jnp.einsum('wst,wo->ost', coarse_residual_vector, first_axis_table, precision=spectral_radius_bound)
    mode_eigenvalues = jnp.einsum('aqm,qb->abm', mode_eigenvalues, table_y, precision=spectral_radius_bound)
    mode_eigenvalues = jnp.einsum('abm,mk->abk', mode_eigenvalues, table_z, precision=spectral_radius_bound)
    denominator = coarse_eigen(jnp.arange(cells_horizontal), cells_horizontal)[:, None, None] + coarse_eigen(jnp.arange(elems_y), elems_y)[None, :, None] + coarse_eigen(jnp.arange(element_tally_along_height), element_tally_along_height)[None, None, :]
    scaled = mode_eigenvalues / denominator
    coarse_solution_vector = jnp.einsum('abk,mk->abm', scaled, table_z, precision=spectral_radius_bound)
    coarse_solution_vector = jnp.einsum('abm,qb->aqm', coarse_solution_vector, table_y, precision=spectral_radius_bound)
    coarse_solution_vector = jnp.einsum('bek,wb->wek', coarse_solution_vector, first_axis_table, precision=spectral_radius_bound)
    padded_sol = jnp.concatenate([coarse_solution_vector, jnp.zeros((cells_horizontal + 1, elems_y + 1, 1), jnp.float32)], axis=2)
    fine_level_portion = prolong_along(prolong_along(prolong_along(padded_sol, 2, sample_nodes_list), 1, sample_nodes_list), 0, sample_nodes_list)
    correction = approx + interior * fine_level_portion
    return (correction, coarse_solution_vector[:cells_horizontal, :elems_y, :])
```

```python
import functools
import math

import jax
import jax.numpy as jnp
import ml_dtypes
import numpy as np
from jax import lax
from jax.experimental import pallas as pl
from jax.experimental.pallas import tpu as pltpu
from jax.sharding import PartitionSpec as P

theta_cheb = 1.125
delta_cheb = 0.875
start_points = [
    -0.8717401485096066,
    -0.5917001814331423,
    -0.2092992179024789,
    0.2092992179024789,
    0.5917001814331423,
    0.8717401485096066,
]


def legendre_pair(value):
    before, now = (1.0, value)
    for order in range(1, 7):
        before, now = (now, ((2 * order + 1) * value * now - order * before) / (order + 1))
    return (now, before)


def lobatto_tables():
    point_list = [-1.0]
    for guess in start_points:
        place = guess
        for newton in range(4):
            seventh, sixth = legendre_pair(place)
            slope = 7.0 * (place * seventh - sixth) / (place * place - 1.0)
            curve = (2.0 * place * slope - 56.0 * seventh) / (1.0 - place * place)
            place = place - slope / curve
        point_list.append(place)
    point_list.append(1.0)
    sample_nodes_list = np.array(point_list)
    values = np.array([legendre_pair(place)[0] for place in point_list])
    weights = 2.0 / (56.0 * values * values)
    derivative = np.zeros((8, 8))
    for i in range(8):
        for j in range(8):
            if i != j:
                derivative[i, j] = values[i] / (
                    values[j] * (sample_nodes_list[i] - sample_nodes_list[j])
                )
    derivative[0, 0] = -14.0
    derivative[7, 7] = 14.0
    stiffness = derivative.T @ (weights[:, None] * derivative)
    return (sample_nodes_list, weights, stiffness)


def assemble(elements, stiffness, weights):
    width = 7 * elements + 1
    assembled = np.zeros((width, width))
    masses = np.zeros(width)
    for e in range(elements):
        assembled[7 * e : 7 * e + 8, 7 * e : 7 * e + 8] += stiffness
        masses[7 * e : 7 * e + 8] += weights
    return (assembled, masses)


def jacobi_eigen(matrix):
    order = matrix.shape[0]
    work = [[float(matrix[i, j]) for j in range(order)] for i in range(order)]
    vectors = [[1.0 if i == j else 0.0 for j in range(order)] for i in range(order)]
    for sweep in range(12):
        for p in range(order):
            for q in range(p + 1, order):
                angle = 0.5 * math.atan2(2.0 * work[p][q], work[q][q] - work[p][p])
                cosine = math.cos(angle)
                sine = math.sin(angle)
                for k in range(order):
                    left, right = (work[k][p], work[k][q])
                    work[k][p] = cosine * left - sine * right
                    work[k][q] = sine * left + cosine * right
                for k in range(order):
                    left, right = (work[p][k], work[q][k])
                    work[p][k] = cosine * left - sine * right
                    work[q][k] = sine * left + cosine * right
                for k in range(order):
                    left, right = (vectors[k][p], vectors[k][q])
                    vectors[k][p] = cosine * left - sine * right
                    vectors[k][q] = sine * left + cosine * right
    return (np.array([work[i][i] for i in range(order)]), np.array(vectors))


def schwarz_basis():
    sample_nodes_list, weights, stiffness = lobatto_tables()
    assembled, masses = assemble(3, stiffness, weights)
    block_stiff = assembled[6:16, 6:16]
    inv_root = 1.0 / np.sqrt(masses[6:16])
    eigen_vals, eigen_vecs = jacobi_eigen(inv_root[:, None] * block_stiff * inv_root[None, :])
    return (inv_root[:, None] * eigen_vecs, eigen_vals)


def injection_coefficients(elements, sample_nodes_list):
    matrix = np.zeros((elements + 1, 7 * elements))
    for e in range(elements):
        for m in range(7):
            matrix[e, 7 * e + m] += (1.0 - sample_nodes_list[m]) / 2.0
            matrix[e + 1, 7 * e + m] += (1.0 + sample_nodes_list[m]) / 2.0
    return matrix


MESH = pl.DeviceIdType.MESH
LANES = 64
DIRECTIONS = [(-1, 0), (1, 0), (0, -1), (0, 1), (-1, -1), (-1, 1), (1, -1), (1, 1)]


def round_up(value, unit):
    return -(-value // unit) * unit


def sine_np(vertices, elements):
    modes = np.arange(elements)
    vertex = np.asarray(vertices)[:, None]
    entries = np.sqrt(2.0 / elements) * np.sin(np.pi * (vertex * modes % (2 * elements)) / elements)
    entries = entries / np.sqrt((4.0 + 2.0 * np.cos(np.pi * modes / elements)) / 3.0)
    inside = (modes > 0) & (vertex > 0) & (vertex < elements)
    return np.where(inside, entries, 0.0)


def eigen_np(elements):
    modes = np.arange(elements)
    cosine = np.cos(np.pi * modes / elements)
    return np.where(modes > 0, 3.0 * (1.0 - cosine) / (4.0 + 2.0 * cosine), 1.0)


def split_np(matrix):
    high = matrix.astype(np.float32).astype(ml_dtypes.bfloat16)
    low = (matrix - high.astype(np.float64)).astype(np.float32).astype(ml_dtypes.bfloat16)
    return np.stack([high, low])


def pad_np(matrix, rows, columns, value=0.0):
    out = np.full((rows, columns), value)
    out[: matrix.shape[0], : matrix.shape[1]] = matrix
    return out


class Line:
    def __init__(self, elements, stiffness, weights, eigen_basis, points):
        self.elements = elements
        self.nodes = 7 * elements
        around, masses = assemble(elements + 4, stiffness, weights)
        self.around, self.masses, self.shift = around, masses, 14
        self.forward = np.zeros((10 * elements, self.nodes + 3))
        self.backward = np.zeros((self.nodes, 10 * elements))
        for e in range(elements):
            self.forward[10 * e : 10 * e + 10, 7 * e : 7 * e + 10] = eigen_basis.T
            self.backward[7 * e : 7 * e + 7, 10 * e : 10 * e + 10] = eigen_basis[1:8]
        hats = injection_coefficients(elements + 4, points)
        kept = slice(self.shift, self.shift + self.nodes)
        rows = slice(1, 1 + elements + 2)
        full = np.zeros((hats.shape[0], self.around.shape[0]))
        full[:, : hats.shape[1]] = hats
        self.hats = hats[rows, kept]
        self.hats_stiff = (full @ around)[rows, kept]
        self.hats_mass = (full * masses)[rows, kept]

    def stiff(self, i, j):
        return self.around[i + self.shift, j + self.shift]

    def mass(self, i):
        return self.masses[i + self.shift]

    def values(self, side):
        n = self.nodes
        return {-1: [-1], 0: list(range(n)), 1: [n, n + 1]}[side]

    def sums(self, side):
        n = self.nodes
        return {-1: [-1, 0], 0: [], 1: [n, n + 1]}[side]


def segments(lines, with_sums):
    line_x, line_y = lines
    out, start = [], 0
    for dx, dy in DIRECTIONS:
        rows = [("v", i, j) for i in line_x.values(dx) for j in line_y.values(dy)]
        if with_sums:
            rows += [("x", i, j) for i in line_x.sums(dx) for j in line_y.values(dy)]
            rows += [("y", i, j) for i in line_x.values(dx) for j in line_y.sums(dy)]
        size = round_up(len(rows), 8)
        out.append((start, size, rows))
        start += size
    return out, start


def tables(mesh_x, mesh_y, shape):
    points, weights, stiffness = lobatto_tables()
    eigen_basis, eigen_vals = schwarz_basis()
    nx, ny, nz = shape
    ex, ey, ez = nx // 7, ny // 7, nz // 7
    line_x = Line(ex, stiffness, weights, eigen_basis, points)
    line_y = Line(ey, stiffness, weights, eigen_basis, points)
    lines = (line_x, line_y)
    pitch = round_up(ny, 8)
    own_rows = round_up(nx * pitch, 128)
    zl = round_up(nz, 128)
    cl = round_up(10 * ez, 128)
    coefs = 100 * ex * ey
    own = lambda i, j: i * pitch + j
    own_list = [(i, j) for i in range(nx) for j in range(ny)]
    t = {}
    dims = dict(nx=nx, ny=ny, nz=nz, pitch=pitch, own_rows=own_rows, zl=zl, cl=cl, coefs=coefs)

    forward = lambda i, j: np.kron(line_x.forward[:, i + 1], line_y.forward[:, j + 1])
    seg_b, rows_b = segments(lines, False)
    seg_d, rows_d = segments(lines, True)
    dims.update(seg_b=[s[:2] for s in seg_b], rows_b=rows_b)
    dims.update(seg_d=[s[:2] for s in seg_d], rows_d=rows_d)

    pick = np.zeros((rows_b, own_rows))
    w_halo = np.zeros((coefs, rows_b))
    for (dx, dy), (start, size, rows) in zip(DIRECTIONS, seg_b):
        for r, (kind, i, j) in enumerate(rows):
            pick[start + r, own(i - nx * dx, j - ny * dy)] = 1.0
            w_halo[:, start + r] = forward(i, j)
    w_own = np.zeros((coefs, own_rows))
    back = np.zeros((own_rows, coefs))
    for i, j in own_list:
        w_own[:, own(i, j)] = forward(i, j)
        back[own(i, j)] = np.kron(line_x.backward[i], line_y.backward[j])
    t["pick"] = pick.astype(ml_dtypes.bfloat16)
    t["w_own"], t["w_halo"], t["back"] = split_np(w_own), split_np(w_halo), split_np(back)

    z_fwd = np.zeros((zl, cl))
    z_back = np.zeros((cl, zl))
    for e in range(ez):
        for m in range(10):
            z = 7 * e - 1 + m
            if 0 <= z < nz:
                z_fwd[z, 10 * e : 10 * e + 10] = eigen_basis[m]
                if 1 <= m <= 7 and z > 0:
                    z_back[10 * e : 10 * e + 10, z] = eigen_basis[m]
    t["z_fwd"], t["z_back"] = split_np(z_fwd), split_np(z_back)
    l_x, l_y = np.tile(eigen_vals, ex), np.tile(eigen_vals, ey)
    t["l_xy"] = (l_x[:, None] + l_y[None, :]).reshape(coefs, 1).astype(np.float32)
    l_z = np.ones((1, cl))
    l_z[0, : 10 * ez] = np.tile(eigen_vals, ez)
    t["l_z"] = l_z.astype(np.float32)

    send = np.zeros((rows_d, own_rows))
    wide_y = ny + 3
    points_rows = round_up((nx + 3) * wide_y, 16)
    target = lambda i, j: (i + 1) * wide_y + (j + 1)
    inside_x = lambda i: -1 <= i <= nx + 1
    inside_y = lambda j: -1 <= j <= ny + 1
    dims["points_rows"], dims["wide_y"] = points_rows, wide_y
    lap_own = np.zeros((2 * points_rows, own_rows))
    lap_halo = np.zeros((2 * points_rows, rows_d))

    def value_column(column, i, j, dx, dy):
        for k in range(-1, nx + 2):
            if k not in line_x.sums(dx):
                column[target(k, j)] += line_x.stiff(k, i) * line_y.mass(j)
        for k in range(-1, ny + 2):
            if k not in line_y.sums(dy):
                column[target(i, k)] += line_y.stiff(k, j) * line_x.mass(i)
        column[points_rows + target(i, j)] += line_x.mass(i) * line_y.mass(j)

    for i, j in own_list:
        value_column(lap_own[:, own(i, j)], i, j, 0, 0)
    for (dx, dy), (start, size, rows) in zip(DIRECTIONS, seg_d):
        for r, (kind, i, j) in enumerate(rows):
            p, q = i - nx * dx, j - ny * dy
            if kind == "v":
                send[start + r, own(p, q)] = 1.0
                value_column(lap_halo[:, start + r], i, j, dx, dy)
            elif kind == "x":
                for k in range(nx):
                    send[start + r, own(k, q)] = line_x.stiff(p, k)
                lap_halo[target(i, j), start + r] += line_y.mass(j)
            else:
                for k in range(ny):
                    send[start + r, own(p, k)] = line_y.stiff(q, k)
                lap_halo[target(i, j), start + r] += line_x.mass(i)
    w_all = np.zeros((coefs, points_rows))
    for i in range(-1, nx + 2):
        for j in range(-1, ny + 2):
            w_all[:, target(i, j)] = forward(i, j)
    t["send"], t["lap_own"], t["lap_halo"] = split_np(send), split_np(lap_own), split_np(lap_halo)
    t["w_all"] = split_np(w_all)
    stiff_z, mass_z = assemble(ez, stiffness, weights)
    stiff_z = stiff_z[:nz, :nz]
    t["stiff_z"] = split_np(pad_np(stiff_z, zl, zl))
    t["mass_z"] = pad_np(mass_z[None, :nz], 1, zl).astype(np.float32)

    count_x, count_y = mesh_x * ex, mesh_y * ey
    vx, vy = ex + 2, ey + 2
    dims.update(vy=vy, count_x=count_x, lanes=count_y * LANES)
    coarse = np.zeros((3, 8 * vy, own_rows))
    for i, j in own_list:
        for w in range(vy):
            for v in range(vx):
                row = 8 * w + v
                coarse[0, row, own(i, j)] = line_x.hats[v, i] * line_y.hats[w, j]
                coarse[1, row, own(i, j)] = (
                    line_x.hats_stiff[v, i] * line_y.hats_mass[w, j]
                    + line_x.hats_mass[v, i] * line_y.hats_stiff[w, j]
                )
                coarse[2, row, own(i, j)] = line_x.hats_mass[v, i] * line_y.hats_mass[w, j]
    t["coarse_b"] = split_np(coarse[0])
    t["coarse_x"] = split_np(np.concatenate([coarse[1], coarse[2]]))
    hats_z = injection_coefficients(ez, points)[:ez]
    phi_z = sine_np(np.arange(ez), ez)
    to_modes = pad_np(hats_z.T @ phi_z, zl, LANES)
    to_modes[0] = 0.0
    stiff_modes = pad_np(stiff_z @ to_modes[:nz, :ez], zl, LANES)
    mass_modes = to_modes
    t["to_modes"] = split_np(np.tile(mass_modes, (1, count_y)))
    t["to_modes_k"] = split_np(np.tile(stiff_modes, (1, count_y)))
    y_in = np.zeros((mesh_y, 8 * vy, count_y * LANES))
    y_out = np.zeros((mesh_y, 8 * (ey + 1), count_y * LANES))
    for p in range(mesh_y):
        y_in[p] = np.repeat(np.repeat(sine_np(p * ey - 1 + np.arange(vy), count_y), 8, 0), LANES, 1)
        y_out[p] = np.repeat(np.repeat(sine_np(p * ey + np.arange(ey + 1), count_y), 8, 0), LANES, 1)
    t["y_in"], t["y_out"] = y_in.astype(np.float32), y_out.astype(np.float32)
    x_in = np.zeros((count_x, mesh_x, 8))
    x_out = np.zeros((mesh_x, 8, count_x))
    for p in range(mesh_x):
        x_in[:, p, :vx] = sine_np(p * ex - 1 + np.arange(vx), count_x).T
        x_out[p, : ex + 1] = sine_np(p * ex + np.arange(ex + 1), count_x)
    t["x_in"] = x_in.reshape(count_x, mesh_x * 8).astype(np.float32)
    t["x_out"] = x_out.astype(np.float32)
    mu = np.ones((count_x, count_y, LANES))
    mu[:, :, :ez] = (
        eigen_np(count_x)[:, None, None] + eigen_np(count_y)[None, :, None] + eigen_np(ez)
    )
    t["mu"] = mu.reshape(count_x, count_y * LANES).astype(np.float32)
    z_out = np.zeros((LANES, zl + 128))
    z_out[:ez, :nz] = phi_z.T @ hats_z
    z_out[:, 0] = 0.0
    z_out[:ez, zl : zl + ez] = phi_z.T
    t["z_out"] = split_np(np.tile(z_out, (count_y, 1)))
    spread = np.zeros((own_rows, 8 * (ey + 1)))
    hats_x, hats_y = line_x.hats[1:], line_y.hats[1:]
    for i, j in own_list:
        for q in range(ey + 1):
            for p in range(ex + 1):
                spread[own(i, j), 8 * q + p] = hats_x[p, i] * hats_y[q, j]
    t["spread"] = split_np(spread)
    return t, dims


def halves(value):
    high = value.astype(jnp.bfloat16)
    return high, (value - high.astype(jnp.float32)).astype(jnp.bfloat16)


def mm(a, b):
    return jnp.dot(a, b, preferred_element_type=jnp.float32)


def left(table, parts):
    high, low = parts
    return mm(table[0], high) + (mm(table[0], low) + mm(table[1], high))


def right(parts, table):
    high, low = parts
    return mm(high, table[0]) + (mm(high, table[1]) + mm(low, table[0]))


def exact(a, b):
    return jnp.dot(a, b, precision=lax.Precision.HIGHEST, preferred_element_type=jnp.float32)


def kernel(names, dims, mesh_x, mesh_y, residual, *refs):
    t = dict(zip(names, refs[: len(names)]))
    (fine_out, coarse_out, own, out_b, in_b, out_d, in_d, out_y, in_y, out_x, in_x,
     sent, got, sent_y, got_y, sent_x, got_x) = refs[len(names):]
    nx, ny, nz, pitch = dims["nx"], dims["ny"], dims["nz"], dims["pitch"]
    own_rows, zl = dims["own_rows"], dims["zl"]
    ix, iy = lax.axis_index("gx"), lax.axis_index("gy")

    def exists(dx, dy):
        return (ix + dx >= 0) & (ix + dx < mesh_x) & (iy + dy >= 0) & (iy + dy < mesh_y)

    own[...] = jnp.zeros_like(own)
    in_b[...] = jnp.zeros_like(in_b)
    in_d[...] = jnp.zeros_like(in_d)
    barrier = pltpu.get_barrier_semaphore()
    for o in range(1, mesh_x):
        pl.semaphore_signal(
            barrier, inc=1, device_id=(lax.rem(ix + o, mesh_x), iy), device_id_type=MESH
        )
    for o in range(1, mesh_y):
        pl.semaphore_signal(
            barrier, inc=1, device_id=(ix, lax.rem(iy + o, mesh_y)), device_id_type=MESH
        )
    corners = DIRECTIONS[4:]
    for dx, dy in corners:
        @pl.when(exists(dx, dy))
        def _():
            pl.semaphore_signal(barrier, inc=1, device_id=(ix + dx, iy + dy), device_id_type=MESH)

    row = lax.broadcasted_iota(jnp.int32, (own_rows, 1), 0)
    node_x, node_y = ix * nx + row // pitch, iy * ny + row % pitch
    keep = ((node_x > 0) & (node_y > 0) & (row % pitch < ny) & (row // pitch < nx)).astype(
        jnp.float32
    )
    keep_z = (lax.broadcasted_iota(jnp.int32, (1, nz), 1) > 0).astype(jnp.float32)
    for i in range(nx):
        own[i * pitch : i * pitch + ny, 0:nz] = residual[i] * keep_z
    source = halves(own[...] * keep)
    out_b[...] = mm(t["pick"][...], source[0]) + mm(t["pick"][...], source[1])

    greetings = mesh_x - 1 + mesh_y - 1
    for dx, dy in corners:
        greetings = greetings + exists(dx, dy).astype(jnp.int32)
    pl.semaphore_wait(barrier, greetings)

    def halo(phase, src, dst, places):
        copies = []
        for d, (dx, dy) in enumerate(DIRECTIONS):
            start, size = places[d]
            copies.append(
                pltpu.make_async_remote_copy(
                    src_ref=src.at[pl.ds(start, size)],
                    dst_ref=dst.at[pl.ds(start, size)],
                    send_sem=sent.at[phase, d],
                    recv_sem=got.at[phase, d],
                    device_id=(ix - dx, iy - dy),
                    device_id_type=MESH,
                )
            )
        for d, (dx, dy) in enumerate(DIRECTIONS):
            pl.when(exists(-dx, -dy))(copies[d].start)
        return copies

    def arrived(copies):
        for d, (dx, dy) in enumerate(DIRECTIONS):
            pl.when(exists(dx, dy))(copies[d].wait_recv)

    def left_here(copies):
        for d, (dx, dy) in enumerate(DIRECTIONS):
            pl.when(exists(-dx, -dy))(copies[d].wait_send)

    def solve(coefs):
        modes = right(halves(coefs), t["z_fwd"])
        modes = modes / (t["l_xy"][...] + t["l_z"][...])
        modes = left(t["back"], halves(modes))
        return right(halves(modes), t["z_back"]) * keep

    copies_b = halo(0, out_b, in_b, dims["seg_b"])
    coefs = left(t["w_own"], source)
    coarse_b = left(t["coarse_b"], source)
    arrived(copies_b)
    coefs = coefs + left(t["w_halo"], halves(in_b[...]))
    first = solve(coefs) * (1.0 / theta_cheb)

    parts = halves(first)
    out_d[...] = left(t["send"], parts)
    copies_d = halo(1, out_d, in_d, dims["seg_d"])
    applied = left(t["lap_own"], parts)
    arrived(copies_d)
    applied = applied + left(t["lap_halo"], halves(in_d[...]))
    rows, wide_y = dims["points_rows"], dims["wide_y"]
    spot = lax.broadcasted_iota(jnp.int32, (rows, 1), 0)
    spot_x, spot_y = ix * nx + spot // wide_y - 1, iy * ny + spot % wide_y - 1
    inside = (spot_x > 0) & (spot_x < mesh_x * nx) & (spot_y > 0) & (spot_y < mesh_y * ny)
    lane = lax.broadcasted_iota(jnp.int32, (1, zl), 1)
    inside = (inside & (lane > 0) & (lane < nz)).astype(jnp.float32)
    applied = applied[:rows] * t["mass_z"][...] + right(halves(applied[rows:]), t["stiff_z"])
    coefs = coefs - left(t["w_all"], halves(applied * inside))
    sigma = theta_cheb / delta_cheb
    rho_0 = 1.0 / sigma
    rho_1 = 1.0 / (2.0 * sigma - rho_0)
    total = (1.0 + rho_1 * rho_0) * first + (2.0 * rho_1 / delta_cheb) * solve(coefs)

    vy = dims["vy"]
    parts = left(t["coarse_x"], halves(total))
    parts_b = coarse_b - parts[: 8 * vy] * t["mass_z"][...]
    share = right(halves(parts_b), t["to_modes"]) - right(halves(parts[8 * vy :]), t["to_modes_k"])
    share = share * t["y_in"][iy]
    share = sum(share[8 * w : 8 * w + 8] for w in range(vy))

    def everyone(value, src, dst, count, me, send_sems, recv_sems, place):
        src[...] = value
        copies = []
        for o in range(1, count):
            to = lax.rem(me + o, count)
            copies.append(
                pltpu.make_async_remote_copy(
                    src_ref=src,
                    dst_ref=dst.at[me],
                    send_sem=send_sems.at[o],
                    recv_sem=recv_sems.at[o],
                    device_id=place(to),
                    device_id_type=MESH,
                )
            )
        for copy in copies:
            copy.start()
        dst[me] = value
        for copy in copies:
            copy.wait_recv()
        return copies

    copies_y = everyone(
        share, out_y, in_y, mesh_y, iy, sent_y, got_y, lambda to: (ix, to)
    )
    share = sum(in_y[p] for p in range(mesh_y))
    copies_x = everyone(
        share, out_x, in_x, mesh_x, ix, sent_x, got_x, lambda to: (to, iy)
    )
    gathered = in_x[...].reshape(mesh_x * 8, dims["lanes"])
    modes = exact(t["x_in"][...], gathered) / t["mu"][...]
    lines = exact(t["x_out"][ix], modes)
    y_out = t["y_out"][iy]
    lines = jnp.concatenate([lines] * (y_out.shape[0] // 8), axis=0) * y_out
    nodes = right(halves(lines), t["z_out"])
    ex, ey, ez = nx // 7, ny // 7, nz // 7
    for p in range(ex):
        for q in range(ey):
            coarse_out[p, q : q + 1, :] = nodes[8 * q + p : 8 * q + p + 1, zl : zl + ez]
    result = total + left(t["spread"], halves(nodes[:, :zl])) * keep
    for i in range(nx):
        fine_out[i] = result[i * pitch : i * pitch + ny, :nz]
    left_here(copies_b)
    left_here(copies_d)
    for copy in copies_y + copies_x:
        copy.wait_send()


def per_device(mesh_x, mesh_y, residual_in):
    t, dims = tables(mesh_x, mesh_y, residual_in.shape)
    names = list(t)
    nx, ny, nz = residual_in.shape
    own_rows, zl, lanes = dims["own_rows"], dims["zl"], dims["lanes"]
    f32 = jnp.float32
    vmem = pl.BlockSpec(memory_space=pltpu.VMEM)
    return pl.pallas_call(
        functools.partial(kernel, names, dims, mesh_x, mesh_y),
        out_shape=(
            jax.ShapeDtypeStruct((nx, ny, nz), f32),
            jax.ShapeDtypeStruct((nx // 7, ny // 7, nz // 7), f32),
        ),
        in_specs=[vmem] * (1 + len(names)),
        out_specs=(vmem, vmem),
        scratch_shapes=[
            pltpu.VMEM((own_rows, zl), f32),
            pltpu.VMEM((dims["rows_b"], zl), f32),
            pltpu.VMEM((dims["rows_b"], zl), f32),
            pltpu.VMEM((dims["rows_d"], zl), f32),
            pltpu.VMEM((dims["rows_d"], zl), f32),
            pltpu.VMEM((8, lanes), f32),
            pltpu.VMEM((mesh_y, 8, lanes), f32),
            pltpu.VMEM((8, lanes), f32),
            pltpu.VMEM((mesh_x, 8, lanes), f32),
            pltpu.SemaphoreType.DMA((2, 8)),
            pltpu.SemaphoreType.DMA((2, 8)),
            pltpu.SemaphoreType.DMA((mesh_y,)),
            pltpu.SemaphoreType.DMA((mesh_y,)),
            pltpu.SemaphoreType.DMA((mesh_x,)),
            pltpu.SemaphoreType.DMA((mesh_x,)),
        ],
        compiler_params=pltpu.CompilerParams(
            collective_id=0, has_side_effects=True, vmem_limit_bytes=56 * 2**20
        ),
        cost_estimate=pl.CostEstimate(flops=10**9, bytes_accessed=10**7, transcendentals=0),
    )(residual_in, *[jnp.asarray(t[name]) for name in names])


def solution(mesh):
    return jax.shard_map(
        functools.partial(per_device, mesh.shape["gx"], mesh.shape["gy"]),
        mesh=mesh,
        in_specs=(P("gx", "gy", None),),
        out_specs=(P("gx", "gy", None), P("gx", "gy", None)),
        check_vma=False,
    )
```

```python
import functools
import math

import jax
import jax.numpy as jnp
import ml_dtypes
import numpy as np
from jax import lax
from jax.experimental import pallas as pl
from jax.experimental.pallas import tpu as pltpu
from jax.sharding import PartitionSpec as P

theta_cheb = 1.125
delta_cheb = 0.875
start_points = [
    -0.8717401485096066,
    -0.5917001814331423,
    -0.2092992179024789,
    0.2092992179024789,
    0.5917001814331423,
    0.8717401485096066,
]


def legendre_pair(value):
    before, now = (1.0, value)
    for order in range(1, 7):
        before, now = (now, ((2 * order + 1) * value * now - order * before) / (order + 1))
    return (now, before)


def lobatto_tables():
    point_list = [-1.0]
    for guess in start_points:
        place = guess
        for newton in range(4):
            seventh, sixth = legendre_pair(place)
            slope = 7.0 * (place * seventh - sixth) / (place * place - 1.0)
            curve = (2.0 * place * slope - 56.0 * seventh) / (1.0 - place * place)
            place = place - slope / curve
        point_list.append(place)
    point_list.append(1.0)
    sample_nodes_list = np.array(point_list)
    values = np.array([legendre_pair(place)[0] for place in point_list])
    weights = 2.0 / (56.0 * values * values)
    derivative = np.zeros((8, 8))
    for i in range(8):
        for j in range(8):
            if i != j:
                derivative[i, j] = values[i] / (
                    values[j] * (sample_nodes_list[i] - sample_nodes_list[j])
                )
    derivative[0, 0] = -14.0
    derivative[7, 7] = 14.0
    stiffness = derivative.T @ (weights[:, None] * derivative)
    return (sample_nodes_list, weights, stiffness)


def assemble(elements, stiffness, weights):
    width = 7 * elements + 1
    assembled = np.zeros((width, width))
    masses = np.zeros(width)
    for e in range(elements):
        assembled[7 * e : 7 * e + 8, 7 * e : 7 * e + 8] += stiffness
        masses[7 * e : 7 * e + 8] += weights
    return (assembled, masses)


def jacobi_eigen(matrix):
    order = matrix.shape[0]
    work = [[float(matrix[i, j]) for j in range(order)] for i in range(order)]
    vectors = [[1.0 if i == j else 0.0 for j in range(order)] for i in range(order)]
    for sweep in range(12):
        for p in range(order):
            for q in range(p + 1, order):
                angle = 0.5 * math.atan2(2.0 * work[p][q], work[q][q] - work[p][p])
                cosine = math.cos(angle)
                sine = math.sin(angle)
                for k in range(order):
                    left, right = (work[k][p], work[k][q])
                    work[k][p] = cosine * left - sine * right
                    work[k][q] = sine * left + cosine * right
                for k in range(order):
                    left, right = (work[p][k], work[q][k])
                    work[p][k] = cosine * left - sine * right
                    work[q][k] = sine * left + cosine * right
                for k in range(order):
                    left, right = (vectors[k][p], vectors[k][q])
                    vectors[k][p] = cosine * left - sine * right
                    vectors[k][q] = sine * left + cosine * right
    return (np.array([work[i][i] for i in range(order)]), np.array(vectors))


def schwarz_basis():
    sample_nodes_list, weights, stiffness = lobatto_tables()
    assembled, masses = assemble(3, stiffness, weights)
    block_stiff = assembled[6:16, 6:16]
    inv_root = 1.0 / np.sqrt(masses[6:16])
    eigen_vals, eigen_vecs = jacobi_eigen(inv_root[:, None] * block_stiff * inv_root[None, :])
    return (inv_root[:, None] * eigen_vecs, eigen_vals)


def injection_coefficients(elements, sample_nodes_list):
    matrix = np.zeros((elements + 1, 7 * elements))
    for e in range(elements):
        for m in range(7):
            matrix[e, 7 * e + m] += (1.0 - sample_nodes_list[m]) / 2.0
            matrix[e + 1, 7 * e + m] += (1.0 + sample_nodes_list[m]) / 2.0
    return matrix


MESH = pl.DeviceIdType.MESH
LANES = 64
DIRECTIONS = [(-1, 0), (1, 0), (0, -1), (0, 1), (-1, -1), (-1, 1), (1, -1), (1, 1)]


def round_up(value, unit):
    return -(-value // unit) * unit


def sine_np(vertices, elements):
    modes = np.arange(elements)
    vertex = np.asarray(vertices)[:, None]
    entries = np.sqrt(2.0 / elements) * np.sin(np.pi * (vertex * modes % (2 * elements)) / elements)
    entries = entries / np.sqrt((4.0 + 2.0 * np.cos(np.pi * modes / elements)) / 3.0)
    inside = (modes > 0) & (vertex > 0) & (vertex < elements)
    return np.where(inside, entries, 0.0)


def eigen_np(elements):
    modes = np.arange(elements)
    cosine = np.cos(np.pi * modes / elements)
    return np.where(modes > 0, 3.0 * (1.0 - cosine) / (4.0 + 2.0 * cosine), 1.0)


def split_np(matrix, axis):
    high = matrix.astype(np.float32).astype(ml_dtypes.bfloat16)
    low = (matrix - high.astype(np.float64)).astype(np.float32).astype(ml_dtypes.bfloat16)
    return np.concatenate([high, high, low], axis=axis)


def lhs_np(matrix):
    return split_np(pad_np(matrix, round_up(matrix.shape[0], 16), matrix.shape[1]), 1)


def rhs_np(matrix):
    return split_np(matrix, 0)


def pad_np(matrix, rows, columns, value=0.0):
    out = np.full((rows, columns), value)
    out[: matrix.shape[0], : matrix.shape[1]] = matrix
    return out


class Line:
    def __init__(self, elements, stiffness, weights, eigen_basis, points):
        self.elements = elements
        self.nodes = 7 * elements
        around, masses = assemble(elements + 4, stiffness, weights)
        self.around, self.masses, self.shift = around, masses, 14
        self.forward = np.zeros((10 * elements, self.nodes + 3))
        self.backward = np.zeros((self.nodes, 10 * elements))
        for e in range(elements):
            self.forward[10 * e : 10 * e + 10, 7 * e : 7 * e + 10] = eigen_basis.T
            self.backward[7 * e : 7 * e + 7, 10 * e : 10 * e + 10] = eigen_basis[1:8]
        hats = injection_coefficients(elements + 4, points)
        kept = slice(self.shift, self.shift + self.nodes)
        rows = slice(1, 1 + elements + 2)
        full = np.zeros((hats.shape[0], self.around.shape[0]))
        full[:, : hats.shape[1]] = hats
        self.hats = hats[rows, kept]
        self.hats_stiff = (full @ around)[rows, kept]
        self.hats_mass = (full * masses)[rows, kept]

    def stiff(self, i, j):
        return self.around[i + self.shift, j + self.shift]

    def mass(self, i):
        return self.masses[i + self.shift]

    def values(self, side):
        n = self.nodes
        return {-1: [-1], 0: list(range(n)), 1: [n, n + 1]}[side]

    def sums(self, side):
        n = self.nodes
        return {-1: [-1, 0], 0: [], 1: [n, n + 1]}[side]


def segments(lines, with_sums):
    line_x, line_y = lines
    out, start = [], 0
    for dx, dy in DIRECTIONS:
        rows = [("v", i, j) for i in line_x.values(dx) for j in line_y.values(dy)]
        if with_sums:
            rows += [("x", i, j) for i in line_x.sums(dx) for j in line_y.values(dy)]
            rows += [("y", i, j) for i in line_x.values(dx) for j in line_y.sums(dy)]
        size = round_up(len(rows), 8)
        out.append((start, size, rows))
        start += size
    return out, start


def tables(mesh_x, mesh_y, shape):
    points, weights, stiffness = lobatto_tables()
    eigen_basis, eigen_vals = schwarz_basis()
    nx, ny, nz = shape
    ex, ey, ez = nx // 7, ny // 7, nz // 7
    line_x = Line(ex, stiffness, weights, eigen_basis, points)
    line_y = Line(ey, stiffness, weights, eigen_basis, points)
    lines = (line_x, line_y)
    pitch = round_up(ny, 8)
    own_rows = round_up(nx * pitch, 128)
    zl = round_up(nz, 128)
    cl = round_up(10 * ez, 128)
    coefs = 100 * ex * ey
    own = lambda i, j: i * pitch + j
    own_list = [(i, j) for i in range(nx) for j in range(ny)]
    t = {}
    dims = dict(nx=nx, ny=ny, nz=nz, pitch=pitch, own_rows=own_rows, zl=zl, cl=cl, coefs=coefs)

    forward = lambda i, j: np.kron(line_x.forward[:, i + 1], line_y.forward[:, j + 1])
    seg_b, rows_b = segments(lines, False)
    seg_d, rows_d = segments(lines, True)
    rows_d = round_up(rows_d, 16)
    dims.update(seg_b=[s[:2] for s in seg_b], rows_b=rows_b)
    dims.update(seg_d=[s[:2] for s in seg_d], rows_d=rows_d)

    pick = np.zeros((rows_b, own_rows))
    w_halo = np.zeros((coefs, rows_b))
    for (dx, dy), (start, size, rows) in zip(DIRECTIONS, seg_b):
        for r, (kind, i, j) in enumerate(rows):
            pick[start + r, own(i - nx * dx, j - ny * dy)] = 1.0
            w_halo[:, start + r] = forward(i, j)
    w_own = np.zeros((coefs, own_rows))
    back = np.zeros((own_rows, coefs))
    for i, j in own_list:
        w_own[:, own(i, j)] = forward(i, j)
        back[own(i, j)] = np.kron(line_x.backward[i], line_y.backward[j])
    z_fwd = np.zeros((zl, cl))
    z_back = np.zeros((cl, zl))
    for e in range(ez):
        for m in range(10):
            z = 7 * e - 1 + m
            if 0 < z < nz:
                z_fwd[z, 10 * e : 10 * e + 10] = eigen_basis[m]
                if 1 <= m <= 7:
                    z_back[10 * e : 10 * e + 10, z] = eigen_basis[m]
    l_x, l_y = np.tile(eigen_vals, ex), np.tile(eigen_vals, ey)
    l_z = np.ones(cl)
    l_z[: 10 * ez] = np.tile(eigen_vals, ez)
    inverse = 1.0 / ((l_x[:, None] + l_y[None, :]).reshape(coefs, 1) + l_z)
    t["z_fwd"] = rhs_np(z_fwd)
    t["pick"] = pick.astype(ml_dtypes.bfloat16)
    t["w_own"] = lhs_np(w_own)
    t["coarse_b"] = None
    t["to_modes"] = None
    t["w_halo"] = lhs_np(w_halo)
    t["inverse"] = inverse.astype(np.float32)
    t["back"], t["z_back"] = lhs_np(back), rhs_np(z_back)

    send = np.zeros((rows_d, own_rows))
    wide_y = ny + 3
    points_rows = round_up((nx + 3) * wide_y, 16)
    target = lambda i, j: (i + 1) * wide_y + (j + 1)
    inside_x = lambda i: -1 <= i <= nx + 1
    inside_y = lambda j: -1 <= j <= ny + 1
    dims["points_rows"], dims["wide_y"] = points_rows, wide_y
    lap_own = np.zeros((2 * points_rows, own_rows))
    lap_halo = np.zeros((2 * points_rows, rows_d))

    def value_column(column, i, j, dx, dy):
        for k in range(-1, nx + 2):
            if k not in line_x.sums(dx):
                column[target(k, j)] += line_x.stiff(k, i) * line_y.mass(j)
        for k in range(-1, ny + 2):
            if k not in line_y.sums(dy):
                column[target(i, k)] += line_y.stiff(k, j) * line_x.mass(i)
        column[points_rows + target(i, j)] += line_x.mass(i) * line_y.mass(j)

    for i, j in own_list:
        value_column(lap_own[:, own(i, j)], i, j, 0, 0)
    for (dx, dy), (start, size, rows) in zip(DIRECTIONS, seg_d):
        for r, (kind, i, j) in enumerate(rows):
            p, q = i - nx * dx, j - ny * dy
            if kind == "v":
                send[start + r, own(p, q)] = 1.0
                value_column(lap_halo[:, start + r], i, j, dx, dy)
            elif kind == "x":
                for k in range(nx):
                    send[start + r, own(k, q)] = line_x.stiff(p, k)
                lap_halo[target(i, j), start + r] += line_y.mass(j)
            else:
                for k in range(ny):
                    send[start + r, own(p, k)] = line_y.stiff(q, k)
                lap_halo[target(i, j), start + r] += line_x.mass(i)
    w_all = np.zeros((coefs, points_rows))
    for i in range(-1, nx + 2):
        for j in range(-1, ny + 2):
            w_all[:, target(i, j)] = forward(i, j)
    t["send"], t["lap_own"], t["lap_halo"] = lhs_np(send), lhs_np(lap_own), lhs_np(lap_halo)
    stiff_z, mass_z = assemble(ez, stiffness, weights)
    stiff_z = pad_np(stiff_z[:nz, :nz], zl, zl)
    mass_z = np.diag(pad_np(mass_z[None, :nz], 1, zl)[0])
    t["z_lap"] = rhs_np(np.concatenate([mass_z @ z_fwd, stiff_z @ z_fwd]))
    t["w_all"] = lhs_np(w_all)

    count_x, count_y = mesh_x * ex, mesh_y * ey
    vx, vy = ex + 2, ey + 2
    dims.update(vy=vy, count_x=count_x, lanes=count_y * LANES)
    coarse = np.zeros((3, 8 * vy, own_rows))
    for i, j in own_list:
        for w in range(vy):
            for v in range(vx):
                row = 8 * w + v
                coarse[0, row, own(i, j)] = line_x.hats[v, i] * line_y.hats[w, j]
                coarse[1, row, own(i, j)] = (
                    line_x.hats_stiff[v, i] * line_y.hats_mass[w, j]
                    + line_x.hats_mass[v, i] * line_y.hats_stiff[w, j]
                )
                coarse[2, row, own(i, j)] = line_x.hats_mass[v, i] * line_y.hats_mass[w, j]
    t["coarse_b"] = lhs_np(coarse[0])
    coarse_m = []
    for first_x in (0, 1):
        for first_y in (0, 1):
            masked = back.copy()
            for i, j in own_list:
                if (first_x and i == 0) or (first_y and j == 0):
                    masked[own(i, j)] = 0.0
            coarse_m.append(lhs_np(np.concatenate([coarse[1] @ masked, coarse[2] @ masked])))
    t["coarse_m"] = np.stack(coarse_m)
    hats_z = injection_coefficients(ez, points)[:ez]
    phi_z = sine_np(np.arange(ez), ez)
    to_modes = pad_np(hats_z.T @ phi_z, zl, LANES)
    to_modes[0] = 0.0
    t["to_modes"] = rhs_np(np.tile(to_modes, (1, 2)))
    m_modes = np.concatenate([z_back @ mass_z @ to_modes, z_back @ stiff_z @ to_modes])
    t["m_modes"] = rhs_np(np.tile(m_modes, (1, 2)))
    y_in = np.zeros((mesh_y, 8 * vy, count_y * LANES))
    y_out = np.zeros((mesh_y, 8 * (ey + 1), count_y * LANES))
    for p in range(mesh_y):
        y_in[p] = np.repeat(np.repeat(sine_np(p * ey - 1 + np.arange(vy), count_y), 8, 0), LANES, 1)
        y_out[p] = np.repeat(np.repeat(sine_np(p * ey + np.arange(ey + 1), count_y), 8, 0), LANES, 1)
    t["y_in"], t["y_out"] = y_in.astype(np.float32), y_out.astype(np.float32)
    x_in = np.zeros((count_x, mesh_x, 8))
    x_out = np.zeros((mesh_x, 8, count_x))
    for p in range(mesh_x):
        x_in[:, p, :vx] = sine_np(p * ex - 1 + np.arange(vx), count_x).T
        x_out[p, : ex + 1] = sine_np(p * ex + np.arange(ex + 1), count_x)
    t["x_in"] = lhs_np(x_in.reshape(count_x, mesh_x * 8))
    t["x_out"] = np.stack([lhs_np(x_out[p]) for p in range(mesh_x)])
    mu = np.ones((count_x, count_y, LANES))
    mu[:, :, :ez] = (
        eigen_np(count_x)[:, None, None] + eigen_np(count_y)[None, :, None] + eigen_np(ez)
    )
    t["mu"] = (1.0 / mu).reshape(count_x, count_y * LANES).astype(np.float32)
    z_out = np.zeros((LANES, zl + 128))
    z_out[:ez, :nz] = phi_z.T @ hats_z
    z_out[:, 0] = 0.0
    z_out[:ez, zl : zl + ez] = phi_z.T
    t["z_out"] = rhs_np(np.tile(z_out, (2, 1)))
    spread = np.zeros((own_rows, 8 * (ey + 1)))
    hats_x, hats_y = line_x.hats[1:], line_y.hats[1:]
    for i, j in own_list:
        for q in range(ey + 1):
            for p in range(ex + 1):
                spread[own(i, j), 8 * q + p] = hats_x[p, i] * hats_y[q, j]
    t["spread"] = lhs_np(spread)
    return t, dims


def halves(value):
    high = value.astype(jnp.bfloat16)
    return high, (value - high.astype(jnp.float32)).astype(jnp.bfloat16)


def mm(a, b):
    return jnp.dot(a, b, preferred_element_type=jnp.float32)


def left(table, value):
    high, low = halves(value)
    return mm(table, jnp.concatenate([high, low, high], axis=0))


def right(value, table):
    high, low = halves(value)
    return mm(jnp.concatenate([high, low, high], axis=1), table)


PER_DEVICE = ("coarse_m", "y_in", "x_out", "y_out")


def kernel(names, dims, mesh_x, mesh_y, residual, *refs):
    count = len(names)
    far = dict(zip(names, refs[:count]))
    near = dict(zip(names, refs[count + 2 : 2 * count + 2]))
    fine_out, coarse_out = refs[count : count + 2]
    (own, out_b, in_b, out_d, in_d, out_y, in_y, out_x, in_x,
     loaded, sent, got, sent_y, got_y, sent_x, got_x) = refs[2 * count + 2 :]
    nx, ny, nz, pitch = dims["nx"], dims["ny"], dims["nz"], dims["pitch"]
    own_rows, zl = dims["own_rows"], dims["zl"]
    ix, iy = lax.axis_index("gx"), lax.axis_index("gy")
    start_of_grid = 2 * (ix == 0).astype(jnp.int32) + (iy == 0).astype(jnp.int32)
    place = dict(coarse_m=start_of_grid, y_in=iy, x_out=ix, y_out=iy)
    loads = {}
    for n, name in enumerate(names):
        src = far[name].at[place[name]] if name in place else far[name]
        loads[name] = pltpu.make_async_copy(src, near[name], loaded.at[n])
        loads[name].start()

    def table(name):
        if name in loads:
            loads.pop(name).wait()
        return near[name][...]

    def exists(dx, dy):
        return (ix + dx >= 0) & (ix + dx < mesh_x) & (iy + dy >= 0) & (iy + dy < mesh_y)

    own[...] = jnp.zeros_like(own)
    in_b[...] = jnp.zeros_like(in_b)
    in_d[...] = jnp.zeros_like(in_d)
    barrier = pltpu.get_barrier_semaphore()
    for o in range(1, mesh_x):
        pl.semaphore_signal(
            barrier, inc=1, device_id=(lax.rem(ix + o, mesh_x), iy), device_id_type=MESH
        )
    for o in range(1, mesh_y):
        pl.semaphore_signal(
            barrier, inc=1, device_id=(ix, lax.rem(iy + o, mesh_y)), device_id_type=MESH
        )
    corners = DIRECTIONS[4:]
    for dx, dy in corners:
        @pl.when(exists(dx, dy))
        def _():
            pl.semaphore_signal(barrier, inc=1, device_id=(ix + dx, iy + dy), device_id_type=MESH)

    row = lax.broadcasted_iota(jnp.int32, (own_rows, 1), 0)
    node_x, node_y = ix * nx + row // pitch, iy * ny + row % pitch
    keep = ((node_x > 0) & (node_y > 0) & (row % pitch < ny) & (row // pitch < nx)).astype(
        jnp.float32
    )
    for i in range(nx):
        own[i * pitch : i * pitch + ny, 0:nz] = residual[i]
    source = own[...] * keep
    high, low = halves(source)
    pick = table("pick")
    out_b[...] = mm(pick, high) + mm(pick, low)

    greetings = mesh_x - 1 + mesh_y - 1
    for dx, dy in corners:
        greetings = greetings + exists(dx, dy).astype(jnp.int32)
    pl.semaphore_wait(barrier, greetings)

    def halo(phase, src, dst, places):
        copies = []
        for d, (dx, dy) in enumerate(DIRECTIONS):
            start, size = places[d]
            copies.append(
                pltpu.make_async_remote_copy(
                    src_ref=src.at[pl.ds(start, size)],
                    dst_ref=dst.at[pl.ds(start, size)],
                    send_sem=sent.at[phase, d],
                    recv_sem=got.at[phase, d],
                    device_id=(ix - dx, iy - dy),
                    device_id_type=MESH,
                )
            )
        for d, (dx, dy) in enumerate(DIRECTIONS):
            pl.when(exists(-dx, -dy))(copies[d].start)
        return copies

    def arrived(copies):
        for d, (dx, dy) in enumerate(DIRECTIONS):
            pl.when(exists(dx, dy))(copies[d].wait_recv)

    def left_here(copies):
        for d, (dx, dy) in enumerate(DIRECTIONS):
            pl.when(exists(-dx, -dy))(copies[d].wait_send)

    copies_b = halo(0, out_b, in_b, dims["seg_b"])
    z_fwd = table("z_fwd")
    coefs = left(table("w_own"), right(source, z_fwd))
    coarse_b = right(left(table("coarse_b"), source), table("to_modes"))
    arrived(copies_b)
    coefs = coefs + left(table("w_halo"), right(in_b[...], z_fwd))
    modes_0 = coefs * table("inverse")
    first = right(left(table("back"), modes_0), table("z_back")) * (keep * (1.0 / theta_cheb))

    out_d[...] = left(table("send"), first)
    copies_d = halo(1, out_d, in_d, dims["seg_d"])
    applied = left(table("lap_own"), first)
    rows, wide_y = dims["points_rows"], dims["wide_y"]
    spot = lax.broadcasted_iota(jnp.int32, (rows, 1), 0)
    spot_x, spot_y = ix * nx + spot // wide_y - 1, iy * ny + spot % wide_y - 1
    inside = (spot_x > 0) & (spot_x < mesh_x * nx) & (spot_y > 0) & (spot_y < mesh_y * ny)
    inside = inside.astype(jnp.float32)
    arrived(copies_d)
    applied = applied + left(table("lap_halo"), in_d[...])
    applied = jnp.concatenate([applied[:rows] * inside, applied[rows:] * inside], axis=1)
    coefs = coefs - left(table("w_all"), right(applied, table("z_lap")))
    sigma = theta_cheb / delta_cheb
    rho_0 = 1.0 / sigma
    rho_1 = 1.0 / (2.0 * sigma - rho_0)
    weight_0, weight_1 = (1.0 + rho_1 * rho_0) / theta_cheb, 2.0 * rho_1 / delta_cheb
    modes = weight_0 * modes_0 + weight_1 * (coefs * table("inverse"))

    vy = dims["vy"]
    shares = left(table("coarse_m"), modes)
    shares = jnp.concatenate([shares[: 8 * vy], shares[8 * vy :]], axis=1)
    share = coarse_b - right(shares, table("m_modes"))
    share = jnp.concatenate([share] * (dims["lanes"] // 128), axis=1) * table("y_in")
    share = sum(share[8 * w : 8 * w + 8] for w in range(vy))

    def everyone(value, src, dst, count, me, send_sems, recv_sems, place):
        src[...] = value
        copies = []
        for o in range(1, count):
            to = lax.rem(me + o, count)
            copies.append(
                pltpu.make_async_remote_copy(
                    src_ref=src,
                    dst_ref=dst.at[me],
                    send_sem=send_sems.at[o],
                    recv_sem=recv_sems.at[o],
                    device_id=place(to),
                    device_id_type=MESH,
                )
            )
        for copy in copies:
            copy.start()
        dst[me] = value
        return copies

    def all_here(copies):
        for copy in copies:
            copy.wait_recv()

    copies_y = everyone(
        share, out_y, in_y, mesh_y, iy, sent_y, got_y, lambda to: (ix, to)
    )
    total = left(table("back"), modes)
    all_here(copies_y)
    share = sum(in_y[p] for p in range(mesh_y))
    copies_x = everyone(
        share, out_x, in_x, mesh_x, ix, sent_x, got_x, lambda to: (to, iy)
    )
    total = right(total, table("z_back")) * keep
    all_here(copies_x)
    gathered = in_x[...].reshape(mesh_x * 8, dims["lanes"])
    scaled = left(table("x_in"), gathered) * table("mu")
    lines = left(table("x_out"), scaled)[:8]
    y_out = table("y_out")
    lines = jnp.concatenate([lines] * (y_out.shape[0] // 8), axis=0) * y_out
    lines = sum(lines[:, 128 * b : 128 * b + 128] for b in range(dims["lanes"] // 128))
    nodes = right(lines, table("z_out"))
    ex, ey, ez = nx // 7, ny // 7, nz // 7
    for p in range(ex):
        for q in range(ey):
            coarse_out[p, q : q + 1, :] = nodes[8 * q + p : 8 * q + p + 1, zl : zl + ez]
    result = total + left(table("spread"), nodes[:, :zl]) * keep
    for i in range(nx):
        fine_out[i] = result[i * pitch : i * pitch + ny, :nz]
    left_here(copies_b)
    left_here(copies_d)
    for copy in copies_y + copies_x:
        copy.wait_send()


def per_device(mesh_x, mesh_y, residual_in):
    t, dims = tables(mesh_x, mesh_y, residual_in.shape)
    names = list(t)
    nx, ny, nz = residual_in.shape
    own_rows, zl, lanes = dims["own_rows"], dims["zl"], dims["lanes"]
    f32 = jnp.float32
    vmem = pl.BlockSpec(memory_space=pltpu.VMEM)
    return pl.pallas_call(
        functools.partial(kernel, names, dims, mesh_x, mesh_y),
        out_shape=(
            jax.ShapeDtypeStruct((nx, ny, nz), f32),
            jax.ShapeDtypeStruct((nx // 7, ny // 7, nz // 7), f32),
        ),
        in_specs=[vmem] + [pl.BlockSpec(memory_space=pl.ANY)] * len(names),
        out_specs=(vmem, vmem),
        scratch_shapes=[
            pltpu.VMEM(t[name].shape[name in PER_DEVICE :], t[name].dtype) for name in names
        ]
        + [
            pltpu.VMEM((own_rows, zl), f32),
            pltpu.VMEM((dims["rows_b"], zl), f32),
            pltpu.VMEM((dims["rows_b"], zl), f32),
            pltpu.VMEM((dims["rows_d"], zl), f32),
            pltpu.VMEM((dims["rows_d"], zl), f32),
            pltpu.VMEM((8, lanes), f32),
            pltpu.VMEM((mesh_y, 8, lanes), f32),
            pltpu.VMEM((8, lanes), f32),
            pltpu.VMEM((mesh_x, 8, lanes), f32),
            pltpu.SemaphoreType.DMA((len(names),)),
            pltpu.SemaphoreType.DMA((2, 8)),
            pltpu.SemaphoreType.DMA((2, 8)),
            pltpu.SemaphoreType.DMA((mesh_y,)),
            pltpu.SemaphoreType.DMA((mesh_y,)),
            pltpu.SemaphoreType.DMA((mesh_x,)),
            pltpu.SemaphoreType.DMA((mesh_x,)),
        ],
        compiler_params=pltpu.CompilerParams(
            collective_id=0, has_side_effects=True, vmem_limit_bytes=56 * 2**20
        ),
        cost_estimate=pl.CostEstimate(flops=10**9, bytes_accessed=10**7, transcendentals=0),
    )(residual_in, *[jnp.asarray(t[name]) for name in names])


def solution(mesh):
    return jax.shard_map(
        functools.partial(per_device, mesh.shape["gx"], mesh.shape["gy"]),
        mesh=mesh,
        in_specs=(P("gx", "gy", None),),
        out_specs=(P("gx", "gy", None), P("gx", "gy", None)),
        check_vma=False,
    )
```

```python
import functools
import math

import jax
import jax.numpy as jnp
import ml_dtypes
import numpy as np
from jax import lax
from jax.experimental import pallas as pl
from jax.experimental.pallas import tpu as pltpu
from jax.sharding import PartitionSpec as P

theta_cheb = 1.125
delta_cheb = 0.875
start_points = [
    -0.8717401485096066,
    -0.5917001814331423,
    -0.2092992179024789,
    0.2092992179024789,
    0.5917001814331423,
    0.8717401485096066,
]


def legendre_pair(value):
    before, now = (1.0, value)
    for order in range(1, 7):
        before, now = (now, ((2 * order + 1) * value * now - order * before) / (order + 1))
    return (now, before)


def lobatto_tables():
    point_list = [-1.0]
    for guess in start_points:
        place = guess
        for newton in range(4):
            seventh, sixth = legendre_pair(place)
            slope = 7.0 * (place * seventh - sixth) / (place * place - 1.0)
            curve = (2.0 * place * slope - 56.0 * seventh) / (1.0 - place * place)
            place = place - slope / curve
        point_list.append(place)
    point_list.append(1.0)
    sample_nodes_list = np.array(point_list)
    values = np.array([legendre_pair(place)[0] for place in point_list])
    weights = 2.0 / (56.0 * values * values)
    derivative = np.zeros((8, 8))
    for i in range(8):
        for j in range(8):
            if i != j:
                derivative[i, j] = values[i] / (
                    values[j] * (sample_nodes_list[i] - sample_nodes_list[j])
                )
    derivative[0, 0] = -14.0
    derivative[7, 7] = 14.0
    stiffness = derivative.T @ (weights[:, None] * derivative)
    return (sample_nodes_list, weights, stiffness)


def assemble(elements, stiffness, weights):
    width = 7 * elements + 1
    assembled = np.zeros((width, width))
    masses = np.zeros(width)
    for e in range(elements):
        assembled[7 * e : 7 * e + 8, 7 * e : 7 * e + 8] += stiffness
        masses[7 * e : 7 * e + 8] += weights
    return (assembled, masses)


def jacobi_eigen(matrix):
    order = matrix.shape[0]
    work = [[float(matrix[i, j]) for j in range(order)] for i in range(order)]
    vectors = [[1.0 if i == j else 0.0 for j in range(order)] for i in range(order)]
    for sweep in range(12):
        for p in range(order):
            for q in range(p + 1, order):
                angle = 0.5 * math.atan2(2.0 * work[p][q], work[q][q] - work[p][p])
                cosine = math.cos(angle)
                sine = math.sin(angle)
                for k in range(order):
                    left, right = (work[k][p], work[k][q])
                    work[k][p] = cosine * left - sine * right
                    work[k][q] = sine * left + cosine * right
                for k in range(order):
                    left, right = (work[p][k], work[q][k])
                    work[p][k] = cosine * left - sine * right
                    work[q][k] = sine * left + cosine * right
                for k in range(order):
                    left, right = (vectors[k][p], vectors[k][q])
                    vectors[k][p] = cosine * left - sine * right
                    vectors[k][q] = sine * left + cosine * right
    return (np.array([work[i][i] for i in range(order)]), np.array(vectors))


def schwarz_basis():
    sample_nodes_list, weights, stiffness = lobatto_tables()
    assembled, masses = assemble(3, stiffness, weights)
    block_stiff = assembled[6:16, 6:16]
    inv_root = 1.0 / np.sqrt(masses[6:16])
    eigen_vals, eigen_vecs = jacobi_eigen(inv_root[:, None] * block_stiff * inv_root[None, :])
    return (inv_root[:, None] * eigen_vecs, eigen_vals)


def injection_coefficients(elements, sample_nodes_list):
    matrix = np.zeros((elements + 1, 7 * elements))
    for e in range(elements):
        for m in range(7):
            matrix[e, 7 * e + m] += (1.0 - sample_nodes_list[m]) / 2.0
            matrix[e + 1, 7 * e + m] += (1.0 + sample_nodes_list[m]) / 2.0
    return matrix


MESH = pl.DeviceIdType.MESH
LANES = 64
DIRECTIONS = [(-1, 0), (1, 0), (0, -1), (0, 1), (-1, -1), (-1, 1), (1, -1), (1, 1)]


def round_up(value, unit):
    return -(-value // unit) * unit


def sine_np(vertices, elements):
    modes = np.arange(elements)
    vertex = np.asarray(vertices)[:, None]
    entries = np.sqrt(2.0 / elements) * np.sin(np.pi * (vertex * modes % (2 * elements)) / elements)
    entries = entries / np.sqrt((4.0 + 2.0 * np.cos(np.pi * modes / elements)) / 3.0)
    inside = (modes > 0) & (vertex > 0) & (vertex < elements)
    return np.where(inside, entries, 0.0)


def eigen_np(elements):
    modes = np.arange(elements)
    cosine = np.cos(np.pi * modes / elements)
    return np.where(modes > 0, 3.0 * (1.0 - cosine) / (4.0 + 2.0 * cosine), 1.0)


def split_np(matrix, axis):
    high = matrix.astype(np.float32).astype(ml_dtypes.bfloat16)
    low = (matrix - high.astype(np.float64)).astype(np.float32).astype(ml_dtypes.bfloat16)
    return np.concatenate([high, high, low], axis=axis)


def lhs_np(matrix):
    return split_np(pad_np(matrix, round_up(matrix.shape[0], 16), matrix.shape[1]), 1)


def rhs_np(matrix):
    return split_np(matrix, 0)


def pad_np(matrix, rows, columns, value=0.0):
    out = np.full((rows, columns), value)
    out[: matrix.shape[0], : matrix.shape[1]] = matrix
    return out


class Line:
    def __init__(self, elements, stiffness, weights, eigen_basis, points):
        self.elements = elements
        self.nodes = 7 * elements
        around, masses = assemble(elements + 4, stiffness, weights)
        self.around, self.masses, self.shift = around, masses, 14
        self.forward = np.zeros((10 * elements, self.nodes + 3))
        self.backward = np.zeros((self.nodes, 10 * elements))
        for e in range(elements):
            self.forward[10 * e : 10 * e + 10, 7 * e : 7 * e + 10] = eigen_basis.T
            self.backward[7 * e : 7 * e + 7, 10 * e : 10 * e + 10] = eigen_basis[1:8]
        hats = injection_coefficients(elements + 4, points)
        kept = slice(self.shift, self.shift + self.nodes)
        rows = slice(1, 1 + elements + 2)
        full = np.zeros((hats.shape[0], self.around.shape[0]))
        full[:, : hats.shape[1]] = hats
        self.hats = hats[rows, kept]
        self.hats_stiff = (full @ around)[rows, kept]
        self.hats_mass = (full * masses)[rows, kept]

    def stiff(self, i, j):
        return self.around[i + self.shift, j + self.shift]

    def mass(self, i):
        return self.masses[i + self.shift]

    def values(self, side):
        n = self.nodes
        return {-1: [-1], 0: list(range(n)), 1: [n, n + 1]}[side]

    def sums(self, side):
        n = self.nodes
        return {-1: [-1, 0], 0: [], 1: [n, n + 1]}[side]


def segments(lines, with_sums):
    line_x, line_y = lines
    out, start = [], 0
    for dx, dy in DIRECTIONS:
        rows = [("v", i, j) for i in line_x.values(dx) for j in line_y.values(dy)]
        if with_sums:
            rows += [("x", i, j) for i in line_x.sums(dx) for j in line_y.values(dy)]
            rows += [("y", i, j) for i in line_x.values(dx) for j in line_y.sums(dy)]
        size = round_up(len(rows), 8)
        out.append((start, size, rows))
        start += size
    return out, start


def tables(mesh_x, mesh_y, shape):
    points, weights, stiffness = lobatto_tables()
    eigen_basis, eigen_vals = schwarz_basis()
    nx, ny, nz = shape
    ex, ey, ez = nx // 7, ny // 7, nz // 7
    line_x = Line(ex, stiffness, weights, eigen_basis, points)
    line_y = Line(ey, stiffness, weights, eigen_basis, points)
    lines = (line_x, line_y)
    pitch = round_up(ny, 8)
    own_rows = round_up(nx * pitch, 128)
    zl = round_up(nz, 128)
    cl = round_up(10 * ez, 128)
    coefs = 100 * ex * ey
    own = lambda i, j: i * pitch + j
    own_list = [(i, j) for i in range(nx) for j in range(ny)]
    t = {}
    dims = dict(nx=nx, ny=ny, nz=nz, pitch=pitch, own_rows=own_rows, zl=zl, cl=cl, coefs=coefs)

    forward = lambda i, j: np.kron(line_x.forward[:, i + 1], line_y.forward[:, j + 1])
    seg_b, rows_b = segments(lines, False)
    seg_d, rows_d = segments(lines, True)
    rows_d = round_up(rows_d, 16)
    dims.update(seg_b=[s[:2] for s in seg_b], rows_b=rows_b)
    dims.update(seg_d=[s[:2] for s in seg_d], rows_d=rows_d)

    pick = np.zeros((rows_b, own_rows))
    w_halo = np.zeros((coefs, rows_b))
    for (dx, dy), (start, size, rows) in zip(DIRECTIONS, seg_b):
        for r, (kind, i, j) in enumerate(rows):
            pick[start + r, own(i - nx * dx, j - ny * dy)] = 1.0
            w_halo[:, start + r] = forward(i, j)
    w_own = np.zeros((coefs, own_rows))
    back = np.zeros((own_rows, coefs))
    for i, j in own_list:
        w_own[:, own(i, j)] = forward(i, j)
        back[own(i, j)] = np.kron(line_x.backward[i], line_y.backward[j])
    z_fwd = np.zeros((zl, cl))
    z_back = np.zeros((cl, zl))
    for e in range(ez):
        for m in range(10):
            z = 7 * e - 1 + m
            if 0 < z < nz:
                z_fwd[z, 10 * e : 10 * e + 10] = eigen_basis[m]
                if 1 <= m <= 7:
                    z_back[10 * e : 10 * e + 10, z] = eigen_basis[m]
    l_x, l_y = np.tile(eigen_vals, ex), np.tile(eigen_vals, ey)
    l_z = np.ones(cl)
    l_z[: 10 * ez] = np.tile(eigen_vals, ez)
    inverse = 1.0 / ((l_x[:, None] + l_y[None, :]).reshape(coefs, 1) + l_z)
    t["z_fwd"] = rhs_np(z_fwd)
    t["pick"] = pick.astype(ml_dtypes.bfloat16)
    t["w_own"] = lhs_np(w_own)
    t["coarse_b"] = None
    t["to_modes"] = None
    t["w_halo"] = lhs_np(w_halo)
    t["inverse"] = inverse.astype(np.float32)
    t["send_m"] = None
    t["z_back"], t["back"] = rhs_np(z_back), lhs_np(back)

    send = np.zeros((rows_d, own_rows))
    wide_y = ny + 3
    points_rows = round_up((nx + 3) * wide_y, 16)
    target = lambda i, j: (i + 1) * wide_y + (j + 1)
    inside_x = lambda i: -1 <= i <= nx + 1
    inside_y = lambda j: -1 <= j <= ny + 1
    dims["points_rows"], dims["wide_y"] = points_rows, wide_y
    lap_own = np.zeros((2 * points_rows, own_rows))
    lap_halo = np.zeros((2 * points_rows, rows_d))

    def value_column(column, i, j, dx, dy):
        for k in range(-1, nx + 2):
            if k not in line_x.sums(dx):
                column[target(k, j)] += line_x.stiff(k, i) * line_y.mass(j)
        for k in range(-1, ny + 2):
            if k not in line_y.sums(dy):
                column[target(i, k)] += line_y.stiff(k, j) * line_x.mass(i)
        column[points_rows + target(i, j)] += line_x.mass(i) * line_y.mass(j)

    for i, j in own_list:
        value_column(lap_own[:, own(i, j)], i, j, 0, 0)
    for (dx, dy), (start, size, rows) in zip(DIRECTIONS, seg_d):
        for r, (kind, i, j) in enumerate(rows):
            p, q = i - nx * dx, j - ny * dy
            if kind == "v":
                send[start + r, own(p, q)] = 1.0
                value_column(lap_halo[:, start + r], i, j, dx, dy)
            elif kind == "x":
                for k in range(nx):
                    send[start + r, own(k, q)] = line_x.stiff(p, k)
                lap_halo[target(i, j), start + r] += line_y.mass(j)
            else:
                for k in range(ny):
                    send[start + r, own(p, k)] = line_y.stiff(q, k)
                lap_halo[target(i, j), start + r] += line_x.mass(i)
    w_all = np.zeros((coefs, points_rows))
    for i in range(-1, nx + 2):
        for j in range(-1, ny + 2):
            w_all[:, target(i, j)] = forward(i, j)
    masked_backs = []
    for first_x in (0, 1):
        for first_y in (0, 1):
            masked = back.copy()
            for i, j in own_list:
                if (first_x and i == 0) or (first_y and j == 0):
                    masked[own(i, j)] = 0.0
            masked_backs.append(masked)
    t["send_m"] = np.stack([lhs_np(send @ masked / theta_cheb) for masked in masked_backs])
    t["lap_own"], t["lap_halo"] = lhs_np(lap_own), lhs_np(lap_halo)
    stiff_z, mass_z = assemble(ez, stiffness, weights)
    stiff_z = pad_np(stiff_z[:nz, :nz], zl, zl)
    mass_z = np.diag(pad_np(mass_z[None, :nz], 1, zl)[0])
    t["z_lap"] = rhs_np(np.concatenate([mass_z @ z_fwd, stiff_z @ z_fwd]))
    t["w_all"] = lhs_np(w_all)

    count_x, count_y = mesh_x * ex, mesh_y * ey
    vx, vy = ex + 2, ey + 2
    assert vx == 4 and vy == 4 and count_y % 4 == 0
    half_y = count_y // 2
    dims.update(count_x=count_x, half_y=half_y, lanes=half_y * LANES)
    coarse = np.zeros((3, 16, own_rows))
    for i, j in own_list:
        for w in range(vy):
            for v in range(vx):
                row = 4 * w + v
                coarse[0, row, own(i, j)] = line_x.hats[v, i] * line_y.hats[w, j]
                coarse[1, row, own(i, j)] = (
                    line_x.hats_stiff[v, i] * line_y.hats_mass[w, j]
                    + line_x.hats_mass[v, i] * line_y.hats_stiff[w, j]
                )
                coarse[2, row, own(i, j)] = line_x.hats_mass[v, i] * line_y.hats_mass[w, j]
    t["coarse_b"] = lhs_np(coarse[0])
    coarse_m = [
        lhs_np(np.concatenate([coarse[1] @ masked, coarse[2] @ masked])) for masked in masked_backs
    ]
    t["coarse_m"] = np.stack(coarse_m)
    hats_z = injection_coefficients(ez, points)[:ez]
    phi_z = sine_np(np.arange(ez), ez)
    to_modes = pad_np(hats_z.T @ phi_z, zl, LANES)
    to_modes[0] = 0.0
    t["to_modes"] = rhs_np(np.tile(to_modes, (1, 2)))
    m_modes = np.concatenate([z_back @ mass_z @ to_modes, z_back @ stiff_z @ to_modes])
    t["m_modes"] = rhs_np(np.tile(m_modes, (1, 2)))
    y_in = np.zeros((mesh_y, count_y, 2, 4, 2, LANES))
    y_out = np.zeros((mesh_y, 8, half_y * LANES))
    for p in range(mesh_y):
        inward = sine_np(p * ey - 1 + np.arange(vy), count_y)
        outward = sine_np(p * ey + np.arange(ey + 1), count_y)
        for w in range(vy):
            y_in[p, :, w % 2, :, w // 2, :] = inward[w][:, None, None]
        for q in range(ey + 1):
            for h in range(2):
                y_out[p, 2 * q + h] = np.repeat(outward[q, h * half_y : (h + 1) * half_y], LANES)
    t["y_in"] = y_in.reshape(mesh_y * count_y * 8, 2 * LANES).astype(np.float32)
    x_in = np.zeros((2, count_x, mesh_x, 2, 4))
    x_out = np.zeros((mesh_x, 2, 8, 2, count_x))
    for p in range(mesh_x):
        for h in range(2):
            x_in[h, :, p, h] = sine_np(p * ex - 1 + np.arange(vx), count_x).T
            x_out[p, h, : ex + 1, h] = sine_np(p * ex + np.arange(ex + 1), count_x)
    t["x_in"] = lhs_np(x_in.reshape(2 * count_x, mesh_x * 8))
    mu = np.ones((count_x, count_y, LANES))
    mu[:, :, :ez] = (
        eigen_np(count_x)[:, None, None] + eigen_np(count_y)[None, :, None] + eigen_np(ez)
    )
    mu = mu.reshape(count_x, 2, half_y * LANES).transpose(1, 0, 2)
    t["mu"] = (1.0 / mu).reshape(2 * count_x, half_y * LANES).astype(np.float32)
    t["x_out"] = np.stack([lhs_np(x_out[p].reshape(16, 2 * count_x)) for p in range(mesh_x)])
    t["y_out"] = y_out.astype(np.float32)
    z_out = np.zeros((LANES, zl + 128))
    z_out[:ez, :nz] = phi_z.T @ hats_z
    z_out[:, 0] = 0.0
    z_out[:ez, zl : zl + ez] = phi_z.T
    t["z_out"] = rhs_np(np.tile(z_out, (2, 1)))
    spread = np.zeros((own_rows, 8 * (ey + 1)))
    hats_x, hats_y = line_x.hats[1:], line_y.hats[1:]
    for i, j in own_list:
        for q in range(ey + 1):
            for p in range(ex + 1):
                spread[own(i, j), 8 * q + p] = hats_x[p, i] * hats_y[q, j]
    return t, dims, lhs_np(spread)


def halves(value):
    high = value.astype(jnp.bfloat16)
    return high, (value - high.astype(jnp.float32)).astype(jnp.bfloat16)


def mm(a, b):
    return jnp.dot(a, b, preferred_element_type=jnp.float32)


def left(table, value):
    high, low = halves(value)
    return mm(table, jnp.concatenate([high, low, high], axis=0))


def right(value, table):
    high, low = halves(value)
    return mm(jnp.concatenate([high, low, high], axis=1), table)


PER_DEVICE = ("send_m", "coarse_m", "x_out", "y_out")


def kernel(names, dims, mesh_x, mesh_y, residual, *refs):
    count = len(names)
    far = dict(zip(names, refs[:count]))
    near = dict(zip(names, refs[count + 2 : 2 * count + 2]))
    total_out, nodes_out = refs[count : count + 2]
    (block, own, out_b, in_b, out_d, in_d, out_y, in_y, out_x, in_x,
     local, loaded, sent, got, sent_y, got_y, sent_x, got_x) = refs[2 * count + 2 :]
    nx, ny, nz, pitch = dims["nx"], dims["ny"], dims["nz"], dims["pitch"]
    own_rows, zl = dims["own_rows"], dims["zl"]
    ix, iy = lax.axis_index("gx"), lax.axis_index("gy")
    def exists(dx, dy):
        return (ix + dx >= 0) & (ix + dx < mesh_x) & (iy + dy >= 0) & (iy + dy < mesh_y)

    in_b[...] = jnp.zeros_like(in_b)
    in_d[...] = jnp.zeros_like(in_d)
    barrier = pltpu.get_barrier_semaphore()
    for o in range(1, mesh_x):
        pl.semaphore_signal(
            barrier, inc=1, device_id=(lax.rem(ix + o, mesh_x), iy), device_id_type=MESH
        )
    for o in range(1, mesh_y):
        pl.semaphore_signal(
            barrier, inc=1, device_id=(ix, lax.rem(iy + o, mesh_y)), device_id_type=MESH
        )
    corners = DIRECTIONS[4:]
    for dx, dy in corners:
        @pl.when(exists(dx, dy))
        def _():
            pl.semaphore_signal(barrier, inc=1, device_id=(ix + dx, iy + dy), device_id_type=MESH)

    residual_in = pltpu.make_async_copy(residual, block, local.at[0])
    residual_in.start()
    start_of_grid = 2 * (ix == 0).astype(jnp.int32) + (iy == 0).astype(jnp.int32)
    place = dict(send_m=start_of_grid, coarse_m=start_of_grid, x_out=ix, y_out=iy)
    loads = {}
    for n, name in enumerate(names):
        src = far[name].at[place[name]] if name in place else far[name]
        loads[name] = pltpu.make_async_copy(src, near[name], loaded.at[n])
        loads[name].start()

    def table(name):
        if name in loads:
            loads.pop(name).wait()
        return near[name][...]

    own[...] = jnp.zeros_like(own)
    row = lax.broadcasted_iota(jnp.int32, (own_rows, 1), 0)
    node_x, node_y = ix * nx + row // pitch, iy * ny + row % pitch
    keep = ((node_x > 0) & (node_y > 0) & (row % pitch < ny) & (row // pitch < nx)).astype(
        jnp.float32
    )
    residual_in.wait()
    for i in range(nx):
        own[i * pitch : i * pitch + ny, 0:nz] = block[i]
    source = own[...] * keep
    high, low = halves(source)
    pick = table("pick")
    out_b[...] = mm(pick, high) + mm(pick, low)

    greetings = mesh_x - 1 + mesh_y - 1
    for dx, dy in corners:
        greetings = greetings + exists(dx, dy).astype(jnp.int32)
    pl.semaphore_wait(barrier, greetings)

    def halo(phase, src, dst, places):
        copies = []
        for d, (dx, dy) in enumerate(DIRECTIONS):
            start, size = places[d]
            copies.append(
                pltpu.make_async_remote_copy(
                    src_ref=src.at[pl.ds(start, size)],
                    dst_ref=dst.at[pl.ds(start, size)],
                    send_sem=sent.at[phase, d],
                    recv_sem=got.at[phase, d],
                    device_id=(ix - dx, iy - dy),
                    device_id_type=MESH,
                )
            )
        for d, (dx, dy) in enumerate(DIRECTIONS):
            pl.when(exists(-dx, -dy))(copies[d].start)
        return copies

    def arrived(copies):
        for d, (dx, dy) in enumerate(DIRECTIONS):
            pl.when(exists(dx, dy))(copies[d].wait_recv)

    def left_here(copies):
        for d, (dx, dy) in enumerate(DIRECTIONS):
            pl.when(exists(-dx, -dy))(copies[d].wait_send)

    copies_b = halo(0, out_b, in_b, dims["seg_b"])
    z_fwd = table("z_fwd")
    coefs = left(table("w_own"), right(source, z_fwd))
    coarse_b = right(left(table("coarse_b"), source), table("to_modes"))
    arrived(copies_b)
    coefs = coefs + left(table("w_halo"), right(in_b[...], z_fwd))
    modes_0 = coefs * table("inverse")
    out_d[...] = right(left(table("send_m"), modes_0), table("z_back"))
    copies_d = halo(1, out_d, in_d, dims["seg_d"])
    first = right(left(table("back"), modes_0), table("z_back")) * (keep * (1.0 / theta_cheb))
    applied = left(table("lap_own"), first)
    rows, wide_y = dims["points_rows"], dims["wide_y"]
    spot = lax.broadcasted_iota(jnp.int32, (rows, 1), 0)
    spot_x, spot_y = ix * nx + spot // wide_y - 1, iy * ny + spot % wide_y - 1
    inside = (spot_x > 0) & (spot_x < mesh_x * nx) & (spot_y > 0) & (spot_y < mesh_y * ny)
    inside = inside.astype(jnp.float32)
    arrived(copies_d)
    applied = applied + left(table("lap_halo"), in_d[...])
    applied = jnp.concatenate([applied[:rows] * inside, applied[rows:] * inside], axis=1)
    coefs = coefs - left(table("w_all"), right(applied, table("z_lap")))
    sigma = theta_cheb / delta_cheb
    rho_0 = 1.0 / sigma
    rho_1 = 1.0 / (2.0 * sigma - rho_0)
    weight_0, weight_1 = (1.0 + rho_1 * rho_0) / theta_cheb, 2.0 * rho_1 / delta_cheb
    modes = weight_0 * modes_0 + weight_1 * (coefs * table("inverse"))

    lanes = dims["lanes"]
    shares = left(table("coarse_m"), modes)
    shares = jnp.concatenate([shares[:16], shares[16:]], axis=1)
    share = coarse_b - right(shares, table("m_modes"))
    lower_lanes = lax.broadcasted_iota(jnp.int32, (8, 128), 1) < LANES
    lower_rows = lax.broadcasted_iota(jnp.int32, (8, 128), 0) < 4
    share = jnp.where(lower_lanes, share[:8], share[8:])

    def everyone(value, src, dst, count, me, send_sems, recv_sems, place):
        src[...] = value
        copies = []
        for o in range(1, count):
            to = lax.rem(me + o, count)
            copies.append(
                pltpu.make_async_remote_copy(
                    src_ref=src,
                    dst_ref=dst.at[me],
                    send_sem=send_sems.at[o],
                    recv_sem=recv_sems.at[o],
                    device_id=place(to),
                    device_id_type=MESH,
                )
            )
        for copy in copies:
            copy.start()
        dst[me] = value
        return copies

    def all_here(copies):
        for copy in copies:
            copy.wait_recv()

    copies_y = everyone(
        share, out_y, in_y, mesh_y, iy, sent_y, got_y, lambda to: (ix, to)
    )
    total = left(table("back"), modes)
    all_here(copies_y)
    half = dims["half_y"]
    y_in = table("y_in").reshape(mesh_y, 2 * half * 8, 128)
    tiles = []
    for b in range(2 * half):
        tile = sum(in_y[p] * y_in[p, 8 * b : 8 * b + 8] for p in range(mesh_y))
        tile = tile + pltpu.roll(tile, LANES, 1)
        tiles.append(tile + pltpu.roll(tile, 4, 0))
    blocks = []
    for b in range(0, half, 2):
        lower = jnp.where(lower_lanes, tiles[b], tiles[b + 1])
        upper = jnp.where(lower_lanes, tiles[half + b], tiles[half + b + 1])
        blocks.append(jnp.where(lower_rows, lower, upper))
    share = jnp.concatenate(blocks, axis=1)
    copies_x = everyone(
        share, out_x, in_x, mesh_x, ix, sent_x, got_x, lambda to: (to, iy)
    )
    own[...] = right(total, table("z_back")) * keep
    total_copy = pltpu.make_async_copy(own, total_out, local.at[1])
    total_copy.start()
    all_here(copies_x)
    gathered = in_x[...].reshape(mesh_x * 8, lanes)
    scaled = left(table("x_in"), gathered) * table("mu")
    lines = left(table("x_out"), scaled)
    y_out = table("y_out")
    by_row = []
    for q in range(ny // 7 + 1):
        line = lines[:8] * y_out[2 * q : 2 * q + 1] + lines[8:] * y_out[2 * q + 1 : 2 * q + 2]
        by_row.append(sum(line[:, 128 * b : 128 * b + 128] for b in range(lanes // 128)))
    nodes_out[...] = right(jnp.concatenate(by_row, axis=0), table("z_out"))
    total_copy.wait()
    left_here(copies_b)
    left_here(copies_d)
    for copy in copies_y + copies_x:
        copy.wait_send()


def finish(dims, spread, total, nodes, fine_out, coarse_out):
    nx, ny, nz, pitch, zl = dims["nx"], dims["ny"], dims["nz"], dims["pitch"], dims["zl"]
    ix, iy = lax.axis_index("gx"), lax.axis_index("gy")
    row = lax.broadcasted_iota(jnp.int32, (dims["own_rows"], 1), 0)
    keep = (ix * nx + row // pitch > 0) & (iy * ny + row % pitch > 0)
    values = nodes[...]
    for p in range(nx // 7):
        for q in range(ny // 7):
            line = values[8 * q + p : 8 * q + p + 1, zl : zl + nz // 7]
            coarse_out[p, q : q + 1, :] = line
    prolonged = left(spread[...], values[:, :zl])
    result = total[...] + prolonged * keep.astype(jnp.float32)
    for i in range(nx):
        fine_out[i] = result[i * pitch : i * pitch + ny, :nz]


def per_device(mesh_x, mesh_y, residual_in):
    t, dims, spread = tables(mesh_x, mesh_y, residual_in.shape)
    names = list(t)
    nx, ny, nz = residual_in.shape
    own_rows, zl, lanes = dims["own_rows"], dims["zl"], dims["lanes"]
    f32 = jnp.float32
    vmem = pl.BlockSpec(memory_space=pltpu.VMEM)
    total, nodes = pl.pallas_call(
        functools.partial(kernel, names, dims, mesh_x, mesh_y),
        out_shape=(
            jax.ShapeDtypeStruct((own_rows, zl), f32),
            jax.ShapeDtypeStruct((8 * (ny // 7 + 1), zl + 128), f32),
        ),
        in_specs=[pl.BlockSpec(memory_space=pl.ANY)] * (1 + len(names)),
        out_specs=(pl.BlockSpec(memory_space=pl.ANY), vmem),
        scratch_shapes=[
            pltpu.VMEM(t[name].shape[name in PER_DEVICE :], t[name].dtype) for name in names
        ]
        + [
            pltpu.VMEM((nx, ny, nz), f32),
            pltpu.VMEM((own_rows, zl), f32),
            pltpu.VMEM((dims["rows_b"], zl), f32),
            pltpu.VMEM((dims["rows_b"], zl), f32),
            pltpu.VMEM((dims["rows_d"], zl), f32),
            pltpu.VMEM((dims["rows_d"], zl), f32),
            pltpu.VMEM((8, 128), f32),
            pltpu.VMEM((mesh_y, 8, 128), f32),
            pltpu.VMEM((8, lanes), f32),
            pltpu.VMEM((mesh_x, 8, lanes), f32),
            pltpu.SemaphoreType.DMA((2,)),
            pltpu.SemaphoreType.DMA((len(names),)),
            pltpu.SemaphoreType.DMA((2, 8)),
            pltpu.SemaphoreType.DMA((2, 8)),
            pltpu.SemaphoreType.DMA((mesh_y,)),
            pltpu.SemaphoreType.DMA((mesh_y,)),
            pltpu.SemaphoreType.DMA((mesh_x,)),
            pltpu.SemaphoreType.DMA((mesh_x,)),
        ],
        compiler_params=pltpu.CompilerParams(
            collective_id=0, has_side_effects=True, vmem_limit_bytes=56 * 2**20
        ),
        cost_estimate=pl.CostEstimate(flops=10**9, bytes_accessed=10**7, transcendentals=0),
    )(residual_in, *[jnp.asarray(t[name]) for name in names])
    return pl.pallas_call(
        functools.partial(finish, dims),
        out_shape=(
            jax.ShapeDtypeStruct((nx, ny, nz), f32),
            jax.ShapeDtypeStruct((nx // 7, ny // 7, nz // 7), f32),
        ),
        in_specs=[vmem] * 3,
        out_specs=(vmem, vmem),
        compiler_params=pltpu.CompilerParams(vmem_limit_bytes=8 * 2**20),
        cost_estimate=pl.CostEstimate(flops=10**7, bytes_accessed=10**6, transcendentals=0),
    )(jnp.asarray(spread), total, nodes)


def solution(mesh):
    return jax.shard_map(
        functools.partial(per_device, mesh.shape["gx"], mesh.shape["gy"]),
        mesh=mesh,
        in_specs=(P("gx", "gy", None),),
        out_specs=(P("gx", "gy", None), P("gx", "gy", None)),
        check_vma=False,
    )
```

```python
import functools
import math

import jax
import jax.numpy as jnp
import ml_dtypes
import numpy as np
from jax import lax
from jax.experimental import pallas as pl
from jax.experimental.pallas import tpu as pltpu
from jax.sharding import PartitionSpec as P

theta_cheb = 1.125
delta_cheb = 0.875
start_points = [
    -0.8717401485096066,
    -0.5917001814331423,
    -0.2092992179024789,
    0.2092992179024789,
    0.5917001814331423,
    0.8717401485096066,
]


def legendre_pair(value):
    before, now = (1.0, value)
    for order in range(1, 7):
        before, now = (now, ((2 * order + 1) * value * now - order * before) / (order + 1))
    return (now, before)


def lobatto_tables():
    point_list = [-1.0]
    for guess in start_points:
        place = guess
        for newton in range(4):
            seventh, sixth = legendre_pair(place)
            slope = 7.0 * (place * seventh - sixth) / (place * place - 1.0)
            curve = (2.0 * place * slope - 56.0 * seventh) / (1.0 - place * place)
            place = place - slope / curve
        point_list.append(place)
    point_list.append(1.0)
    sample_nodes_list = np.array(point_list)
    values = np.array([legendre_pair(place)[0] for place in point_list])
    weights = 2.0 / (56.0 * values * values)
    derivative = np.zeros((8, 8))
    for i in range(8):
        for j in range(8):
            if i != j:
                derivative[i, j] = values[i] / (
                    values[j] * (sample_nodes_list[i] - sample_nodes_list[j])
                )
    derivative[0, 0] = -14.0
    derivative[7, 7] = 14.0
    stiffness = derivative.T @ (weights[:, None] * derivative)
    return (sample_nodes_list, weights, stiffness)


def assemble(elements, stiffness, weights):
    width = 7 * elements + 1
    assembled = np.zeros((width, width))
    masses = np.zeros(width)
    for e in range(elements):
        assembled[7 * e : 7 * e + 8, 7 * e : 7 * e + 8] += stiffness
        masses[7 * e : 7 * e + 8] += weights
    return (assembled, masses)


def jacobi_eigen(matrix):
    order = matrix.shape[0]
    work = [[float(matrix[i, j]) for j in range(order)] for i in range(order)]
    vectors = [[1.0 if i == j else 0.0 for j in range(order)] for i in range(order)]
    for sweep in range(12):
        for p in range(order):
            for q in range(p + 1, order):
                angle = 0.5 * math.atan2(2.0 * work[p][q], work[q][q] - work[p][p])
                cosine = math.cos(angle)
                sine = math.sin(angle)
                for k in range(order):
                    left, right = (work[k][p], work[k][q])
                    work[k][p] = cosine * left - sine * right
                    work[k][q] = sine * left + cosine * right
                for k in range(order):
                    left, right = (work[p][k], work[q][k])
                    work[p][k] = cosine * left - sine * right
                    work[q][k] = sine * left + cosine * right
                for k in range(order):
                    left, right = (vectors[k][p], vectors[k][q])
                    vectors[k][p] = cosine * left - sine * right
                    vectors[k][q] = sine * left + cosine * right
    return (np.array([work[i][i] for i in range(order)]), np.array(vectors))


def schwarz_basis():
    sample_nodes_list, weights, stiffness = lobatto_tables()
    assembled, masses = assemble(3, stiffness, weights)
    block_stiff = assembled[6:16, 6:16]
    inv_root = 1.0 / np.sqrt(masses[6:16])
    eigen_vals, eigen_vecs = jacobi_eigen(inv_root[:, None] * block_stiff * inv_root[None, :])
    return (inv_root[:, None] * eigen_vecs, eigen_vals)


def injection_coefficients(elements, sample_nodes_list):
    matrix = np.zeros((elements + 1, 7 * elements))
    for e in range(elements):
        for m in range(7):
            matrix[e, 7 * e + m] += (1.0 - sample_nodes_list[m]) / 2.0
            matrix[e + 1, 7 * e + m] += (1.0 + sample_nodes_list[m]) / 2.0
    return matrix


MESH = pl.DeviceIdType.MESH
LANES = 64
DIRECTIONS = [(-1, 0), (1, 0), (0, -1), (0, 1), (-1, -1), (-1, 1), (1, -1), (1, 1)]


def round_up(value, unit):
    return -(-value // unit) * unit


def sine_np(vertices, elements):
    modes = np.arange(elements)
    vertex = np.asarray(vertices)[:, None]
    entries = np.sqrt(2.0 / elements) * np.sin(np.pi * (vertex * modes % (2 * elements)) / elements)
    entries = entries / np.sqrt((4.0 + 2.0 * np.cos(np.pi * modes / elements)) / 3.0)
    inside = (modes > 0) & (vertex > 0) & (vertex < elements)
    return np.where(inside, entries, 0.0)


def eigen_np(elements):
    modes = np.arange(elements)
    cosine = np.cos(np.pi * modes / elements)
    return np.where(modes > 0, 3.0 * (1.0 - cosine) / (4.0 + 2.0 * cosine), 1.0)


def split_np(matrix, axis):
    high = matrix.astype(np.float32).astype(ml_dtypes.bfloat16)
    low = (matrix - high.astype(np.float64)).astype(np.float32).astype(ml_dtypes.bfloat16)
    return np.concatenate([high, high, low], axis=axis)


def lhs_np(matrix):
    return split_np(pad_np(matrix, round_up(matrix.shape[0], 16), matrix.shape[1]), 1)


def rhs_np(matrix):
    return split_np(matrix, 0)


def pad_np(matrix, rows, columns, value=0.0):
    out = np.full((rows, columns), value)
    out[: matrix.shape[0], : matrix.shape[1]] = matrix
    return out


class Line:
    def __init__(self, elements, stiffness, weights, eigen_basis, points):
        self.elements = elements
        self.nodes = 7 * elements
        around, masses = assemble(elements + 4, stiffness, weights)
        self.around, self.masses, self.shift = around, masses, 14
        self.forward = np.zeros((10 * elements, self.nodes + 3))
        self.backward = np.zeros((self.nodes, 10 * elements))
        for e in range(elements):
            self.forward[10 * e : 10 * e + 10, 7 * e : 7 * e + 10] = eigen_basis.T
            self.backward[7 * e : 7 * e + 7, 10 * e : 10 * e + 10] = eigen_basis[1:8]
        hats = injection_coefficients(elements + 4, points)
        kept = slice(self.shift, self.shift + self.nodes)
        rows = slice(1, 1 + elements + 2)
        full = np.zeros((hats.shape[0], self.around.shape[0]))
        full[:, : hats.shape[1]] = hats
        self.hats = hats[rows, kept]
        self.hats_stiff = (full @ around)[rows, kept]
        self.hats_mass = (full * masses)[rows, kept]

    def stiff(self, i, j):
        return self.around[i + self.shift, j + self.shift]

    def mass(self, i):
        return self.masses[i + self.shift]

    def values(self, side):
        n = self.nodes
        return {-1: [-1], 0: list(range(n)), 1: [n, n + 1]}[side]

    def sums(self, side):
        n = self.nodes
        return {-1: [-1, 0], 0: [], 1: [n, n + 1]}[side]


def segments(lines, with_sums):
    line_x, line_y = lines
    out, start = [], 0
    for dx, dy in DIRECTIONS:
        rows = [("v", i, j) for i in line_x.values(dx) for j in line_y.values(dy)]
        if with_sums:
            rows += [("x", i, j) for i in line_x.sums(dx) for j in line_y.values(dy)]
            rows += [("y", i, j) for i in line_x.values(dx) for j in line_y.sums(dy)]
        size = round_up(len(rows), 8)
        out.append((start, size, rows))
        start += size
    return out, start


def tables(mesh_x, mesh_y, shape):
    points, weights, stiffness = lobatto_tables()
    eigen_basis, eigen_vals = schwarz_basis()
    nx, ny, nz = shape
    ex, ey, ez = nx // 7, ny // 7, nz // 7
    line_x = Line(ex, stiffness, weights, eigen_basis, points)
    line_y = Line(ey, stiffness, weights, eigen_basis, points)
    lines = (line_x, line_y)
    pitch = round_up(ny, 8)
    own_rows = round_up(nx * pitch, 16)
    zl = round_up(nz, 128)
    half_z = ez // 2
    assert ez % 2 == 0 and 10 * half_z <= 256 and zl >= 256
    cl = 512
    windows = [0, zl - 256]
    coefs = 100 * ex * ey
    own = lambda i, j: i * pitch + j
    own_list = [(i, j) for i in range(nx) for j in range(ny)]
    t = {}
    dims = dict(nx=nx, ny=ny, nz=nz, pitch=pitch, own_rows=own_rows, zl=zl, windows=windows)

    forward = lambda i, j: np.kron(line_x.forward[:, i + 1], line_y.forward[:, j + 1])
    seg_b, rows_b = segments(lines, False)
    seg_d, rows_d = segments(lines, True)
    rows_d = round_up(rows_d, 16)
    dims.update(seg_b=[s[:2] for s in seg_b], rows_b=rows_b)
    dims.update(seg_d=[s[:2] for s in seg_d], rows_d=rows_d)

    pick = np.zeros((rows_b, own_rows))
    w_halo = np.zeros((coefs, rows_b))
    for (dx, dy), (start, size, rows) in zip(DIRECTIONS, seg_b):
        for r, (kind, i, j) in enumerate(rows):
            pick[start + r, own(i - nx * dx, j - ny * dy)] = 1.0
            w_halo[:, start + r] = forward(i, j)
    w_own = np.zeros((coefs, own_rows))
    back = np.zeros((own_rows, coefs))
    for i, j in own_list:
        w_own[:, own(i, j)] = forward(i, j)
        back[own(i, j)] = np.kron(line_x.backward[i], line_y.backward[j])
    z_fwd = np.zeros((zl, cl))
    z_back = np.zeros((cl, zl))
    l_z = np.ones(cl)
    for e in range(ez):
        lane = 256 * (e // half_z) + 10 * (e % half_z)
        l_z[lane : lane + 10] = eigen_vals
        for m in range(10):
            z = 7 * e - 1 + m
            if 0 < z < nz:
                z_fwd[z, lane : lane + 10] = eigen_basis[m]
                if 1 <= m <= 7:
                    z_back[lane : lane + 10, z] = eigen_basis[m]
    l_x, l_y = np.tile(eigen_vals, ex), np.tile(eigen_vals, ey)
    inverse = 1.0 / ((l_x[:, None] + l_y[None, :]).reshape(coefs, 1) + l_z)

    def window(matrix, c):
        kept = matrix[windows[c] : windows[c] + 256, 256 * c : 256 * c + 256]
        assert np.count_nonzero(kept) == np.count_nonzero(matrix[:, 256 * c : 256 * c + 256])
        return kept

    t["z_fwd"] = np.stack([rhs_np(window(z_fwd, c)) for c in range(2)])
    t["pick"] = pick.astype(ml_dtypes.bfloat16)
    t["w_own"] = lhs_np(w_own)
    t["coarse_b"] = None
    t["to_modes"] = None
    t["w_halo"] = lhs_np(w_halo)
    t["inverse"] = inverse.astype(np.float32)
    t["send_m"] = None
    t["z_back"] = np.stack([rhs_np(window(z_back.T, c).T) for c in range(2)])
    t["back"] = lhs_np(back)

    send = np.zeros((rows_d, own_rows))
    wide_y = ny + 3
    points_rows = round_up((nx + 3) * wide_y, 16)
    target = lambda i, j: (i + 1) * wide_y + (j + 1)
    inside_x = lambda i: -1 <= i <= nx + 1
    inside_y = lambda j: -1 <= j <= ny + 1
    dims["points_rows"], dims["wide_y"] = points_rows, wide_y
    lap_own = np.zeros((2 * points_rows, own_rows))
    lap_halo = np.zeros((2 * points_rows, rows_d))

    def value_column(column, i, j, dx, dy):
        for k in range(-1, nx + 2):
            if k not in line_x.sums(dx):
                column[target(k, j)] += line_x.stiff(k, i) * line_y.mass(j)
        for k in range(-1, ny + 2):
            if k not in line_y.sums(dy):
                column[target(i, k)] += line_y.stiff(k, j) * line_x.mass(i)
        column[points_rows + target(i, j)] += line_x.mass(i) * line_y.mass(j)

    for i, j in own_list:
        value_column(lap_own[:, own(i, j)], i, j, 0, 0)
    for (dx, dy), (start, size, rows) in zip(DIRECTIONS, seg_d):
        for r, (kind, i, j) in enumerate(rows):
            p, q = i - nx * dx, j - ny * dy
            if kind == "v":
                send[start + r, own(p, q)] = 1.0
                value_column(lap_halo[:, start + r], i, j, dx, dy)
            elif kind == "x":
                for k in range(nx):
                    send[start + r, own(k, q)] = line_x.stiff(p, k)
                lap_halo[target(i, j), start + r] += line_y.mass(j)
            else:
                for k in range(ny):
                    send[start + r, own(p, k)] = line_y.stiff(q, k)
                lap_halo[target(i, j), start + r] += line_x.mass(i)
    w_all = np.zeros((coefs, points_rows))
    for i in range(-1, nx + 2):
        for j in range(-1, ny + 2):
            w_all[:, target(i, j)] = forward(i, j)
    masked_backs = []
    for first_x in (0, 1):
        for first_y in (0, 1):
            masked = back.copy()
            for i, j in own_list:
                if (first_x and i == 0) or (first_y and j == 0):
                    masked[own(i, j)] = 0.0
            masked_backs.append(masked)
    t["send_m"] = np.stack([lhs_np(send @ masked / theta_cheb) for masked in masked_backs])
    t["lap_own"], t["lap_halo"] = lhs_np(lap_own), lhs_np(lap_halo)
    stiff_z, mass_z = assemble(ez, stiffness, weights)
    stiff_z = pad_np(stiff_z[:nz, :nz], zl, zl)
    mass_z = np.diag(pad_np(mass_z[None, :nz], 1, zl)[0])
    both_z = [mass_z @ z_fwd, stiff_z @ z_fwd]
    t["z_lap"] = np.stack(
        [rhs_np(np.concatenate([window(matrix, c) for matrix in both_z])) for c in range(2)]
    )
    t["w_all"] = lhs_np(w_all)

    count_x, count_y = mesh_x * ex, mesh_y * ey
    vx, vy = ex + 2, ey + 2
    assert vx == 4 and vy == 4 and count_y % 4 == 0
    half_y = count_y // 2
    dims.update(count_x=count_x, half_y=half_y, lanes=half_y * LANES)
    coarse = np.zeros((3, 16, own_rows))
    for i, j in own_list:
        for w in range(vy):
            for v in range(vx):
                row = 4 * w + v
                coarse[0, row, own(i, j)] = line_x.hats[v, i] * line_y.hats[w, j]
                coarse[1, row, own(i, j)] = (
                    line_x.hats_stiff[v, i] * line_y.hats_mass[w, j]
                    + line_x.hats_mass[v, i] * line_y.hats_stiff[w, j]
                )
                coarse[2, row, own(i, j)] = line_x.hats_mass[v, i] * line_y.hats_mass[w, j]
    t["coarse_b"] = lhs_np(coarse[0])
    coarse_m = [
        lhs_np(np.concatenate([coarse[1] @ masked, coarse[2] @ masked])) for masked in masked_backs
    ]
    t["coarse_m"] = np.stack(coarse_m)
    hats_z = injection_coefficients(ez, points)[:ez]
    phi_z = sine_np(np.arange(ez), ez)
    to_modes = pad_np(hats_z.T @ phi_z, zl, LANES)
    to_modes[0] = 0.0
    t["to_modes"] = rhs_np(np.tile(to_modes, (1, 2)))
    m_modes = np.concatenate([z_back @ mass_z @ to_modes, z_back @ stiff_z @ to_modes])
    t["m_modes"] = rhs_np(np.tile(m_modes, (1, 2)))
    y_in = np.zeros((mesh_y, count_y, 2, 4, 2, LANES))
    y_out = np.zeros((mesh_y, 8, half_y * LANES))
    for p in range(mesh_y):
        inward = sine_np(p * ey - 1 + np.arange(vy), count_y)
        outward = sine_np(p * ey + np.arange(ey + 1), count_y)
        for w in range(vy):
            y_in[p, :, w % 2, :, w // 2, :] = inward[w][:, None, None]
        for q in range(ey + 1):
            for h in range(2):
                y_out[p, 2 * q + h] = np.repeat(outward[q, h * half_y : (h + 1) * half_y], LANES)
    t["y_in"] = y_in.reshape(mesh_y * count_y * 8, 2 * LANES).astype(np.float32)
    x_in = np.zeros((2, count_x, mesh_x, 2, 4))
    x_out = np.zeros((mesh_x, 2, 8, 2, count_x))
    for p in range(mesh_x):
        for h in range(2):
            x_in[h, :, p, h] = sine_np(p * ex - 1 + np.arange(vx), count_x).T
            x_out[p, h, : ex + 1, h] = sine_np(p * ex + np.arange(ex + 1), count_x)
    t["x_in"] = lhs_np(x_in.reshape(2 * count_x, mesh_x * 8))
    mu = np.ones((count_x, count_y, LANES))
    mu[:, :, :ez] = (
        eigen_np(count_x)[:, None, None] + eigen_np(count_y)[None, :, None] + eigen_np(ez)
    )
    mu = mu.reshape(count_x, 2, half_y * LANES).transpose(1, 0, 2)
    t["mu"] = (1.0 / mu).reshape(2 * count_x, half_y * LANES).astype(np.float32)
    t["x_out"] = np.stack([lhs_np(x_out[p].reshape(16, 2 * count_x)) for p in range(mesh_x)])
    t["y_out"] = y_out.astype(np.float32)
    z_out = np.zeros((LANES, zl + 128))
    z_out[:ez, :nz] = phi_z.T @ hats_z
    z_out[:, 0] = 0.0
    z_out[:ez, zl : zl + ez] = phi_z.T
    t["z_out"] = rhs_np(np.tile(z_out, (2, 1)))
    spread = np.zeros((own_rows, 8 * (ey + 1)))
    hats_x, hats_y = line_x.hats[1:], line_y.hats[1:]
    for i, j in own_list:
        for q in range(ey + 1):
            for p in range(ex + 1):
                spread[own(i, j), 8 * q + p] = hats_x[p, i] * hats_y[q, j]
    return t, dims, lhs_np(spread)


def halves(value):
    high = value.astype(jnp.bfloat16)
    return high, (value - high.astype(jnp.float32)).astype(jnp.bfloat16)


def mm(a, b):
    return jnp.dot(a, b, preferred_element_type=jnp.float32)


def left(table, value):
    high, low = halves(value)
    return mm(table, jnp.concatenate([high, low, high], axis=0))


def right(value, table):
    high, low = halves(value)
    return mm(jnp.concatenate([high, low, high], axis=1), table)


def to_coefs(values, table, windows):
    parts = [halves(value) for value in values]
    out = []
    for c, start in enumerate(windows):
        high = [part[0][:, start : start + 256] for part in parts]
        low = [part[1][:, start : start + 256] for part in parts]
        out.append(mm(jnp.concatenate(high + low + high, axis=1), table[c]))
    return jnp.concatenate(out, axis=1)


def from_coefs(value, table, windows, zl):
    total = None
    for c, start in enumerate(windows):
        part = right(value[:, 256 * c : 256 * c + 256], table[c])
        sides = [jnp.zeros((part.shape[0], n), part.dtype) for n in (start, zl - start - 256) if n]
        part = jnp.concatenate([part] + sides if start == 0 else sides + [part], axis=1)
        total = part if total is None else total + part
    return total


PER_DEVICE = ("send_m", "coarse_m", "x_out", "y_out")


def kernel(names, dims, mesh_x, mesh_y, residual, *refs):
    count = len(names)
    far = dict(zip(names, refs[:count]))
    near = dict(zip(names, refs[count + 2 : 2 * count + 2]))
    total_out, nodes_out = refs[count : count + 2]
    (block, own, out_b, in_b, out_d, in_d, out_y, in_y, out_x, in_x,
     local, loaded, sent, got, sent_y, got_y, sent_x, got_x) = refs[2 * count + 2 :]
    nx, ny, nz, pitch = dims["nx"], dims["ny"], dims["nz"], dims["pitch"]
    own_rows, zl, windows = dims["own_rows"], dims["zl"], dims["windows"]
    ix, iy = lax.axis_index("gx"), lax.axis_index("gy")
    def exists(dx, dy):
        return (ix + dx >= 0) & (ix + dx < mesh_x) & (iy + dy >= 0) & (iy + dy < mesh_y)

    in_b[...] = jnp.zeros_like(in_b)
    in_d[...] = jnp.zeros_like(in_d)
    barrier = pltpu.get_barrier_semaphore()
    for o in range(1, mesh_x):
        pl.semaphore_signal(
            barrier, inc=1, device_id=(lax.rem(ix + o, mesh_x), iy), device_id_type=MESH
        )
    for o in range(1, mesh_y):
        pl.semaphore_signal(
            barrier, inc=1, device_id=(ix, lax.rem(iy + o, mesh_y)), device_id_type=MESH
        )
    corners = DIRECTIONS[4:]
    for dx, dy in corners:
        @pl.when(exists(dx, dy))
        def _():
            pl.semaphore_signal(barrier, inc=1, device_id=(ix + dx, iy + dy), device_id_type=MESH)

    residual_in = pltpu.make_async_copy(residual, block, local.at[0])
    residual_in.start()
    start_of_grid = 2 * (ix == 0).astype(jnp.int32) + (iy == 0).astype(jnp.int32)
    place = dict(send_m=start_of_grid, coarse_m=start_of_grid, x_out=ix, y_out=iy)
    loads = {}
    for n, name in enumerate(names):
        src = far[name].at[place[name]] if name in place else far[name]
        loads[name] = pltpu.make_async_copy(src, near[name], loaded.at[n])

    later = names.index("back")
    for name in names[:later]:
        loads[name].start()

    def table(name):
        if name in loads:
            loads.pop(name).wait()
        return near[name][...]

    own[...] = jnp.zeros_like(own)
    row = lax.broadcasted_iota(jnp.int32, (own_rows, 1), 0)
    node_x, node_y = ix * nx + row // pitch, iy * ny + row % pitch
    keep = ((node_x > 0) & (node_y > 0) & (row % pitch < ny) & (row // pitch < nx)).astype(
        jnp.float32
    )
    residual_in.wait()
    for i in range(nx):
        own[i * pitch : i * pitch + ny, 0:nz] = block[i]
    source = own[...] * keep
    high, low = halves(source)
    pick = table("pick")
    out_b[...] = mm(pick, high) + mm(pick, low)

    greetings = mesh_x - 1 + mesh_y - 1
    for dx, dy in corners:
        greetings = greetings + exists(dx, dy).astype(jnp.int32)
    pl.semaphore_wait(barrier, greetings)

    def halo(phase, src, dst, places):
        copies = []
        for d, (dx, dy) in enumerate(DIRECTIONS):
            start, size = places[d]
            copies.append(
                pltpu.make_async_remote_copy(
                    src_ref=src.at[pl.ds(start, size)],
                    dst_ref=dst.at[pl.ds(start, size)],
                    send_sem=sent.at[phase, d],
                    recv_sem=got.at[phase, d],
                    device_id=(ix - dx, iy - dy),
                    device_id_type=MESH,
                )
            )
        for d, (dx, dy) in enumerate(DIRECTIONS):
            pl.when(exists(-dx, -dy))(copies[d].start)
        return copies

    def arrived(copies):
        for d, (dx, dy) in enumerate(DIRECTIONS):
            pl.when(exists(dx, dy))(copies[d].wait_recv)

    def left_here(copies):
        for d, (dx, dy) in enumerate(DIRECTIONS):
            pl.when(exists(-dx, -dy))(copies[d].wait_send)

    copies_b = halo(0, out_b, in_b, dims["seg_b"])
    for name in names[later:]:
        loads[name].start()
    z_fwd = table("z_fwd")
    coefs = left(table("w_own"), to_coefs([source], z_fwd, windows))
    coarse_b = right(left(table("coarse_b"), source), table("to_modes"))
    arrived(copies_b)
    coefs = coefs + left(table("w_halo"), to_coefs([in_b[...]], z_fwd, windows))
    modes_0 = coefs * table("inverse")
    z_back = table("z_back")
    out_d[...] = from_coefs(left(table("send_m"), modes_0), z_back, windows, zl)
    copies_d = halo(1, out_d, in_d, dims["seg_d"])
    first = from_coefs(left(table("back"), modes_0), z_back, windows, zl)
    first = first * (keep * (1.0 / theta_cheb))
    applied = left(table("lap_own"), first)
    rows, wide_y = dims["points_rows"], dims["wide_y"]
    spot = lax.broadcasted_iota(jnp.int32, (rows, 1), 0)
    spot_x, spot_y = ix * nx + spot // wide_y - 1, iy * ny + spot % wide_y - 1
    inside = (spot_x > 0) & (spot_x < mesh_x * nx) & (spot_y > 0) & (spot_y < mesh_y * ny)
    inside = inside.astype(jnp.float32)
    arrived(copies_d)
    applied = applied + left(table("lap_halo"), in_d[...])
    applied = [applied[:rows] * inside, applied[rows:] * inside]
    coefs = coefs - left(table("w_all"), to_coefs(applied, table("z_lap"), windows))
    sigma = theta_cheb / delta_cheb
    rho_0 = 1.0 / sigma
    rho_1 = 1.0 / (2.0 * sigma - rho_0)
    weight_0, weight_1 = (1.0 + rho_1 * rho_0) / theta_cheb, 2.0 * rho_1 / delta_cheb
    modes = weight_0 * modes_0 + weight_1 * (coefs * table("inverse"))

    lanes = dims["lanes"]
    shares = left(table("coarse_m"), modes)
    shares = jnp.concatenate([shares[:16], shares[16:]], axis=1)
    share = coarse_b - right(shares, table("m_modes"))
    lower_lanes = lax.broadcasted_iota(jnp.int32, (8, 128), 1) < LANES
    lower_rows = lax.broadcasted_iota(jnp.int32, (8, 128), 0) < 4
    share = jnp.where(lower_lanes, share[:8], share[8:])

    def everyone(value, src, dst, count, me, send_sems, recv_sems, place):
        src[...] = value
        copies = []
        for o in range(1, count):
            to = lax.rem(me + o, count)
            copies.append(
                pltpu.make_async_remote_copy(
                    src_ref=src,
                    dst_ref=dst.at[me],
                    send_sem=send_sems.at[o],
                    recv_sem=recv_sems.at[o],
                    device_id=place(to),
                    device_id_type=MESH,
                )
            )
        for copy in copies:
            copy.start()
        dst[me] = value
        return copies

    def all_here(copies):
        for copy in copies:
            copy.wait_recv()

    copies_y = everyone(
        share, out_y, in_y, mesh_y, iy, sent_y, got_y, lambda to: (ix, to)
    )
    total = left(table("back"), modes)
    all_here(copies_y)
    half = dims["half_y"]
    y_in = table("y_in").reshape(mesh_y, 2 * half * 8, 128)
    tiles = []
    for b in range(2 * half):
        tile = sum(in_y[p] * y_in[p, 8 * b : 8 * b + 8] for p in range(mesh_y))
        tile = tile + pltpu.roll(tile, LANES, 1)
        tiles.append(tile + pltpu.roll(tile, 4, 0))
    blocks = []
    for b in range(0, half, 2):
        lower = jnp.where(lower_lanes, tiles[b], tiles[b + 1])
        upper = jnp.where(lower_lanes, tiles[half + b], tiles[half + b + 1])
        blocks.append(jnp.where(lower_rows, lower, upper))
    share = jnp.concatenate(blocks, axis=1)
    copies_x = everyone(
        share, out_x, in_x, mesh_x, ix, sent_x, got_x, lambda to: (to, iy)
    )
    own[...] = from_coefs(total, z_back, windows, zl) * keep
    total_copy = pltpu.make_async_copy(own, total_out, local.at[1])
    total_copy.start()
    all_here(copies_x)
    gathered = in_x[...].reshape(mesh_x * 8, lanes)
    scaled = left(table("x_in"), gathered) * table("mu")
    lines = left(table("x_out"), scaled)
    y_out = table("y_out")
    by_row = []
    for q in range(ny // 7 + 1):
        line = lines[:8] * y_out[2 * q : 2 * q + 1] + lines[8:] * y_out[2 * q + 1 : 2 * q + 2]
        by_row.append(sum(line[:, 128 * b : 128 * b + 128] for b in range(lanes // 128)))
    nodes_out[...] = right(jnp.concatenate(by_row, axis=0), table("z_out"))
    total_copy.wait()
    left_here(copies_b)
    left_here(copies_d)
    for copy in copies_y + copies_x:
        copy.wait_send()


def finish(dims, spread, total, nodes, fine_out, coarse_out):
    nx, ny, nz, pitch, zl = dims["nx"], dims["ny"], dims["nz"], dims["pitch"], dims["zl"]
    ix, iy = lax.axis_index("gx"), lax.axis_index("gy")
    row = lax.broadcasted_iota(jnp.int32, (dims["own_rows"], 1), 0)
    keep = (ix * nx + row // pitch > 0) & (iy * ny + row % pitch > 0)
    values = nodes[...]
    for p in range(nx // 7):
        for q in range(ny // 7):
            line = values[8 * q + p : 8 * q + p + 1, zl : zl + nz // 7]
            coarse_out[p, q : q + 1, :] = line
    prolonged = left(spread[...], values[:, :zl])
    result = total[...] + prolonged * keep.astype(jnp.float32)
    for i in range(nx):
        fine_out[i] = result[i * pitch : i * pitch + ny, :nz]


def per_device(mesh_x, mesh_y, residual_in):
    t, dims, spread = tables(mesh_x, mesh_y, residual_in.shape)
    names = list(t)
    nx, ny, nz = residual_in.shape
    own_rows, zl, lanes = dims["own_rows"], dims["zl"], dims["lanes"]
    f32 = jnp.float32
    vmem = pl.BlockSpec(memory_space=pltpu.VMEM)
    total, nodes = pl.pallas_call(
        functools.partial(kernel, names, dims, mesh_x, mesh_y),
        out_shape=(
            jax.ShapeDtypeStruct((own_rows, zl), f32),
            jax.ShapeDtypeStruct((8 * (ny // 7 + 1), zl + 128), f32),
        ),
        in_specs=[pl.BlockSpec(memory_space=pl.ANY)] * (1 + len(names)),
        out_specs=(pl.BlockSpec(memory_space=pl.ANY), vmem),
        scratch_shapes=[
            pltpu.VMEM(t[name].shape[name in PER_DEVICE :], t[name].dtype) for name in names
        ]
        + [
            pltpu.VMEM((nx, ny, nz), f32),
            pltpu.VMEM((own_rows, zl), f32),
            pltpu.VMEM((dims["rows_b"], zl), f32),
            pltpu.VMEM((dims["rows_b"], zl), f32),
            pltpu.VMEM((dims["rows_d"], zl), f32),
            pltpu.VMEM((dims["rows_d"], zl), f32),
            pltpu.VMEM((8, 128), f32),
            pltpu.VMEM((mesh_y, 8, 128), f32),
            pltpu.VMEM((8, lanes), f32),
            pltpu.VMEM((mesh_x, 8, lanes), f32),
            pltpu.SemaphoreType.DMA((2,)),
            pltpu.SemaphoreType.DMA((len(names),)),
            pltpu.SemaphoreType.DMA((2, 8)),
            pltpu.SemaphoreType.DMA((2, 8)),
            pltpu.SemaphoreType.DMA((mesh_y,)),
            pltpu.SemaphoreType.DMA((mesh_y,)),
            pltpu.SemaphoreType.DMA((mesh_x,)),
            pltpu.SemaphoreType.DMA((mesh_x,)),
        ],
        compiler_params=pltpu.CompilerParams(
            collective_id=0, has_side_effects=True, vmem_limit_bytes=56 * 2**20
        ),
        cost_estimate=pl.CostEstimate(flops=10**9, bytes_accessed=10**7, transcendentals=0),
    )(residual_in, *[jnp.asarray(t[name]) for name in names])
    return pl.pallas_call(
        functools.partial(finish, dims),
        out_shape=(
            jax.ShapeDtypeStruct((nx, ny, nz), f32),
            jax.ShapeDtypeStruct((nx // 7, ny // 7, nz // 7), f32),
        ),
        in_specs=[vmem] * 3,
        out_specs=(vmem, vmem),
        compiler_params=pltpu.CompilerParams(vmem_limit_bytes=56 * 2**20),
        cost_estimate=pl.CostEstimate(flops=10**7, bytes_accessed=10**6, transcendentals=0),
    )(jnp.asarray(spread), total, nodes)


def solution(mesh):
    return jax.shard_map(
        functools.partial(per_device, mesh.shape["gx"], mesh.shape["gy"]),
        mesh=mesh,
        in_specs=(P("gx", "gy", None),),
        out_specs=(P("gx", "gy", None), P("gx", "gy", None)),
        check_vma=False,
    )
```

```python
import functools
import math

import jax
import jax.numpy as jnp
import ml_dtypes
import numpy as np
from jax import lax
from jax.experimental import pallas as pl
from jax.experimental.pallas import tpu as pltpu
from jax.sharding import PartitionSpec as P

theta_cheb = 1.125
delta_cheb = 0.875
start_points = [
    -0.8717401485096066,
    -0.5917001814331423,
    -0.2092992179024789,
    0.2092992179024789,
    0.5917001814331423,
    0.8717401485096066,
]


def legendre_pair(value):
    before, now = (1.0, value)
    for order in range(1, 7):
        before, now = (now, ((2 * order + 1) * value * now - order * before) / (order + 1))
    return (now, before)


def lobatto_tables():
    point_list = [-1.0]
    for guess in start_points:
        place = guess
        for newton in range(4):
            seventh, sixth = legendre_pair(place)
            slope = 7.0 * (place * seventh - sixth) / (place * place - 1.0)
            curve = (2.0 * place * slope - 56.0 * seventh) / (1.0 - place * place)
            place = place - slope / curve
        point_list.append(place)
    point_list.append(1.0)
    sample_nodes_list = np.array(point_list)
    values = np.array([legendre_pair(place)[0] for place in point_list])
    weights = 2.0 / (56.0 * values * values)
    derivative = np.zeros((8, 8))
    for i in range(8):
        for j in range(8):
            if i != j:
                derivative[i, j] = values[i] / (
                    values[j] * (sample_nodes_list[i] - sample_nodes_list[j])
                )
    derivative[0, 0] = -14.0
    derivative[7, 7] = 14.0
    stiffness = derivative.T @ (weights[:, None] * derivative)
    return (sample_nodes_list, weights, stiffness)


def assemble(elements, stiffness, weights):
    width = 7 * elements + 1
    assembled = np.zeros((width, width))
    masses = np.zeros(width)
    for e in range(elements):
        assembled[7 * e : 7 * e + 8, 7 * e : 7 * e + 8] += stiffness
        masses[7 * e : 7 * e + 8] += weights
    return (assembled, masses)


def jacobi_eigen(matrix):
    order = matrix.shape[0]
    work = [[float(matrix[i, j]) for j in range(order)] for i in range(order)]
    vectors = [[1.0 if i == j else 0.0 for j in range(order)] for i in range(order)]
    for sweep in range(12):
        for p in range(order):
            for q in range(p + 1, order):
                angle = 0.5 * math.atan2(2.0 * work[p][q], work[q][q] - work[p][p])
                cosine = math.cos(angle)
                sine = math.sin(angle)
                for k in range(order):
                    left, right = (work[k][p], work[k][q])
                    work[k][p] = cosine * left - sine * right
                    work[k][q] = sine * left + cosine * right
                for k in range(order):
                    left, right = (work[p][k], work[q][k])
                    work[p][k] = cosine * left - sine * right
                    work[q][k] = sine * left + cosine * right
                for k in range(order):
                    left, right = (vectors[k][p], vectors[k][q])
                    vectors[k][p] = cosine * left - sine * right
                    vectors[k][q] = sine * left + cosine * right
    return (np.array([work[i][i] for i in range(order)]), np.array(vectors))


def schwarz_basis():
    sample_nodes_list, weights, stiffness = lobatto_tables()
    assembled, masses = assemble(3, stiffness, weights)
    block_stiff = assembled[6:16, 6:16]
    inv_root = 1.0 / np.sqrt(masses[6:16])
    eigen_vals, eigen_vecs = jacobi_eigen(inv_root[:, None] * block_stiff * inv_root[None, :])
    return (inv_root[:, None] * eigen_vecs, eigen_vals)


def injection_coefficients(elements, sample_nodes_list):
    matrix = np.zeros((elements + 1, 7 * elements))
    for e in range(elements):
        for m in range(7):
            matrix[e, 7 * e + m] += (1.0 - sample_nodes_list[m]) / 2.0
            matrix[e + 1, 7 * e + m] += (1.0 + sample_nodes_list[m]) / 2.0
    return matrix


MESH = pl.DeviceIdType.MESH
LANES = 64
DIRECTIONS = [(-1, 0), (1, 0), (0, -1), (0, 1), (-1, -1), (-1, 1), (1, -1), (1, 1)]


def round_up(value, unit):
    return -(-value // unit) * unit


def sine_np(vertices, elements):
    modes = np.arange(elements)
    vertex = np.asarray(vertices)[:, None]
    entries = np.sqrt(2.0 / elements) * np.sin(np.pi * (vertex * modes % (2 * elements)) / elements)
    entries = entries / np.sqrt((4.0 + 2.0 * np.cos(np.pi * modes / elements)) / 3.0)
    inside = (modes > 0) & (vertex > 0) & (vertex < elements)
    return np.where(inside, entries, 0.0)


def eigen_np(elements):
    modes = np.arange(elements)
    cosine = np.cos(np.pi * modes / elements)
    return np.where(modes > 0, 3.0 * (1.0 - cosine) / (4.0 + 2.0 * cosine), 1.0)


def split_np(matrix, axis):
    high = matrix.astype(np.float32).astype(ml_dtypes.bfloat16)
    low = (matrix - high.astype(np.float64)).astype(np.float32).astype(ml_dtypes.bfloat16)
    return np.concatenate([high, high, low], axis=axis)


def lhs_np(matrix):
    return split_np(pad_np(matrix, round_up(matrix.shape[0], 16), matrix.shape[1]), 1)


def rhs_np(matrix):
    return split_np(matrix, 0)


def pad_np(matrix, rows, columns, value=0.0):
    out = np.full((rows, columns), value)
    out[: matrix.shape[0], : matrix.shape[1]] = matrix
    return out


class Line:
    def __init__(self, elements, stiffness, weights, eigen_basis, points):
        self.elements = elements
        self.nodes = 7 * elements
        around, masses = assemble(elements + 4, stiffness, weights)
        self.around, self.masses, self.shift = around, masses, 14
        self.forward = np.zeros((10 * elements, self.nodes + 3))
        self.backward = np.zeros((self.nodes, 10 * elements))
        for e in range(elements):
            self.forward[10 * e : 10 * e + 10, 7 * e : 7 * e + 10] = eigen_basis.T
            self.backward[7 * e : 7 * e + 7, 10 * e : 10 * e + 10] = eigen_basis[1:8]
        hats = injection_coefficients(elements + 4, points)
        kept = slice(self.shift, self.shift + self.nodes)
        rows = slice(1, 1 + elements + 2)
        full = np.zeros((hats.shape[0], self.around.shape[0]))
        full[:, : hats.shape[1]] = hats
        self.hats = hats[rows, kept]
        self.hats_stiff = (full @ around)[rows, kept]
        self.hats_mass = (full * masses)[rows, kept]

    def stiff(self, i, j):
        return self.around[i + self.shift, j + self.shift]

    def mass(self, i):
        return self.masses[i + self.shift]

    def values(self, side):
        n = self.nodes
        return {-1: [-1], 0: list(range(n)), 1: [n, n + 1]}[side]

    def sums(self, side):
        n = self.nodes
        return {-1: [-1, 0], 0: [], 1: [n, n + 1]}[side]


def segments(lines, with_sums):
    line_x, line_y = lines
    out, start = [], 0
    for dx, dy in DIRECTIONS:
        rows = [("v", i, j) for i in line_x.values(dx) for j in line_y.values(dy)]
        if with_sums:
            rows += [("x", i, j) for i in line_x.sums(dx) for j in line_y.values(dy)]
            rows += [("y", i, j) for i in line_x.values(dx) for j in line_y.sums(dy)]
        size = round_up(len(rows), 8)
        out.append((start, size, rows))
        start += size
    return out, start


def tables(mesh_x, mesh_y, shape):
    points, weights, stiffness = lobatto_tables()
    eigen_basis, eigen_vals = schwarz_basis()
    nx, ny, nz = shape
    ex, ey, ez = nx // 7, ny // 7, nz // 7
    line_x = Line(ex, stiffness, weights, eigen_basis, points)
    line_y = Line(ey, stiffness, weights, eigen_basis, points)
    lines = (line_x, line_y)
    pitch = round_up(ny, 8)
    own_rows = round_up(nx * pitch, 16)
    zl = round_up(nz, 128)
    half_z = ez // 2
    assert ez % 2 == 0 and 10 * half_z <= 256 and zl >= 256
    cl = 512
    windows = [0, zl - 256]
    coefs = 100 * ex * ey
    own = lambda i, j: i * pitch + j
    own_list = [(i, j) for i in range(nx) for j in range(ny)]
    t = {}
    dims = dict(nx=nx, ny=ny, nz=nz, pitch=pitch, own_rows=own_rows, zl=zl, windows=windows)

    forward = lambda i, j: np.kron(line_x.forward[:, i + 1], line_y.forward[:, j + 1])
    seg_b, rows_b = segments(lines, False)
    seg_d, rows_d = segments(lines, True)
    rows_d = round_up(rows_d, 16)
    dims.update(seg_b=[s[:2] for s in seg_b], rows_b=rows_b)
    dims.update(seg_d=[s[:2] for s in seg_d], rows_d=rows_d)

    pick = np.zeros((rows_b, own_rows))
    w_halo = np.zeros((coefs, rows_b))
    for (dx, dy), (start, size, rows) in zip(DIRECTIONS, seg_b):
        for r, (kind, i, j) in enumerate(rows):
            pick[start + r, own(i - nx * dx, j - ny * dy)] = 1.0
            w_halo[:, start + r] = forward(i, j)
    w_own = np.zeros((coefs, own_rows))
    back = np.zeros((own_rows, coefs))
    for i, j in own_list:
        w_own[:, own(i, j)] = forward(i, j)
        back[own(i, j)] = np.kron(line_x.backward[i], line_y.backward[j])
    z_fwd = np.zeros((zl, cl))
    z_back = np.zeros((cl, zl))
    l_z = np.ones(cl)
    for e in range(ez):
        lane = 256 * (e // half_z) + 10 * (e % half_z)
        l_z[lane : lane + 10] = eigen_vals
        for m in range(10):
            z = 7 * e - 1 + m
            if 0 < z < nz:
                z_fwd[z, lane : lane + 10] = eigen_basis[m]
                if 1 <= m <= 7:
                    z_back[lane : lane + 10, z] = eigen_basis[m]
    l_x, l_y = np.tile(eigen_vals, ex), np.tile(eigen_vals, ey)
    inverse = 1.0 / ((l_x[:, None] + l_y[None, :]).reshape(coefs, 1) + l_z)

    def window(matrix, c):
        kept = matrix[windows[c] : windows[c] + 256, 256 * c : 256 * c + 256]
        assert np.count_nonzero(kept) == np.count_nonzero(matrix[:, 256 * c : 256 * c + 256])
        return kept

    t["z_fwd"] = np.stack([rhs_np(window(z_fwd, c)) for c in range(2)])
    t["pick"] = pick.astype(ml_dtypes.bfloat16)
    t["w_own"] = lhs_np(w_own)
    t["coarse_b"] = None
    t["to_modes"] = None
    t["w_halo"] = lhs_np(w_halo)
    t["inverse"] = inverse.astype(np.float32)
    t["send_m"] = None
    t["z_back"] = np.stack([rhs_np(window(z_back.T, c).T) for c in range(2)])
    t["back"] = lhs_np(back)

    send = np.zeros((rows_d, own_rows))
    wide_y = ny + 3
    points_rows = round_up((nx + 3) * wide_y, 16)
    target = lambda i, j: (i + 1) * wide_y + (j + 1)
    inside_x = lambda i: -1 <= i <= nx + 1
    inside_y = lambda j: -1 <= j <= ny + 1
    lap_own = np.zeros((2 * points_rows, own_rows))
    lap_halo = np.zeros((2 * points_rows, rows_d))

    def value_column(column, i, j, dx, dy):
        for k in range(-1, nx + 2):
            if k not in line_x.sums(dx):
                column[target(k, j)] += line_x.stiff(k, i) * line_y.mass(j)
        for k in range(-1, ny + 2):
            if k not in line_y.sums(dy):
                column[target(i, k)] += line_y.stiff(k, j) * line_x.mass(i)
        column[points_rows + target(i, j)] += line_x.mass(i) * line_y.mass(j)

    for i, j in own_list:
        value_column(lap_own[:, own(i, j)], i, j, 0, 0)
    for (dx, dy), (start, size, rows) in zip(DIRECTIONS, seg_d):
        for r, (kind, i, j) in enumerate(rows):
            p, q = i - nx * dx, j - ny * dy
            if kind == "v":
                send[start + r, own(p, q)] = 1.0
                value_column(lap_halo[:, start + r], i, j, dx, dy)
            elif kind == "x":
                for k in range(nx):
                    send[start + r, own(k, q)] = line_x.stiff(p, k)
                lap_halo[target(i, j), start + r] += line_y.mass(j)
            else:
                for k in range(ny):
                    send[start + r, own(p, k)] = line_y.stiff(q, k)
                lap_halo[target(i, j), start + r] += line_x.mass(i)
    w_all = np.zeros((coefs, points_rows))
    for i in range(-1, nx + 2):
        for j in range(-1, ny + 2):
            w_all[:, target(i, j)] = forward(i, j)
    masked_backs = []
    for first_x in (0, 1):
        for first_y in (0, 1):
            masked = back.copy()
            for i, j in own_list:
                if (first_x and i == 0) or (first_y and j == 0):
                    masked[own(i, j)] = 0.0
            masked_backs.append(masked)
    t["send_m"] = np.stack([lhs_np(send @ masked / theta_cheb) for masked in masked_backs])
    stiff_z, mass_z = assemble(ez, stiffness, weights)
    stiff_z = pad_np(stiff_z[:nz, :nz], zl, zl)
    mass_z = np.diag(pad_np(mass_z[None, :nz], 1, zl)[0])
    both_z = [mass_z @ z_fwd, stiff_z @ z_fwd]
    t["z_lap"] = np.stack(
        [rhs_np(np.concatenate([window(matrix, c) for matrix in both_z], 1)) for c in range(2)]
    )
    t["lap_own"], t["lap_halo"] = [], []
    for place_x in range(3):
        for place_y in range(3):
            inner = np.zeros(points_rows)
            for i in range(-1, nx + 2):
                for j in range(-1, ny + 2):
                    out_x = (place_x == 0 and i <= 0) or (place_x == 2 and i >= nx)
                    out_y = (place_y == 0 and j <= 0) or (place_y == 2 and j >= ny)
                    inner[target(i, j)] = 0.0 if out_x or out_y else 1.0
            masked = w_all * inner
            for name, lap in (("lap_own", lap_own), ("lap_halo", lap_halo)):
                pair = [masked @ lap[:points_rows], masked @ lap[points_rows:]]
                pair = np.concatenate(pair, 1)
                t[name].append(lhs_np(pair)[:, pair.shape[1] :])
    t["lap_own"], t["lap_halo"] = np.stack(t["lap_own"]), np.stack(t["lap_halo"])

    count_x, count_y = mesh_x * ex, mesh_y * ey
    vx, vy = ex + 2, ey + 2
    assert vx == 4 and vy == 4 and count_y % 4 == 0
    half_y = count_y // 2
    dims.update(count_x=count_x, half_y=half_y, lanes=half_y * LANES)
    coarse = np.zeros((3, 16, own_rows))
    for i, j in own_list:
        for w in range(vy):
            for v in range(vx):
                row = 4 * w + v
                coarse[0, row, own(i, j)] = line_x.hats[v, i] * line_y.hats[w, j]
                coarse[1, row, own(i, j)] = (
                    line_x.hats_stiff[v, i] * line_y.hats_mass[w, j]
                    + line_x.hats_mass[v, i] * line_y.hats_stiff[w, j]
                )
                coarse[2, row, own(i, j)] = line_x.hats_mass[v, i] * line_y.hats_mass[w, j]
    t["coarse_b"] = lhs_np(coarse[0])
    coarse_m = [
        lhs_np(np.concatenate([coarse[1] @ masked, coarse[2] @ masked])) for masked in masked_backs
    ]
    t["coarse_m"] = np.stack(coarse_m)
    hats_z = injection_coefficients(ez, points)[:ez]
    phi_z = sine_np(np.arange(ez), ez)
    to_modes = pad_np(hats_z.T @ phi_z, zl, LANES)
    to_modes[0] = 0.0
    t["to_modes"] = rhs_np(np.tile(to_modes, (1, 2)))
    m_modes = np.concatenate([z_back @ mass_z @ to_modes, z_back @ stiff_z @ to_modes])
    t["m_modes"] = rhs_np(np.tile(m_modes, (1, 2)))
    y_in = np.zeros((mesh_y, count_y, 2, 4, 2, LANES))
    y_out = np.zeros((mesh_y, 8, half_y * LANES))
    for p in range(mesh_y):
        inward = sine_np(p * ey - 1 + np.arange(vy), count_y)
        outward = sine_np(p * ey + np.arange(ey + 1), count_y)
        for w in range(vy):
            y_in[p, :, w % 2, :, w // 2, :] = inward[w][:, None, None]
        for q in range(ey + 1):
            for h in range(2):
                y_out[p, 2 * q + h] = np.repeat(outward[q, h * half_y : (h + 1) * half_y], LANES)
    t["y_in"] = y_in.reshape(mesh_y * count_y * 8, 2 * LANES).astype(np.float32)
    x_in = np.zeros((2, count_x, mesh_x, 2, 4))
    x_out = np.zeros((mesh_x, 2, 8, 2, count_x))
    for p in range(mesh_x):
        for h in range(2):
            x_in[h, :, p, h] = sine_np(p * ex - 1 + np.arange(vx), count_x).T
            x_out[p, h, : ex + 1, h] = sine_np(p * ex + np.arange(ex + 1), count_x)
    t["x_in"] = lhs_np(x_in.reshape(2 * count_x, mesh_x * 8))
    mu = np.ones((count_x, count_y, LANES))
    mu[:, :, :ez] = (
        eigen_np(count_x)[:, None, None] + eigen_np(count_y)[None, :, None] + eigen_np(ez)
    )
    mu = mu.reshape(count_x, 2, half_y * LANES).transpose(1, 0, 2)
    t["mu"] = (1.0 / mu).reshape(2 * count_x, half_y * LANES).astype(np.float32)
    t["x_out"] = np.stack([lhs_np(x_out[p].reshape(16, 2 * count_x)) for p in range(mesh_x)])
    t["y_out"] = y_out.astype(np.float32)
    z_out = np.zeros((LANES, zl + 128))
    z_out[:ez, :nz] = phi_z.T @ hats_z
    z_out[:, 0] = 0.0
    z_out[:ez, zl : zl + ez] = phi_z.T
    t["z_out"] = rhs_np(np.tile(z_out, (2, 1)))
    spread = np.zeros((own_rows, 8 * (ey + 1)))
    hats_x, hats_y = line_x.hats[1:], line_y.hats[1:]
    for i, j in own_list:
        for q in range(ey + 1):
            for p in range(ex + 1):
                spread[own(i, j), 8 * q + p] = hats_x[p, i] * hats_y[q, j]
    return t, dims, lhs_np(spread)


def halves(value):
    high = value.astype(jnp.bfloat16)
    return high, (value - high.astype(jnp.float32)).astype(jnp.bfloat16)


def mm(a, b):
    return jnp.dot(a, b, preferred_element_type=jnp.float32)


def left(table, value):
    high, low = halves(value)
    return mm(table, jnp.concatenate([high, low, high], axis=0))


def left_two(table, value):
    high, low = halves(value)
    both = mm(table, jnp.concatenate([high, high], axis=0))
    return both + mm(table[:, : value.shape[0]], low)


def right(value, table):
    high, low = halves(value)
    return mm(jnp.concatenate([high, low, high], axis=1), table)


def to_coefs(value, table, windows):
    high, low = halves(value)
    out = []
    for c, start in enumerate(windows):
        near = slice(start, start + 256)
        out.append(mm(jnp.concatenate([high[:, near], low[:, near], high[:, near]], 1), table[c]))
    count = out[0].shape[1] // 256
    rows = [
        jnp.concatenate([part[:, 256 * n : 256 * n + 256] for part in out], 1) for n in range(count)
    ]
    return rows[0] if count == 1 else jnp.concatenate(rows, 0)


def from_coefs(value, table, windows, zl):
    total = None
    for c, start in enumerate(windows):
        part = right(value[:, 256 * c : 256 * c + 256], table[c])
        sides = [jnp.zeros((part.shape[0], n), part.dtype) for n in (start, zl - start - 256) if n]
        part = jnp.concatenate([part] + sides if start == 0 else sides + [part], axis=1)
        total = part if total is None else total + part
    return total


PER_DEVICE = ("send_m", "lap_own", "lap_halo", "coarse_m", "x_out", "y_out")


def kernel(names, dims, mesh_x, mesh_y, residual, *refs):
    count = len(names)
    far = dict(zip(names, refs[:count]))
    near = dict(zip(names, refs[count + 2 : 2 * count + 2]))
    total_out, nodes_out = refs[count : count + 2]
    (block, own, out_b, in_b, out_d, in_d, out_y, in_y, out_x, in_x,
     local, loaded, sent, got, sent_y, got_y, sent_x, got_x) = refs[2 * count + 2 :]
    nx, ny, nz, pitch = dims["nx"], dims["ny"], dims["nz"], dims["pitch"]
    own_rows, zl, windows = dims["own_rows"], dims["zl"], dims["windows"]
    ix, iy = lax.axis_index("gx"), lax.axis_index("gy")
    def exists(dx, dy):
        return (ix + dx >= 0) & (ix + dx < mesh_x) & (iy + dy >= 0) & (iy + dy < mesh_y)

    in_b[...] = jnp.zeros_like(in_b)
    in_d[...] = jnp.zeros_like(in_d)
    barrier = pltpu.get_barrier_semaphore()
    for o in range(1, mesh_x):
        pl.semaphore_signal(
            barrier, inc=1, device_id=(lax.rem(ix + o, mesh_x), iy), device_id_type=MESH
        )
    for o in range(1, mesh_y):
        pl.semaphore_signal(
            barrier, inc=1, device_id=(ix, lax.rem(iy + o, mesh_y)), device_id_type=MESH
        )
    corners = DIRECTIONS[4:]
    for dx, dy in corners:
        @pl.when(exists(dx, dy))
        def _():
            pl.semaphore_signal(barrier, inc=1, device_id=(ix + dx, iy + dy), device_id_type=MESH)

    residual_in = pltpu.make_async_copy(residual, block, local.at[0])
    residual_in.start()
    start_of_grid = 2 * (ix == 0).astype(jnp.int32) + (iy == 0).astype(jnp.int32)
    place_x = 1 - (ix == 0).astype(jnp.int32) + (ix == mesh_x - 1).astype(jnp.int32)
    place_y = 1 - (iy == 0).astype(jnp.int32) + (iy == mesh_y - 1).astype(jnp.int32)
    in_grid = 3 * place_x + place_y
    place = dict(send_m=start_of_grid, lap_own=in_grid, lap_halo=in_grid)
    place.update(coarse_m=start_of_grid, x_out=ix, y_out=iy)
    loads = {}
    for n, name in enumerate(names):
        src = far[name].at[place[name]] if name in place else far[name]
        loads[name] = pltpu.make_async_copy(src, near[name], loaded.at[n])

    later = names.index("back")
    for name in names[:later]:
        loads[name].start()

    def table(name):
        if name in loads:
            loads.pop(name).wait()
        return near[name][...]

    own[...] = jnp.zeros_like(own)
    row = lax.broadcasted_iota(jnp.int32, (own_rows, 1), 0)
    node_x, node_y = ix * nx + row // pitch, iy * ny + row % pitch
    keep = ((node_x > 0) & (node_y > 0) & (row % pitch < ny) & (row // pitch < nx)).astype(
        jnp.float32
    )
    residual_in.wait()
    for i in range(nx):
        own[i * pitch : i * pitch + ny, 0:nz] = block[i]
    source = own[...] * keep
    high, low = halves(source)
    pick = table("pick")
    out_b[...] = mm(pick, high) + mm(pick, low)

    greetings = mesh_x - 1 + mesh_y - 1
    for dx, dy in corners:
        greetings = greetings + exists(dx, dy).astype(jnp.int32)
    pl.semaphore_wait(barrier, greetings)

    def halo(phase, src, dst, places):
        copies = []
        for d, (dx, dy) in enumerate(DIRECTIONS):
            start, size = places[d]
            copies.append(
                pltpu.make_async_remote_copy(
                    src_ref=src.at[pl.ds(start, size)],
                    dst_ref=dst.at[pl.ds(start, size)],
                    send_sem=sent.at[phase, d],
                    recv_sem=got.at[phase, d],
                    device_id=(ix - dx, iy - dy),
                    device_id_type=MESH,
                )
            )
        for d in (2, 3, 4, 5, 6, 7, 0, 1):
            dx, dy = DIRECTIONS[d]
            pl.when(exists(-dx, -dy))(copies[d].start)
        return copies

    def arrived(copies):
        for d, (dx, dy) in enumerate(DIRECTIONS):
            pl.when(exists(dx, dy))(copies[d].wait_recv)

    def left_here(copies):
        for d, (dx, dy) in enumerate(DIRECTIONS):
            pl.when(exists(-dx, -dy))(copies[d].wait_send)

    copies_b = halo(0, out_b, in_b, dims["seg_b"])
    for name in names[later:]:
        loads[name].start()
    z_fwd = table("z_fwd")
    coefs = left(table("w_own"), to_coefs(source, z_fwd, windows))
    coarse_b = right(left(table("coarse_b"), source), table("to_modes"))
    arrived(copies_b)
    coefs = coefs + left(table("w_halo"), to_coefs(in_b[...], z_fwd, windows))
    modes_0 = coefs * table("inverse")
    z_back = table("z_back")
    out_d[...] = from_coefs(left(table("send_m"), modes_0), z_back, windows, zl)
    copies_d = halo(1, out_d, in_d, dims["seg_d"])
    first = from_coefs(left(table("back"), modes_0), z_back, windows, zl)
    first = first * (keep * (1.0 / theta_cheb))
    z_lap = table("z_lap")
    coefs = coefs - left_two(table("lap_own"), to_coefs(first, z_lap, windows))
    arrived(copies_d)
    coefs = coefs - left_two(table("lap_halo"), to_coefs(in_d[...], z_lap, windows))
    sigma = theta_cheb / delta_cheb
    rho_0 = 1.0 / sigma
    rho_1 = 1.0 / (2.0 * sigma - rho_0)
    weight_0, weight_1 = (1.0 + rho_1 * rho_0) / theta_cheb, 2.0 * rho_1 / delta_cheb
    modes = weight_0 * modes_0 + weight_1 * (coefs * table("inverse"))

    lanes = dims["lanes"]
    shares = left(table("coarse_m"), modes)
    shares = jnp.concatenate([shares[:16], shares[16:]], axis=1)
    share = coarse_b - right(shares, table("m_modes"))
    lower_lanes = lax.broadcasted_iota(jnp.int32, (8, 128), 1) < LANES
    lower_rows = lax.broadcasted_iota(jnp.int32, (8, 128), 0) < 4
    share = jnp.where(lower_lanes, share[:8], share[8:])

    def everyone(value, src, dst, count, me, send_sems, recv_sems, place):
        src[...] = value
        copies = []
        for o in range(1, count):
            to = lax.rem(me + o, count)
            copies.append(
                pltpu.make_async_remote_copy(
                    src_ref=src,
                    dst_ref=dst.at[me],
                    send_sem=send_sems.at[o],
                    recv_sem=recv_sems.at[o],
                    device_id=place(to),
                    device_id_type=MESH,
                )
            )
        for copy in copies:
            copy.start()
        dst[me] = value
        return copies

    def all_here(copies):
        for copy in copies:
            copy.wait_recv()

    copies_y = everyone(
        share, out_y, in_y, mesh_y, iy, sent_y, got_y, lambda to: (ix, to)
    )
    total = left(table("back"), modes)
    all_here(copies_y)
    half = dims["half_y"]
    y_in = table("y_in").reshape(mesh_y, 2 * half * 8, 128)
    tiles = []
    for b in range(2 * half):
        tile = sum(in_y[p] * y_in[p, 8 * b : 8 * b + 8] for p in range(mesh_y))
        tile = tile + pltpu.roll(tile, LANES, 1)
        tiles.append(tile + pltpu.roll(tile, 4, 0))
    blocks = []
    for b in range(0, half, 2):
        lower = jnp.where(lower_lanes, tiles[b], tiles[b + 1])
        upper = jnp.where(lower_lanes, tiles[half + b], tiles[half + b + 1])
        blocks.append(jnp.where(lower_rows, lower, upper))
    share = jnp.concatenate(blocks, axis=1)
    copies_x = everyone(
        share, out_x, in_x, mesh_x, ix, sent_x, got_x, lambda to: (to, iy)
    )
    own[...] = from_coefs(total, z_back, windows, zl) * keep
    total_copy = pltpu.make_async_copy(own, total_out, local.at[1])
    total_copy.start()
    all_here(copies_x)
    gathered = in_x[...].reshape(mesh_x * 8, lanes)
    scaled = left(table("x_in"), gathered) * table("mu")
    lines = left(table("x_out"), scaled)
    y_out = table("y_out")
    by_row = []
    for q in range(ny // 7 + 1):
        line = lines[:8] * y_out[2 * q : 2 * q + 1] + lines[8:] * y_out[2 * q + 1 : 2 * q + 2]
        by_row.append(sum(line[:, 128 * b : 128 * b + 128] for b in range(lanes // 128)))
    nodes_out[...] = right(jnp.concatenate(by_row, axis=0), table("z_out"))
    total_copy.wait()
    left_here(copies_b)
    left_here(copies_d)
    for copy in copies_y + copies_x:
        copy.wait_send()


def finish(dims, spread, total, nodes, fine_out, coarse_out):
    nx, ny, nz, pitch, zl = dims["nx"], dims["ny"], dims["nz"], dims["pitch"], dims["zl"]
    ix, iy = lax.axis_index("gx"), lax.axis_index("gy")
    row = lax.broadcasted_iota(jnp.int32, (dims["own_rows"], 1), 0)
    keep = (ix * nx + row // pitch > 0) & (iy * ny + row % pitch > 0)
    values = nodes[...]
    for p in range(nx // 7):
        for q in range(ny // 7):
            line = values[8 * q + p : 8 * q + p + 1, zl : zl + nz // 7]
            coarse_out[p, q : q + 1, :] = line
    prolonged = left(spread[...], values[:, :zl])
    result = total[...] + prolonged * keep.astype(jnp.float32)
    for i in range(nx):
        fine_out[i] = result[i * pitch : i * pitch + ny, :nz]


def per_device(mesh_x, mesh_y, residual_in):
    t, dims, spread = tables(mesh_x, mesh_y, residual_in.shape)
    names = list(t)
    nx, ny, nz = residual_in.shape
    own_rows, zl, lanes = dims["own_rows"], dims["zl"], dims["lanes"]
    f32 = jnp.float32
    vmem = pl.BlockSpec(memory_space=pltpu.VMEM)
    total, nodes = pl.pallas_call(
        functools.partial(kernel, names, dims, mesh_x, mesh_y),
        out_shape=(
            jax.ShapeDtypeStruct((own_rows, zl), f32),
            jax.ShapeDtypeStruct((8 * (ny // 7 + 1), zl + 128), f32),
        ),
        in_specs=[pl.BlockSpec(memory_space=pl.ANY)] * (1 + len(names)),
        out_specs=(pl.BlockSpec(memory_space=pl.ANY), vmem),
        scratch_shapes=[
            pltpu.VMEM(t[name].shape[name in PER_DEVICE :], t[name].dtype) for name in names
        ]
        + [
            pltpu.VMEM((nx, ny, nz), f32),
            pltpu.VMEM((own_rows, zl), f32),
            pltpu.VMEM((dims["rows_b"], zl), f32),
            pltpu.VMEM((dims["rows_b"], zl), f32),
            pltpu.VMEM((dims["rows_d"], zl), f32),
            pltpu.VMEM((dims["rows_d"], zl), f32),
            pltpu.VMEM((8, 128), f32),
            pltpu.VMEM((mesh_y, 8, 128), f32),
            pltpu.VMEM((8, lanes), f32),
            pltpu.VMEM((mesh_x, 8, lanes), f32),
            pltpu.SemaphoreType.DMA((2,)),
            pltpu.SemaphoreType.DMA((len(names),)),
            pltpu.SemaphoreType.DMA((2, 8)),
            pltpu.SemaphoreType.DMA((2, 8)),
            pltpu.SemaphoreType.DMA((mesh_y,)),
            pltpu.SemaphoreType.DMA((mesh_y,)),
            pltpu.SemaphoreType.DMA((mesh_x,)),
            pltpu.SemaphoreType.DMA((mesh_x,)),
        ],
        compiler_params=pltpu.CompilerParams(
            collective_id=0, has_side_effects=True, vmem_limit_bytes=56 * 2**20
        ),
        cost_estimate=pl.CostEstimate(flops=10**9, bytes_accessed=10**7, transcendentals=0),
    )(residual_in, *[jnp.asarray(t[name]) for name in names])
    return pl.pallas_call(
        functools.partial(finish, dims),
        out_shape=(
            jax.ShapeDtypeStruct((nx, ny, nz), f32),
            jax.ShapeDtypeStruct((nx // 7, ny // 7, nz // 7), f32),
        ),
        in_specs=[vmem] * 3,
        out_specs=(vmem, vmem),
        compiler_params=pltpu.CompilerParams(vmem_limit_bytes=56 * 2**20),
        cost_estimate=pl.CostEstimate(flops=10**7, bytes_accessed=10**6, transcendentals=0),
    )(jnp.asarray(spread), total, nodes)


def solution(mesh):
    return jax.shard_map(
        functools.partial(per_device, mesh.shape["gx"], mesh.shape["gy"]),
        mesh=mesh,
        in_specs=(P("gx", "gy", None),),
        out_specs=(P("gx", "gy", None), P("gx", "gy", None)),
        check_vma=False,
    )
```

```python
import functools
import math

import jax
import jax.numpy as jnp
import ml_dtypes
import numpy as np
from jax import lax
from jax.experimental import pallas as pl
from jax.experimental.pallas import tpu as pltpu
from jax.sharding import PartitionSpec as P

theta_cheb = 1.125
delta_cheb = 0.875
start_points = [
    -0.8717401485096066,
    -0.5917001814331423,
    -0.2092992179024789,
    0.2092992179024789,
    0.5917001814331423,
    0.8717401485096066,
]


def legendre_pair(value):
    before, now = (1.0, value)
    for order in range(1, 7):
        before, now = (now, ((2 * order + 1) * value * now - order * before) / (order + 1))
    return (now, before)


def lobatto_tables():
    point_list = [-1.0]
    for guess in start_points:
        place = guess
        for newton in range(4):
            seventh, sixth = legendre_pair(place)
            slope = 7.0 * (place * seventh - sixth) / (place * place - 1.0)
            curve = (2.0 * place * slope - 56.0 * seventh) / (1.0 - place * place)
            place = place - slope / curve
        point_list.append(place)
    point_list.append(1.0)
    sample_nodes_list = np.array(point_list)
    values = np.array([legendre_pair(place)[0] for place in point_list])
    weights = 2.0 / (56.0 * values * values)
    derivative = np.zeros((8, 8))
    for i in range(8):
        for j in range(8):
            if i != j:
                derivative[i, j] = values[i] / (
                    values[j] * (sample_nodes_list[i] - sample_nodes_list[j])
                )
    derivative[0, 0] = -14.0
    derivative[7, 7] = 14.0
    stiffness = derivative.T @ (weights[:, None] * derivative)
    return (sample_nodes_list, weights, stiffness)


def assemble(elements, stiffness, weights):
    width = 7 * elements + 1
    assembled = np.zeros((width, width))
    masses = np.zeros(width)
    for e in range(elements):
        assembled[7 * e : 7 * e + 8, 7 * e : 7 * e + 8] += stiffness
        masses[7 * e : 7 * e + 8] += weights
    return (assembled, masses)


def jacobi_eigen(matrix):
    order = matrix.shape[0]
    work = [[float(matrix[i, j]) for j in range(order)] for i in range(order)]
    vectors = [[1.0 if i == j else 0.0 for j in range(order)] for i in range(order)]
    for sweep in range(12):
        for p in range(order):
            for q in range(p + 1, order):
                angle = 0.5 * math.atan2(2.0 * work[p][q], work[q][q] - work[p][p])
                cosine = math.cos(angle)
                sine = math.sin(angle)
                for k in range(order):
                    left, right = (work[k][p], work[k][q])
                    work[k][p] = cosine * left - sine * right
                    work[k][q] = sine * left + cosine * right
                for k in range(order):
                    left, right = (work[p][k], work[q][k])
                    work[p][k] = cosine * left - sine * right
                    work[q][k] = sine * left + cosine * right
                for k in range(order):
                    left, right = (vectors[k][p], vectors[k][q])
                    vectors[k][p] = cosine * left - sine * right
                    vectors[k][q] = sine * left + cosine * right
    return (np.array([work[i][i] for i in range(order)]), np.array(vectors))


def schwarz_basis():
    sample_nodes_list, weights, stiffness = lobatto_tables()
    assembled, masses = assemble(3, stiffness, weights)
    block_stiff = assembled[6:16, 6:16]
    inv_root = 1.0 / np.sqrt(masses[6:16])
    eigen_vals, eigen_vecs = jacobi_eigen(inv_root[:, None] * block_stiff * inv_root[None, :])
    return (inv_root[:, None] * eigen_vecs, eigen_vals)


def injection_coefficients(elements, sample_nodes_list):
    matrix = np.zeros((elements + 1, 7 * elements))
    for e in range(elements):
        for m in range(7):
            matrix[e, 7 * e + m] += (1.0 - sample_nodes_list[m]) / 2.0
            matrix[e + 1, 7 * e + m] += (1.0 + sample_nodes_list[m]) / 2.0
    return matrix


MESH = pl.DeviceIdType.MESH
LANES = 64
DIRECTIONS = [(-1, 0), (1, 0), (0, -1), (0, 1), (-1, -1), (-1, 1), (1, -1), (1, 1)]


def round_up(value, unit):
    return -(-value // unit) * unit


def sine_np(vertices, elements):
    modes = np.arange(elements)
    vertex = np.asarray(vertices)[:, None]
    entries = np.sqrt(2.0 / elements) * np.sin(np.pi * (vertex * modes % (2 * elements)) / elements)
    entries = entries / np.sqrt((4.0 + 2.0 * np.cos(np.pi * modes / elements)) / 3.0)
    inside = (modes > 0) & (vertex > 0) & (vertex < elements)
    return np.where(inside, entries, 0.0)


def eigen_np(elements):
    modes = np.arange(elements)
    cosine = np.cos(np.pi * modes / elements)
    return np.where(modes > 0, 3.0 * (1.0 - cosine) / (4.0 + 2.0 * cosine), 1.0)


def split_np(matrix, axis):
    high = matrix.astype(np.float32).astype(ml_dtypes.bfloat16)
    low = (matrix - high.astype(np.float64)).astype(np.float32).astype(ml_dtypes.bfloat16)
    return np.concatenate([high, high, low], axis=axis)


def lhs_np(matrix):
    return split_np(pad_np(matrix, round_up(matrix.shape[0], 16), matrix.shape[1]), 1)


def rhs_np(matrix):
    return split_np(matrix, 0)


def pad_np(matrix, rows, columns, value=0.0):
    out = np.full((rows, columns), value)
    out[: matrix.shape[0], : matrix.shape[1]] = matrix
    return out


class Line:
    def __init__(self, elements, stiffness, weights, eigen_basis, points):
        self.elements = elements
        self.nodes = 7 * elements
        around, masses = assemble(elements + 4, stiffness, weights)
        self.around, self.masses, self.shift = around, masses, 14
        self.forward = np.zeros((10 * elements, self.nodes + 3))
        self.backward = np.zeros((self.nodes, 10 * elements))
        for e in range(elements):
            self.forward[10 * e : 10 * e + 10, 7 * e : 7 * e + 10] = eigen_basis.T
            self.backward[7 * e : 7 * e + 7, 10 * e : 10 * e + 10] = eigen_basis[1:8]
        hats = injection_coefficients(elements + 4, points)
        kept = slice(self.shift, self.shift + self.nodes)
        rows = slice(1, 1 + elements + 2)
        full = np.zeros((hats.shape[0], self.around.shape[0]))
        full[:, : hats.shape[1]] = hats
        self.hats = hats[rows, kept]
        self.hats_stiff = (full @ around)[rows, kept]
        self.hats_mass = (full * masses)[rows, kept]

    def stiff(self, i, j):
        return self.around[i + self.shift, j + self.shift]

    def mass(self, i):
        return self.masses[i + self.shift]

    def values(self, side):
        n = self.nodes
        return {-1: [-1], 0: list(range(n)), 1: [n, n + 1]}[side]

    def sums(self, side):
        n = self.nodes
        return {-1: [-1, 0], 0: [], 1: [n, n + 1]}[side]


def segments(lines, with_sums):
    line_x, line_y = lines
    out, start = [], 0
    for dx, dy in DIRECTIONS:
        rows = [("v", i, j) for i in line_x.values(dx) for j in line_y.values(dy)]
        if with_sums:
            rows += [("x", i, j) for i in line_x.sums(dx) for j in line_y.values(dy)]
            rows += [("y", i, j) for i in line_x.values(dx) for j in line_y.sums(dy)]
        size = round_up(len(rows), 8)
        out.append((start, size, rows))
        start += size
    return out, start


def tables(mesh_x, mesh_y, shape):
    points, weights, stiffness = lobatto_tables()
    eigen_basis, eigen_vals = schwarz_basis()
    nx, ny, nz = shape
    ex, ey, ez = nx // 7, ny // 7, nz // 7
    line_x = Line(ex, stiffness, weights, eigen_basis, points)
    line_y = Line(ey, stiffness, weights, eigen_basis, points)
    lines = (line_x, line_y)
    pitch = round_up(ny, 8)
    own_rows = round_up(nx * pitch, 16)
    zl = round_up(nz, 128)
    half_z = ez // 2
    assert ez % 2 == 0 and 10 * half_z <= 256 and zl >= 256
    cl = 512
    windows = [0, zl - 256]
    coefs = 100 * ex * ey
    own = lambda i, j: i * pitch + j
    own_list = [(i, j) for i in range(nx) for j in range(ny)]
    t = {}
    dims = dict(nx=nx, ny=ny, nz=nz, pitch=pitch, own_rows=own_rows, zl=zl, windows=windows)

    forward = lambda i, j: np.kron(line_x.forward[:, i + 1], line_y.forward[:, j + 1])
    seg_b, rows_b = segments(lines, False)
    seg_d, rows_d = segments(lines, True)
    rows_d = round_up(rows_d, 16)
    dims.update(seg_b=[s[:2] for s in seg_b], rows_b=rows_b)
    dims.update(seg_d=[s[:2] for s in seg_d], rows_d=rows_d)

    pick = np.zeros((rows_b, own_rows))
    w_halo = np.zeros((coefs, rows_b))
    for (dx, dy), (start, size, rows) in zip(DIRECTIONS, seg_b):
        for r, (kind, i, j) in enumerate(rows):
            pick[start + r, own(i - nx * dx, j - ny * dy)] = 1.0
            w_halo[:, start + r] = forward(i, j)
    w_own = np.zeros((coefs, own_rows))
    back = np.zeros((own_rows, coefs))
    for i, j in own_list:
        w_own[:, own(i, j)] = forward(i, j)
        back[own(i, j)] = np.kron(line_x.backward[i], line_y.backward[j])
    z_fwd = np.zeros((zl, cl))
    z_back = np.zeros((cl, zl))
    l_z = np.ones(cl)
    for e in range(ez):
        lane = 256 * (e // half_z) + 10 * (e % half_z)
        l_z[lane : lane + 10] = eigen_vals
        for m in range(10):
            z = 7 * e - 1 + m
            if 0 < z < nz:
                z_fwd[z, lane : lane + 10] = eigen_basis[m]
                if 1 <= m <= 7:
                    z_back[lane : lane + 10, z] = eigen_basis[m]
    l_x, l_y = np.tile(eigen_vals, ex), np.tile(eigen_vals, ey)
    inverse = 1.0 / ((l_x[:, None] + l_y[None, :]).reshape(coefs, 1) + l_z)

    def window(matrix, c):
        kept = matrix[windows[c] : windows[c] + 256, 256 * c : 256 * c + 256]
        assert np.count_nonzero(kept) == np.count_nonzero(matrix[:, 256 * c : 256 * c + 256])
        return kept

    t["pick"] = pick.astype(ml_dtypes.bfloat16)
    t["z_fwd"] = np.stack([rhs_np(window(z_fwd, c)) for c in range(2)])
    t["w_own"] = lhs_np(w_own)
    t["coarse_b"] = None
    t["to_modes"] = None
    t["w_halo"] = lhs_np(w_halo)
    t["inverse"] = inverse.astype(np.float32)
    t["send_m"] = None
    t["z_back"] = np.stack([rhs_np(window(z_back.T, c).T) for c in range(2)])
    t["back"] = lhs_np(back)

    send = np.zeros((rows_d, own_rows))
    wide_y = ny + 3
    points_rows = round_up((nx + 3) * wide_y, 16)
    target = lambda i, j: (i + 1) * wide_y + (j + 1)
    inside_x = lambda i: -1 <= i <= nx + 1
    inside_y = lambda j: -1 <= j <= ny + 1
    lap_own = np.zeros((2 * points_rows, own_rows))
    lap_halo = np.zeros((2 * points_rows, rows_d))

    def value_column(column, i, j, dx, dy):
        for k in range(-1, nx + 2):
            if k not in line_x.sums(dx):
                column[target(k, j)] += line_x.stiff(k, i) * line_y.mass(j)
        for k in range(-1, ny + 2):
            if k not in line_y.sums(dy):
                column[target(i, k)] += line_y.stiff(k, j) * line_x.mass(i)
        column[points_rows + target(i, j)] += line_x.mass(i) * line_y.mass(j)

    for i, j in own_list:
        value_column(lap_own[:, own(i, j)], i, j, 0, 0)
    for (dx, dy), (start, size, rows) in zip(DIRECTIONS, seg_d):
        for r, (kind, i, j) in enumerate(rows):
            p, q = i - nx * dx, j - ny * dy
            if kind == "v":
                send[start + r, own(p, q)] = 1.0
                value_column(lap_halo[:, start + r], i, j, dx, dy)
            elif kind == "x":
                for k in range(nx):
                    send[start + r, own(k, q)] = line_x.stiff(p, k)
                lap_halo[target(i, j), start + r] += line_y.mass(j)
            else:
                for k in range(ny):
                    send[start + r, own(p, k)] = line_y.stiff(q, k)
                lap_halo[target(i, j), start + r] += line_x.mass(i)
    w_all = np.zeros((coefs, points_rows))
    for i in range(-1, nx + 2):
        for j in range(-1, ny + 2):
            w_all[:, target(i, j)] = forward(i, j)
    masked_backs = []
    for first_x in (0, 1):
        for first_y in (0, 1):
            masked = back.copy()
            for i, j in own_list:
                if (first_x and i == 0) or (first_y and j == 0):
                    masked[own(i, j)] = 0.0
            masked_backs.append(masked)
    t["send_m"] = np.stack([lhs_np(send @ masked / theta_cheb) for masked in masked_backs])
    stiff_z, mass_z = assemble(ez, stiffness, weights)
    stiff_z = pad_np(stiff_z[:nz, :nz], zl, zl)
    mass_z = np.diag(pad_np(mass_z[None, :nz], 1, zl)[0])
    both_z = [mass_z @ z_fwd, stiff_z @ z_fwd]
    t["z_lap"] = np.stack(
        [rhs_np(np.concatenate([window(matrix, c) for matrix in both_z], 1)) for c in range(2)]
    )
    t["lap_own"], t["lap_halo"] = [], []
    for place_x in range(3):
        for place_y in range(3):
            inner = np.zeros(points_rows)
            for i in range(-1, nx + 2):
                for j in range(-1, ny + 2):
                    out_x = (place_x == 0 and i <= 0) or (place_x == 2 and i >= nx)
                    out_y = (place_y == 0 and j <= 0) or (place_y == 2 and j >= ny)
                    inner[target(i, j)] = 0.0 if out_x or out_y else 1.0
            masked = w_all * inner
            for name, lap in (("lap_own", lap_own), ("lap_halo", lap_halo)):
                pair = [masked @ lap[:points_rows], masked @ lap[points_rows:]]
                pair = np.concatenate(pair, 1)
                t[name].append(lhs_np(pair)[:, pair.shape[1] :])
    t["lap_own"], t["lap_halo"] = np.stack(t["lap_own"]), np.stack(t["lap_halo"])

    count_x, count_y = mesh_x * ex, mesh_y * ey
    vx, vy = ex + 2, ey + 2
    assert vx == 4 and vy == 4 and count_y % 4 == 0
    half_y = count_y // 2
    dims.update(count_x=count_x, half_y=half_y, lanes=half_y * LANES)
    coarse = np.zeros((3, 16, own_rows))
    for i, j in own_list:
        for w in range(vy):
            for v in range(vx):
                row = 4 * w + v
                coarse[0, row, own(i, j)] = line_x.hats[v, i] * line_y.hats[w, j]
                coarse[1, row, own(i, j)] = (
                    line_x.hats_stiff[v, i] * line_y.hats_mass[w, j]
                    + line_x.hats_mass[v, i] * line_y.hats_stiff[w, j]
                )
                coarse[2, row, own(i, j)] = line_x.hats_mass[v, i] * line_y.hats_mass[w, j]
    t["coarse_b"] = lhs_np(coarse[0])
    coarse_m = [
        lhs_np(np.concatenate([coarse[1] @ masked, coarse[2] @ masked])) for masked in masked_backs
    ]
    t["coarse_m"] = np.stack(coarse_m)
    hats_z = injection_coefficients(ez, points)[:ez]
    phi_z = sine_np(np.arange(ez), ez)
    to_modes = pad_np(hats_z.T @ phi_z, zl, LANES)
    to_modes[0] = 0.0
    t["to_modes"] = rhs_np(np.tile(to_modes, (1, 2)))
    m_modes = np.concatenate([z_back @ mass_z @ to_modes, z_back @ stiff_z @ to_modes])
    t["m_modes"] = rhs_np(np.tile(m_modes, (1, 2)))
    y_in = np.zeros((mesh_y, count_y, 2, 4, 2, LANES))
    y_out = np.zeros((mesh_y, 8, half_y * LANES))
    for p in range(mesh_y):
        inward = sine_np(p * ey - 1 + np.arange(vy), count_y)
        outward = sine_np(p * ey + np.arange(ey + 1), count_y)
        for w in range(vy):
            y_in[p, :, w % 2, :, w // 2, :] = inward[w][:, None, None]
        for q in range(ey + 1):
            for h in range(2):
                y_out[p, 2 * q + h] = np.repeat(outward[q, h * half_y : (h + 1) * half_y], LANES)
    t["y_in"] = y_in.reshape(mesh_y * count_y * 8, 2 * LANES).astype(np.float32)
    x_in = np.zeros((2, count_x, mesh_x, 2, 4))
    x_out = np.zeros((mesh_x, 2, 8, 2, count_x))
    for p in range(mesh_x):
        for h in range(2):
            x_in[h, :, p, h] = sine_np(p * ex - 1 + np.arange(vx), count_x).T
            x_out[p, h, : ex + 1, h] = sine_np(p * ex + np.arange(ex + 1), count_x)
    t["x_in"] = lhs_np(x_in.reshape(2 * count_x, mesh_x * 8))
    mu = np.ones((count_x, count_y, LANES))
    mu[:, :, :ez] = (
        eigen_np(count_x)[:, None, None] + eigen_np(count_y)[None, :, None] + eigen_np(ez)
    )
    mu = mu.reshape(count_x, 2, half_y * LANES).transpose(1, 0, 2)
    t["mu"] = (1.0 / mu).reshape(2 * count_x, half_y * LANES).astype(np.float32)
    t["x_out"] = np.stack([lhs_np(x_out[p].reshape(16, 2 * count_x)) for p in range(mesh_x)])
    t["y_out"] = y_out.astype(np.float32)
    z_out = np.zeros((LANES, zl + 128))
    z_out[:ez, :nz] = phi_z.T @ hats_z
    z_out[:, 0] = 0.0
    z_out[:ez, zl : zl + ez] = phi_z.T
    t["z_out"] = rhs_np(np.tile(z_out, (2, 1)))
    spread = np.zeros((own_rows, 8 * (ey + 1)))
    hats_x, hats_y = line_x.hats[1:], line_y.hats[1:]
    for i, j in own_list:
        for q in range(ey + 1):
            for p in range(ex + 1):
                spread[own(i, j), 8 * q + p] = hats_x[p, i] * hats_y[q, j]
    return t, dims, lhs_np(spread)


def halves(value):
    high = value.astype(jnp.bfloat16)
    return high, (value - high.astype(jnp.float32)).astype(jnp.bfloat16)


def mm(a, b):
    return jnp.dot(a, b, preferred_element_type=jnp.float32)


def left(table, value):
    high, low = halves(value)
    return mm(table, jnp.concatenate([high, low, high], axis=0))


def left_two(table, value):
    high, low = halves(value)
    both = mm(table, jnp.concatenate([high, high], axis=0))
    return both + mm(table[:, : value.shape[0]], low)


def right(value, table):
    high, low = halves(value)
    return mm(jnp.concatenate([high, low, high], axis=1), table)


def to_coefs(value, table, windows):
    high, low = halves(value)
    out = []
    for c, start in enumerate(windows):
        near = slice(start, start + 256)
        out.append(mm(jnp.concatenate([high[:, near], low[:, near], high[:, near]], 1), table[c]))
    count = out[0].shape[1] // 256
    rows = [
        jnp.concatenate([part[:, 256 * n : 256 * n + 256] for part in out], 1) for n in range(count)
    ]
    return rows[0] if count == 1 else jnp.concatenate(rows, 0)


def from_coefs(value, table, windows, zl):
    total = None
    for c, start in enumerate(windows):
        part = right(value[:, 256 * c : 256 * c + 256], table[c])
        sides = [jnp.zeros((part.shape[0], n), part.dtype) for n in (start, zl - start - 256) if n]
        part = jnp.concatenate([part] + sides if start == 0 else sides + [part], axis=1)
        total = part if total is None else total + part
    return total


PER_DEVICE = ("send_m", "lap_own", "lap_halo", "coarse_m", "x_out", "y_out")


def kernel(names, dims, mesh_x, mesh_y, residual, *refs):
    count = len(names)
    far = dict(zip(names, refs[:count]))
    near = dict(zip(names, refs[count + 2 : 2 * count + 2]))
    total_out, nodes_out = refs[count : count + 2]
    (block, own, out_b, in_b, out_d, in_d, out_y, in_y, out_x, in_x,
     local, loaded, sent, got, sent_y, got_y, sent_x, got_x) = refs[2 * count + 2 :]
    nx, ny, nz, pitch = dims["nx"], dims["ny"], dims["nz"], dims["pitch"]
    own_rows, zl, windows = dims["own_rows"], dims["zl"], dims["windows"]
    ix, iy = lax.axis_index("gx"), lax.axis_index("gy")
    def exists(dx, dy):
        return (ix + dx >= 0) & (ix + dx < mesh_x) & (iy + dy >= 0) & (iy + dy < mesh_y)

    residual_in = pltpu.make_async_copy(residual, block, local.at[0])
    residual_in.start()
    in_b[...] = jnp.zeros_like(in_b)
    in_d[...] = jnp.zeros_like(in_d)
    barrier = pltpu.get_barrier_semaphore()
    for o in range(1, mesh_x):
        pl.semaphore_signal(
            barrier, inc=1, device_id=(lax.rem(ix + o, mesh_x), iy), device_id_type=MESH
        )
    for o in range(1, mesh_y):
        pl.semaphore_signal(
            barrier, inc=1, device_id=(ix, lax.rem(iy + o, mesh_y)), device_id_type=MESH
        )
    corners = DIRECTIONS[4:]
    for dx, dy in corners:
        @pl.when(exists(dx, dy))
        def _():
            pl.semaphore_signal(barrier, inc=1, device_id=(ix + dx, iy + dy), device_id_type=MESH)

    start_of_grid = 2 * (ix == 0).astype(jnp.int32) + (iy == 0).astype(jnp.int32)
    own[...] = jnp.zeros_like(own)
    place_x = 1 - (ix == 0).astype(jnp.int32) + (ix == mesh_x - 1).astype(jnp.int32)
    place_y = 1 - (iy == 0).astype(jnp.int32) + (iy == mesh_y - 1).astype(jnp.int32)
    in_grid = 3 * place_x + place_y
    place = dict(send_m=start_of_grid, lap_own=in_grid, lap_halo=in_grid)
    place.update(coarse_m=start_of_grid, x_out=ix, y_out=iy)
    loads = {}
    for n, name in enumerate(names):
        src = far[name].at[place[name]] if name in place else far[name]
        loads[name] = pltpu.make_async_copy(src, near[name], loaded.at[n])

    later = names.index("back")
    for name in names[:later]:
        loads[name].start()

    def table(name):
        if name in loads:
            loads.pop(name).wait()
        return near[name][...]

    row = lax.broadcasted_iota(jnp.int32, (own_rows, 1), 0)
    node_x, node_y = ix * nx + row // pitch, iy * ny + row % pitch
    keep = ((node_x > 0) & (node_y > 0) & (row % pitch < ny) & (row // pitch < nx)).astype(
        jnp.float32
    )
    residual_in.wait()
    for i in range(nx):
        own[i * pitch : i * pitch + ny, 0:nz] = block[i]
    source = own[...] * keep
    high, low = halves(source)
    pick = table("pick")
    out_b[...] = mm(pick, high) + mm(pick, low)

    greetings = mesh_x - 1 + mesh_y - 1
    for dx, dy in corners:
        greetings = greetings + exists(dx, dy).astype(jnp.int32)
    pl.semaphore_wait(barrier, greetings)

    def halo(phase, src, dst, places):
        copies = []
        for d, (dx, dy) in enumerate(DIRECTIONS):
            start, size = places[d]
            copies.append(
                pltpu.make_async_remote_copy(
                    src_ref=src.at[pl.ds(start, size)],
                    dst_ref=dst.at[pl.ds(start, size)],
                    send_sem=sent.at[phase, d],
                    recv_sem=got.at[phase, d],
                    device_id=(ix - dx, iy - dy),
                    device_id_type=MESH,
                )
            )
        for d in (2, 3, 4, 5, 6, 7, 0, 1):
            dx, dy = DIRECTIONS[d]
            pl.when(exists(-dx, -dy))(copies[d].start)
        return copies

    def arrived(copies):
        for d, (dx, dy) in enumerate(DIRECTIONS):
            pl.when(exists(dx, dy))(copies[d].wait_recv)

    def left_here(copies):
        for d, (dx, dy) in enumerate(DIRECTIONS):
            pl.when(exists(-dx, -dy))(copies[d].wait_send)

    copies_b = halo(0, out_b, in_b, dims["seg_b"])
    for name in names[later:]:
        loads[name].start()
    z_fwd = table("z_fwd")
    coefs = left(table("w_own"), to_coefs(source, z_fwd, windows))
    coarse_b = right(left(table("coarse_b"), source), table("to_modes"))
    arrived(copies_b)
    coefs = coefs + left(table("w_halo"), to_coefs(in_b[...], z_fwd, windows))
    modes_0 = coefs * table("inverse")
    z_back = table("z_back")
    out_d[...] = from_coefs(left(table("send_m"), modes_0), z_back, windows, zl)
    copies_d = halo(1, out_d, in_d, dims["seg_d"])
    first = from_coefs(left(table("back"), modes_0), z_back, windows, zl)
    first = first * (keep * (1.0 / theta_cheb))
    z_lap = table("z_lap")
    coefs = coefs - left_two(table("lap_own"), to_coefs(first, z_lap, windows))
    arrived(copies_d)
    coefs = coefs - left_two(table("lap_halo"), to_coefs(in_d[...], z_lap, windows))
    sigma = theta_cheb / delta_cheb
    rho_0 = 1.0 / sigma
    rho_1 = 1.0 / (2.0 * sigma - rho_0)
    weight_0, weight_1 = (1.0 + rho_1 * rho_0) / theta_cheb, 2.0 * rho_1 / delta_cheb
    modes = weight_0 * modes_0 + weight_1 * (coefs * table("inverse"))

    lanes = dims["lanes"]
    shares = left(table("coarse_m"), modes)
    shares = jnp.concatenate([shares[:16], shares[16:]], axis=1)
    share = coarse_b - right(shares, table("m_modes"))
    lower_lanes = lax.broadcasted_iota(jnp.int32, (8, 128), 1) < LANES
    lower_rows = lax.broadcasted_iota(jnp.int32, (8, 128), 0) < 4
    share = jnp.where(lower_lanes, share[:8], share[8:])

    def everyone(value, src, dst, count, me, send_sems, recv_sems, place):
        src[...] = value
        copies = []
        for o in range(1, count):
            to = lax.rem(me + o, count)
            copies.append(
                pltpu.make_async_remote_copy(
                    src_ref=src,
                    dst_ref=dst.at[me],
                    send_sem=send_sems.at[o],
                    recv_sem=recv_sems.at[o],
                    device_id=place(to),
                    device_id_type=MESH,
                )
            )
        for copy in copies:
            copy.start()
        dst[me] = value
        return copies

    def all_here(copies):
        for copy in copies:
            copy.wait_recv()

    copies_y = everyone(
        share, out_y, in_y, mesh_y, iy, sent_y, got_y, lambda to: (ix, to)
    )
    total = left(table("back"), modes)
    all_here(copies_y)
    half = dims["half_y"]
    y_in = table("y_in").reshape(mesh_y, 2 * half * 8, 128)
    tiles = []
    for b in range(2 * half):
        tile = sum(in_y[p] * y_in[p, 8 * b : 8 * b + 8] for p in range(mesh_y))
        tile = tile + pltpu.roll(tile, LANES, 1)
        tiles.append(tile + pltpu.roll(tile, 4, 0))
    blocks = []
    for b in range(0, half, 2):
        lower = jnp.where(lower_lanes, tiles[b], tiles[b + 1])
        upper = jnp.where(lower_lanes, tiles[half + b], tiles[half + b + 1])
        blocks.append(jnp.where(lower_rows, lower, upper))
    share = jnp.concatenate(blocks, axis=1)
    copies_x = everyone(
        share, out_x, in_x, mesh_x, ix, sent_x, got_x, lambda to: (to, iy)
    )
    own[...] = from_coefs(total, z_back, windows, zl) * keep
    total_copy = pltpu.make_async_copy(own, total_out, local.at[1])
    total_copy.start()
    all_here(copies_x)
    gathered = in_x[...].reshape(mesh_x * 8, lanes)
    scaled = left(table("x_in"), gathered) * table("mu")
    lines = left(table("x_out"), scaled)
    y_out = table("y_out")
    by_row = []
    for q in range(ny // 7 + 1):
        line = lines[:8] * y_out[2 * q : 2 * q + 1] + lines[8:] * y_out[2 * q + 1 : 2 * q + 2]
        by_row.append(sum(line[:, 128 * b : 128 * b + 128] for b in range(lanes // 128)))
    nodes_out[...] = right(jnp.concatenate(by_row, axis=0), table("z_out"))
    total_copy.wait()
    left_here(copies_b)
    left_here(copies_d)
    for copy in copies_y + copies_x:
        copy.wait_send()


def finish(dims, spread, total, nodes, fine_out, coarse_out):
    nx, ny, nz, pitch, zl = dims["nx"], dims["ny"], dims["nz"], dims["pitch"], dims["zl"]
    ix, iy = lax.axis_index("gx"), lax.axis_index("gy")
    row = lax.broadcasted_iota(jnp.int32, (dims["own_rows"], 1), 0)
    keep = (ix * nx + row // pitch > 0) & (iy * ny + row % pitch > 0)
    values = nodes[...]
    for p in range(nx // 7):
        for q in range(ny // 7):
            line = values[8 * q + p : 8 * q + p + 1, zl : zl + nz // 7]
            coarse_out[p, q : q + 1, :] = line
    prolonged = left(spread[...], values[:, :zl])
    result = total[...] + prolonged * keep.astype(jnp.float32)
    for i in range(nx):
        fine_out[i] = result[i * pitch : i * pitch + ny, :nz]


def per_device(mesh_x, mesh_y, residual_in):
    t, dims, spread = tables(mesh_x, mesh_y, residual_in.shape)
    names = list(t)
    nx, ny, nz = residual_in.shape
    own_rows, zl, lanes = dims["own_rows"], dims["zl"], dims["lanes"]
    f32 = jnp.float32
    vmem = pl.BlockSpec(memory_space=pltpu.VMEM)
    total, nodes = pl.pallas_call(
        functools.partial(kernel, names, dims, mesh_x, mesh_y),
        out_shape=(
            jax.ShapeDtypeStruct((own_rows, zl), f32),
            jax.ShapeDtypeStruct((8 * (ny // 7 + 1), zl + 128), f32),
        ),
        in_specs=[pl.BlockSpec(memory_space=pl.ANY)] * (1 + len(names)),
        out_specs=(pl.BlockSpec(memory_space=pl.ANY), vmem),
        scratch_shapes=[
            pltpu.VMEM(t[name].shape[name in PER_DEVICE :], t[name].dtype) for name in names
        ]
        + [
            pltpu.VMEM((nx, ny, nz), f32),
            pltpu.VMEM((own_rows, zl), f32),
            pltpu.VMEM((dims["rows_b"], zl), f32),
            pltpu.VMEM((dims["rows_b"], zl), f32),
            pltpu.VMEM((dims["rows_d"], zl), f32),
            pltpu.VMEM((dims["rows_d"], zl), f32),
            pltpu.VMEM((8, 128), f32),
            pltpu.VMEM((mesh_y, 8, 128), f32),
            pltpu.VMEM((8, lanes), f32),
            pltpu.VMEM((mesh_x, 8, lanes), f32),
            pltpu.SemaphoreType.DMA((2,)),
            pltpu.SemaphoreType.DMA((len(names),)),
            pltpu.SemaphoreType.DMA((2, 8)),
            pltpu.SemaphoreType.DMA((2, 8)),
            pltpu.SemaphoreType.DMA((mesh_y,)),
            pltpu.SemaphoreType.DMA((mesh_y,)),
            pltpu.SemaphoreType.DMA((mesh_x,)),
            pltpu.SemaphoreType.DMA((mesh_x,)),
        ],
        compiler_params=pltpu.CompilerParams(
            collective_id=0, has_side_effects=True, vmem_limit_bytes=56 * 2**20
        ),
        cost_estimate=pl.CostEstimate(flops=10**9, bytes_accessed=10**7, transcendentals=0),
    )(residual_in, *[jnp.asarray(t[name]) for name in names])
    return pl.pallas_call(
        functools.partial(finish, dims),
        out_shape=(
            jax.ShapeDtypeStruct((nx, ny, nz), f32),
            jax.ShapeDtypeStruct((nx // 7, ny // 7, nz // 7), f32),
        ),
        in_specs=[vmem] * 3,
        out_specs=(vmem, vmem),
        compiler_params=pltpu.CompilerParams(vmem_limit_bytes=56 * 2**20),
        cost_estimate=pl.CostEstimate(flops=10**7, bytes_accessed=10**6, transcendentals=0),
    )(jnp.asarray(spread), total, nodes)


def solution(mesh):
    return jax.shard_map(
        functools.partial(per_device, mesh.shape["gx"], mesh.shape["gy"]),
        mesh=mesh,
        in_specs=(P("gx", "gy", None),),
        out_specs=(P("gx", "gy", None), P("gx", "gy", None)),
        check_vma=False,
    )
```

```python
import functools
import math

import jax
import jax.numpy as jnp
import ml_dtypes
import numpy as np
from jax import lax
from jax.experimental import pallas as pl
from jax.experimental.pallas import tpu as pltpu
from jax.sharding import PartitionSpec as P

theta_cheb = 1.125
delta_cheb = 0.875
start_points = [
    -0.8717401485096066,
    -0.5917001814331423,
    -0.2092992179024789,
    0.2092992179024789,
    0.5917001814331423,
    0.8717401485096066,
]


def legendre_pair(value):
    before, now = (1.0, value)
    for order in range(1, 7):
        before, now = (now, ((2 * order + 1) * value * now - order * before) / (order + 1))
    return (now, before)


def lobatto_tables():
    point_list = [-1.0]
    for guess in start_points:
        place = guess
        for newton in range(4):
            seventh, sixth = legendre_pair(place)
            slope = 7.0 * (place * seventh - sixth) / (place * place - 1.0)
            curve = (2.0 * place * slope - 56.0 * seventh) / (1.0 - place * place)
            place = place - slope / curve
        point_list.append(place)
    point_list.append(1.0)
    sample_nodes_list = np.array(point_list)
    values = np.array([legendre_pair(place)[0] for place in point_list])
    weights = 2.0 / (56.0 * values * values)
    derivative = np.zeros((8, 8))
    for i in range(8):
        for j in range(8):
            if i != j:
                derivative[i, j] = values[i] / (
                    values[j] * (sample_nodes_list[i] - sample_nodes_list[j])
                )
    derivative[0, 0] = -14.0
    derivative[7, 7] = 14.0
    stiffness = derivative.T @ (weights[:, None] * derivative)
    return (sample_nodes_list, weights, stiffness)


def assemble(elements, stiffness, weights):
    width = 7 * elements + 1
    assembled = np.zeros((width, width))
    masses = np.zeros(width)
    for e in range(elements):
        assembled[7 * e : 7 * e + 8, 7 * e : 7 * e + 8] += stiffness
        masses[7 * e : 7 * e + 8] += weights
    return (assembled, masses)


def jacobi_eigen(matrix):
    order = matrix.shape[0]
    work = [[float(matrix[i, j]) for j in range(order)] for i in range(order)]
    vectors = [[1.0 if i == j else 0.0 for j in range(order)] for i in range(order)]
    for sweep in range(12):
        for p in range(order):
            for q in range(p + 1, order):
                angle = 0.5 * math.atan2(2.0 * work[p][q], work[q][q] - work[p][p])
                cosine = math.cos(angle)
                sine = math.sin(angle)
                for k in range(order):
                    left, right = (work[k][p], work[k][q])
                    work[k][p] = cosine * left - sine * right
                    work[k][q] = sine * left + cosine * right
                for k in range(order):
                    left, right = (work[p][k], work[q][k])
                    work[p][k] = cosine * left - sine * right
                    work[q][k] = sine * left + cosine * right
                for k in range(order):
                    left, right = (vectors[k][p], vectors[k][q])
                    vectors[k][p] = cosine * left - sine * right
                    vectors[k][q] = sine * left + cosine * right
    return (np.array([work[i][i] for i in range(order)]), np.array(vectors))


def schwarz_basis():
    sample_nodes_list, weights, stiffness = lobatto_tables()
    assembled, masses = assemble(3, stiffness, weights)
    block_stiff = assembled[6:16, 6:16]
    inv_root = 1.0 / np.sqrt(masses[6:16])
    eigen_vals, eigen_vecs = jacobi_eigen(inv_root[:, None] * block_stiff * inv_root[None, :])
    return (inv_root[:, None] * eigen_vecs, eigen_vals)


def injection_coefficients(elements, sample_nodes_list):
    matrix = np.zeros((elements + 1, 7 * elements))
    for e in range(elements):
        for m in range(7):
            matrix[e, 7 * e + m] += (1.0 - sample_nodes_list[m]) / 2.0
            matrix[e + 1, 7 * e + m] += (1.0 + sample_nodes_list[m]) / 2.0
    return matrix


MESH = pl.DeviceIdType.MESH
LANES = 64
DIRECTIONS = [(-1, 0), (1, 0), (0, -1), (0, 1), (-1, -1), (-1, 1), (1, -1), (1, 1)]


def round_up(value, unit):
    return -(-value // unit) * unit


def sine_np(vertices, elements):
    modes = np.arange(elements)
    vertex = np.asarray(vertices)[:, None]
    entries = np.sqrt(2.0 / elements) * np.sin(np.pi * (vertex * modes % (2 * elements)) / elements)
    entries = entries / np.sqrt((4.0 + 2.0 * np.cos(np.pi * modes / elements)) / 3.0)
    inside = (modes > 0) & (vertex > 0) & (vertex < elements)
    return np.where(inside, entries, 0.0)


def eigen_np(elements):
    modes = np.arange(elements)
    cosine = np.cos(np.pi * modes / elements)
    return np.where(modes > 0, 3.0 * (1.0 - cosine) / (4.0 + 2.0 * cosine), 1.0)


def split_np(matrix, axis):
    high = matrix.astype(np.float32).astype(ml_dtypes.bfloat16)
    low = (matrix - high.astype(np.float64)).astype(np.float32).astype(ml_dtypes.bfloat16)
    return np.concatenate([high, high, low], axis=axis)


def lhs_np(matrix):
    return split_np(pad_np(matrix, round_up(matrix.shape[0], 16), matrix.shape[1]), 1)


def rhs_np(matrix):
    return split_np(matrix, 0)


def pad_np(matrix, rows, columns, value=0.0):
    out = np.full((rows, columns), value)
    out[: matrix.shape[0], : matrix.shape[1]] = matrix
    return out


class Line:
    def __init__(self, elements, stiffness, weights, eigen_basis, points):
        self.elements = elements
        self.nodes = 7 * elements
        around, masses = assemble(elements + 4, stiffness, weights)
        self.around, self.masses, self.shift = around, masses, 14
        self.forward = np.zeros((10 * elements, self.nodes + 3))
        self.backward = np.zeros((self.nodes, 10 * elements))
        for e in range(elements):
            self.forward[10 * e : 10 * e + 10, 7 * e : 7 * e + 10] = eigen_basis.T
            self.backward[7 * e : 7 * e + 7, 10 * e : 10 * e + 10] = eigen_basis[1:8]
        hats = injection_coefficients(elements + 4, points)
        kept = slice(self.shift, self.shift + self.nodes)
        rows = slice(1, 1 + elements + 2)
        full = np.zeros((hats.shape[0], self.around.shape[0]))
        full[:, : hats.shape[1]] = hats
        self.hats = hats[rows, kept]
        self.hats_stiff = (full @ around)[rows, kept]
        self.hats_mass = (full * masses)[rows, kept]

    def stiff(self, i, j):
        return self.around[i + self.shift, j + self.shift]

    def mass(self, i):
        return self.masses[i + self.shift]

    def values(self, side):
        n = self.nodes
        return {-1: [-1], 0: list(range(n)), 1: [n, n + 1]}[side]

    def sums(self, side):
        n = self.nodes
        return {-1: [-1, 0], 0: [], 1: [n, n + 1]}[side]


def segments(lines, with_sums):
    line_x, line_y = lines
    out, start = [], 0
    for dx, dy in DIRECTIONS:
        rows = [("v", i, j) for i in line_x.values(dx) for j in line_y.values(dy)]
        if with_sums:
            rows += [("x", i, j) for i in line_x.sums(dx) for j in line_y.values(dy)]
            rows += [("y", i, j) for i in line_x.values(dx) for j in line_y.sums(dy)]
        size = round_up(len(rows), 8)
        out.append((start, size, rows))
        start += size
    return out, start


def tables(mesh_x, mesh_y, shape):
    points, weights, stiffness = lobatto_tables()
    eigen_basis, eigen_vals = schwarz_basis()
    nx, ny, nz = shape
    ex, ey, ez = nx // 7, ny // 7, nz // 7
    line_x = Line(ex, stiffness, weights, eigen_basis, points)
    line_y = Line(ey, stiffness, weights, eigen_basis, points)
    lines = (line_x, line_y)
    pitch = round_up(ny, 8)
    own_rows = round_up(nx * pitch, 16)
    zl = round_up(nz, 128)
    half_z = ez // 2
    assert ez % 2 == 0 and 10 * half_z <= 256 and zl >= 256
    cl = 512
    windows = [0, zl - 256]
    coefs = 100 * ex * ey
    own = lambda i, j: i * pitch + j
    own_list = [(i, j) for i in range(nx) for j in range(ny)]
    t = {}
    dims = dict(nx=nx, ny=ny, nz=nz, pitch=pitch, own_rows=own_rows, zl=zl, windows=windows)

    forward = lambda i, j: np.kron(line_x.forward[:, i + 1], line_y.forward[:, j + 1])
    seg_b, rows_b = segments(lines, False)
    seg_d, rows_d = segments(lines, True)
    rows_d = round_up(rows_d, 16)
    dims.update(seg_b=[s[:2] for s in seg_b], rows_b=rows_b)
    dims.update(seg_d=[s[:2] for s in seg_d], rows_d=rows_d)

    pick = np.zeros((rows_b, own_rows))
    w_halo = np.zeros((coefs, rows_b))
    for (dx, dy), (start, size, rows) in zip(DIRECTIONS, seg_b):
        for r, (kind, i, j) in enumerate(rows):
            pick[start + r, own(i - nx * dx, j - ny * dy)] = 1.0
            w_halo[:, start + r] = forward(i, j)
    w_own = np.zeros((coefs, own_rows))
    back = np.zeros((own_rows, coefs))
    for i, j in own_list:
        w_own[:, own(i, j)] = forward(i, j)
        back[own(i, j)] = np.kron(line_x.backward[i], line_y.backward[j])
    z_fwd = np.zeros((zl, cl))
    z_back = np.zeros((cl, zl))
    l_z = np.ones(cl)
    for e in range(ez):
        lane = 256 * (e // half_z) + 10 * (e % half_z)
        l_z[lane : lane + 10] = eigen_vals
        for m in range(10):
            z = 7 * e - 1 + m
            if 0 < z < nz:
                z_fwd[z, lane : lane + 10] = eigen_basis[m]
                if 1 <= m <= 7:
                    z_back[lane : lane + 10, z] = eigen_basis[m]
    l_x, l_y = np.tile(eigen_vals, ex), np.tile(eigen_vals, ey)
    inverse = 1.0 / ((l_x[:, None] + l_y[None, :]).reshape(coefs, 1) + l_z)

    def window(matrix, c):
        kept = matrix[windows[c] : windows[c] + 256, 256 * c : 256 * c + 256]
        assert np.count_nonzero(kept) == np.count_nonzero(matrix[:, 256 * c : 256 * c + 256])
        return kept

    t["pick"] = pick.astype(ml_dtypes.bfloat16)
    t["z_fwd"] = np.stack([rhs_np(window(z_fwd, c)) for c in range(2)])
    t["w_own"] = lhs_np(w_own)
    t["coarse_b"] = None
    t["to_modes"] = None
    t["w_halo"] = lhs_np(w_halo)
    t["inverse"] = inverse.astype(np.float32)
    t["send_m"] = None
    t["z_back"] = np.stack([rhs_np(window(z_back.T, c).T) for c in range(2)])
    t["back"] = lhs_np(back)

    send = np.zeros((rows_d, own_rows))
    wide_y = ny + 3
    points_rows = round_up((nx + 3) * wide_y, 16)
    target = lambda i, j: (i + 1) * wide_y + (j + 1)
    inside_x = lambda i: -1 <= i <= nx + 1
    inside_y = lambda j: -1 <= j <= ny + 1
    lap_own = np.zeros((2 * points_rows, own_rows))
    lap_halo = np.zeros((2 * points_rows, rows_d))

    def value_column(column, i, j, dx, dy):
        for k in range(-1, nx + 2):
            if k not in line_x.sums(dx):
                column[target(k, j)] += line_x.stiff(k, i) * line_y.mass(j)
        for k in range(-1, ny + 2):
            if k not in line_y.sums(dy):
                column[target(i, k)] += line_y.stiff(k, j) * line_x.mass(i)
        column[points_rows + target(i, j)] += line_x.mass(i) * line_y.mass(j)

    for i, j in own_list:
        value_column(lap_own[:, own(i, j)], i, j, 0, 0)
    for (dx, dy), (start, size, rows) in zip(DIRECTIONS, seg_d):
        for r, (kind, i, j) in enumerate(rows):
            p, q = i - nx * dx, j - ny * dy
            if kind == "v":
                send[start + r, own(p, q)] = 1.0
                value_column(lap_halo[:, start + r], i, j, dx, dy)
            elif kind == "x":
                for k in range(nx):
                    send[start + r, own(k, q)] = line_x.stiff(p, k)
                lap_halo[target(i, j), start + r] += line_y.mass(j)
            else:
                for k in range(ny):
                    send[start + r, own(p, k)] = line_y.stiff(q, k)
                lap_halo[target(i, j), start + r] += line_x.mass(i)
    w_all = np.zeros((coefs, points_rows))
    for i in range(-1, nx + 2):
        for j in range(-1, ny + 2):
            w_all[:, target(i, j)] = forward(i, j)
    masked_backs = []
    for first_x in (0, 1):
        for first_y in (0, 1):
            masked = back.copy()
            for i, j in own_list:
                if (first_x and i == 0) or (first_y and j == 0):
                    masked[own(i, j)] = 0.0
            masked_backs.append(masked)
    t["send_m"] = np.stack([lhs_np(send @ masked / theta_cheb) for masked in masked_backs])
    stiff_z, mass_z = assemble(ez, stiffness, weights)
    stiff_z = pad_np(stiff_z[:nz, :nz], zl, zl)
    mass_z = np.diag(pad_np(mass_z[None, :nz], 1, zl)[0])
    both_z = [mass_z @ z_fwd, stiff_z @ z_fwd]
    t["z_lap"] = np.stack(
        [rhs_np(np.concatenate([window(matrix, c) for matrix in both_z], 1)) for c in range(2)]
    )
    t["lap_own"], t["lap_halo"] = [], []
    for place_x in range(3):
        for place_y in range(3):
            inner = np.zeros(points_rows)
            for i in range(-1, nx + 2):
                for j in range(-1, ny + 2):
                    out_x = (place_x == 0 and i <= 0) or (place_x == 2 and i >= nx)
                    out_y = (place_y == 0 and j <= 0) or (place_y == 2 and j >= ny)
                    inner[target(i, j)] = 0.0 if out_x or out_y else 1.0
            masked = w_all * inner
            for name, lap in (("lap_own", lap_own), ("lap_halo", lap_halo)):
                pair = [masked @ lap[:points_rows], masked @ lap[points_rows:]]
                pair = np.concatenate(pair, 1)
                t[name].append(lhs_np(pair)[:, pair.shape[1] :])
    t["lap_own"], t["lap_halo"] = np.stack(t["lap_own"]), np.stack(t["lap_halo"])

    count_x, count_y = mesh_x * ex, mesh_y * ey
    vx, vy = ex + 2, ey + 2
    assert vx == 4 and vy == 4 and count_y % 4 == 0
    half_y = count_y // 2
    dims.update(count_x=count_x, half_y=half_y, lanes=half_y * LANES)
    coarse = np.zeros((3, 16, own_rows))
    for i, j in own_list:
        for w in range(vy):
            for v in range(vx):
                row = 4 * w + v
                coarse[0, row, own(i, j)] = line_x.hats[v, i] * line_y.hats[w, j]
                coarse[1, row, own(i, j)] = (
                    line_x.hats_stiff[v, i] * line_y.hats_mass[w, j]
                    + line_x.hats_mass[v, i] * line_y.hats_stiff[w, j]
                )
                coarse[2, row, own(i, j)] = line_x.hats_mass[v, i] * line_y.hats_mass[w, j]
    t["coarse_b"] = lhs_np(coarse[0])
    coarse_m = [
        lhs_np(np.concatenate([coarse[1] @ masked, coarse[2] @ masked])) for masked in masked_backs
    ]
    t["coarse_m"] = np.stack(coarse_m)
    hats_z = injection_coefficients(ez, points)[:ez]
    phi_z = sine_np(np.arange(ez), ez)
    to_modes = pad_np(hats_z.T @ phi_z, zl, LANES)
    to_modes[0] = 0.0
    t["to_modes"] = rhs_np(np.tile(to_modes, (1, 2)))
    m_modes = np.concatenate([z_back @ mass_z @ to_modes, z_back @ stiff_z @ to_modes])
    t["m_modes"] = rhs_np(np.tile(m_modes, (1, 2)))
    y_in = np.zeros((mesh_y, count_y, 2, 4, 2, LANES))
    y_out = np.zeros((mesh_y, 8, half_y * LANES))
    for p in range(mesh_y):
        inward = sine_np(p * ey - 1 + np.arange(vy), count_y)
        outward = sine_np(p * ey + np.arange(ey + 1), count_y)
        for w in range(vy):
            y_in[p, :, w % 2, :, w // 2, :] = inward[w][:, None, None]
        for q in range(ey + 1):
            for h in range(2):
                y_out[p, 2 * q + h] = np.repeat(outward[q, h * half_y : (h + 1) * half_y], LANES)
    t["y_in"] = y_in.reshape(mesh_y * count_y * 8, 2 * LANES).astype(np.float32)
    x_in = np.zeros((2, count_x, mesh_x, 2, 4))
    x_out = np.zeros((mesh_x, 2, 8, 2, count_x))
    for p in range(mesh_x):
        for h in range(2):
            x_in[h, :, p, h] = sine_np(p * ex - 1 + np.arange(vx), count_x).T
            x_out[p, h, : ex + 1, h] = sine_np(p * ex + np.arange(ex + 1), count_x)
    t["x_in"] = lhs_np(x_in.reshape(2 * count_x, mesh_x * 8))
    mu = np.ones((count_x, count_y, LANES))
    mu[:, :, :ez] = (
        eigen_np(count_x)[:, None, None] + eigen_np(count_y)[None, :, None] + eigen_np(ez)
    )
    mu = mu.reshape(count_x, 2, half_y * LANES).transpose(1, 0, 2)
    t["mu"] = (1.0 / mu).reshape(2 * count_x, half_y * LANES).astype(np.float32)
    t["x_out"] = np.stack([lhs_np(x_out[p].reshape(16, 2 * count_x)) for p in range(mesh_x)])
    t["y_out"] = y_out.astype(np.float32)
    z_out = np.zeros((LANES, zl + 128))
    z_out[:ez, :nz] = phi_z.T @ hats_z
    z_out[:, 0] = 0.0
    z_out[:ez, zl : zl + ez] = phi_z.T
    t["z_out"] = rhs_np(np.tile(z_out, (2, 1)))
    spread = np.zeros((own_rows, 8 * (ey + 1)))
    hats_x, hats_y = line_x.hats[1:], line_y.hats[1:]
    for i, j in own_list:
        for q in range(ey + 1):
            for p in range(ex + 1):
                spread[own(i, j), 8 * q + p] = hats_x[p, i] * hats_y[q, j]
    return t, dims, lhs_np(spread)


def halves(value):
    high = value.astype(jnp.bfloat16)
    return high, (value - high.astype(jnp.float32)).astype(jnp.bfloat16)


def mm(a, b):
    return jnp.dot(a, b, preferred_element_type=jnp.float32)


def left(table, value):
    high, low = halves(value)
    return mm(table, jnp.concatenate([high, low, high], axis=0))


def left_two(table, value):
    high, low = halves(value)
    both = mm(table, jnp.concatenate([high, high], axis=0))
    return both + mm(table[:, : value.shape[0]], low)


def right(value, table):
    high, low = halves(value)
    return mm(jnp.concatenate([high, low, high], axis=1), table)


def to_coefs(value, table, windows):
    high, low = halves(value)
    out = []
    for c, start in enumerate(windows):
        near = slice(start, start + 256)
        out.append(mm(jnp.concatenate([high[:, near], low[:, near], high[:, near]], 1), table[c]))
    count = out[0].shape[1] // 256
    rows = [
        jnp.concatenate([part[:, 256 * n : 256 * n + 256] for part in out], 1) for n in range(count)
    ]
    return rows[0] if count == 1 else jnp.concatenate(rows, 0)


def from_coefs(value, table, windows, zl):
    total = None
    for c, start in enumerate(windows):
        part = right(value[:, 256 * c : 256 * c + 256], table[c])
        sides = [jnp.zeros((part.shape[0], n), part.dtype) for n in (start, zl - start - 256) if n]
        part = jnp.concatenate([part] + sides if start == 0 else sides + [part], axis=1)
        total = part if total is None else total + part
    return total


PER_DEVICE = ("send_m", "lap_own", "lap_halo", "coarse_m", "x_out", "y_out")


def kernel(names, dims, mesh_x, mesh_y, residual, *refs):
    count = len(names)
    far = dict(zip(names, refs[:count]))
    near = dict(zip(names, refs[count + 2 : 2 * count + 2]))
    total_out, nodes_out = refs[count : count + 2]
    (block, own, out_b, in_b, out_d, in_d, out_y, in_y, out_x, in_x,
     local, loaded, sent, got, sent_y, got_y, sent_x, got_x) = refs[2 * count + 2 :]
    nx, ny, nz, pitch = dims["nx"], dims["ny"], dims["nz"], dims["pitch"]
    own_rows, zl, windows = dims["own_rows"], dims["zl"], dims["windows"]
    ix, iy = lax.axis_index("gx"), lax.axis_index("gy")
    def exists(dx, dy):
        return (ix + dx >= 0) & (ix + dx < mesh_x) & (iy + dy >= 0) & (iy + dy < mesh_y)

    residual_in = pltpu.make_async_copy(residual, block, local.at[0])
    residual_in.start()
    in_b[...] = jnp.zeros_like(in_b)
    in_d[...] = jnp.zeros_like(in_d)
    barrier = pltpu.get_barrier_semaphore()

    def greet_x(o):
        to = lax.rem(ix + o, mesh_x)
        pl.semaphore_signal(barrier, inc=1, device_id=(to, iy), device_id_type=MESH)

    def greet_y(o):
        to = lax.rem(iy + o, mesh_y)
        pl.semaphore_signal(barrier, inc=1, device_id=(ix, to), device_id_type=MESH)

    near_x, near_y = sorted({1, mesh_x - 1}), sorted({1, mesh_y - 1})
    for o in near_y:
        greet_y(o)
    for o in near_x:
        greet_x(o)
    corners = DIRECTIONS[4:]
    for dx, dy in corners:
        @pl.when(exists(dx, dy))
        def _():
            pl.semaphore_signal(barrier, inc=1, device_id=(ix + dx, iy + dy), device_id_type=MESH)

    start_of_grid = 2 * (ix == 0).astype(jnp.int32) + (iy == 0).astype(jnp.int32)
    for o in range(2, mesh_y - 1):
        greet_y(o)
    for o in range(2, mesh_x - 1):
        greet_x(o)
    own[...] = jnp.zeros_like(own)
    place_x = 1 - (ix == 0).astype(jnp.int32) + (ix == mesh_x - 1).astype(jnp.int32)
    place_y = 1 - (iy == 0).astype(jnp.int32) + (iy == mesh_y - 1).astype(jnp.int32)
    in_grid = 3 * place_x + place_y
    place = dict(send_m=start_of_grid, lap_own=in_grid, lap_halo=in_grid)
    place.update(coarse_m=start_of_grid, x_out=ix, y_out=iy)
    loads = {}
    for n, name in enumerate(names):
        src = far[name].at[place[name]] if name in place else far[name]
        loads[name] = pltpu.make_async_copy(src, near[name], loaded.at[n])

    later = names.index("back")
    for name in names[:later]:
        loads[name].start()

    def table(name):
        if name in loads:
            loads.pop(name).wait()
        return near[name][...]

    row = lax.broadcasted_iota(jnp.int32, (own_rows, 1), 0)
    node_x, node_y = ix * nx + row // pitch, iy * ny + row % pitch
    keep = ((node_x > 0) & (node_y > 0) & (row % pitch < ny) & (row // pitch < nx)).astype(
        jnp.float32
    )
    residual_in.wait()
    for i in range(nx):
        own[i * pitch : i * pitch + ny, 0:nz] = block[i]
    source = own[...] * keep
    high, low = halves(source)
    pick = table("pick")
    out_b[...] = mm(pick, high) + mm(pick, low)

    greetings = mesh_x - 1 + mesh_y - 1
    for dx, dy in corners:
        greetings = greetings + exists(dx, dy).astype(jnp.int32)
    pl.semaphore_wait(barrier, greetings)

    def halo(phase, src, dst, places):
        copies = []
        for d, (dx, dy) in enumerate(DIRECTIONS):
            start, size = places[d]
            copies.append(
                pltpu.make_async_remote_copy(
                    src_ref=src.at[pl.ds(start, size)],
                    dst_ref=dst.at[pl.ds(start, size)],
                    send_sem=sent.at[phase, d],
                    recv_sem=got.at[phase, d],
                    device_id=(ix - dx, iy - dy),
                    device_id_type=MESH,
                )
            )
        for d in (2, 3, 4, 5, 6, 7, 0, 1):
            dx, dy = DIRECTIONS[d]
            pl.when(exists(-dx, -dy))(copies[d].start)
        return copies

    def arrived(copies):
        for d, (dx, dy) in enumerate(DIRECTIONS):
            pl.when(exists(dx, dy))(copies[d].wait_recv)

    def left_here(copies):
        for d, (dx, dy) in enumerate(DIRECTIONS):
            pl.when(exists(-dx, -dy))(copies[d].wait_send)

    copies_b = halo(0, out_b, in_b, dims["seg_b"])
    for name in names[later:]:
        loads[name].start()
    z_fwd = table("z_fwd")
    coefs = left(table("w_own"), to_coefs(source, z_fwd, windows))
    coarse_b = right(left(table("coarse_b"), source), table("to_modes"))
    arrived(copies_b)
    coefs = coefs + left(table("w_halo"), to_coefs(in_b[...], z_fwd, windows))
    modes_0 = coefs * table("inverse")
    z_back = table("z_back")
    out_d[...] = from_coefs(left(table("send_m"), modes_0), z_back, windows, zl)
    copies_d = halo(1, out_d, in_d, dims["seg_d"])
    first = from_coefs(left(table("back"), modes_0), z_back, windows, zl)
    first = first * (keep * (1.0 / theta_cheb))
    z_lap = table("z_lap")
    coefs = coefs - left_two(table("lap_own"), to_coefs(first, z_lap, windows))
    sigma = theta_cheb / delta_cheb
    rho_0 = 1.0 / sigma
    rho_1 = 1.0 / (2.0 * sigma - rho_0)
    weight_0, weight_1 = (1.0 + rho_1 * rho_0) / theta_cheb, 2.0 * rho_1 / delta_cheb
    inverse = weight_1 * table("inverse")
    modes = weight_0 * modes_0 + coefs * inverse
    arrived(copies_d)
    rest = left_two(table("lap_halo"), to_coefs(in_d[...], z_lap, windows))
    modes = modes - rest * inverse

    lanes = dims["lanes"]
    shares = left(table("coarse_m"), modes)
    shares = jnp.concatenate([shares[:16], shares[16:]], axis=1)
    share = coarse_b - right(shares, table("m_modes"))
    lower_lanes = lax.broadcasted_iota(jnp.int32, (8, 128), 1) < LANES
    lower_rows = lax.broadcasted_iota(jnp.int32, (8, 128), 0) < 4
    share = jnp.where(lower_lanes, share[:8], share[8:])

    def everyone(value, src, dst, count, me, send_sems, recv_sems, place):
        src[...] = value
        copies = []
        for o in range(1, count):
            to = lax.rem(me + o, count)
            copies.append(
                pltpu.make_async_remote_copy(
                    src_ref=src,
                    dst_ref=dst.at[me],
                    send_sem=send_sems.at[o],
                    recv_sem=recv_sems.at[o],
                    device_id=place(to),
                    device_id_type=MESH,
                )
            )
        for copy in copies:
            copy.start()
        dst[me] = value
        return copies

    def all_here(copies):
        for copy in copies:
            copy.wait_recv()

    copies_y = everyone(
        share, out_y, in_y, mesh_y, iy, sent_y, got_y, lambda to: (ix, to)
    )
    total = left(table("back"), modes)
    all_here(copies_y)
    half = dims["half_y"]
    y_in = table("y_in").reshape(mesh_y, 2 * half * 8, 128)
    tiles = []
    for b in range(2 * half):
        tile = sum(in_y[p] * y_in[p, 8 * b : 8 * b + 8] for p in range(mesh_y))
        tile = tile + pltpu.roll(tile, LANES, 1)
        tiles.append(tile + pltpu.roll(tile, 4, 0))
    blocks = []
    for b in range(0, half, 2):
        lower = jnp.where(lower_lanes, tiles[b], tiles[b + 1])
        upper = jnp.where(lower_lanes, tiles[half + b], tiles[half + b + 1])
        blocks.append(jnp.where(lower_rows, lower, upper))
    share = jnp.concatenate(blocks, axis=1)
    copies_x = everyone(
        share, out_x, in_x, mesh_x, ix, sent_x, got_x, lambda to: (to, iy)
    )
    own[...] = from_coefs(total, z_back, windows, zl) * keep
    total_copy = pltpu.make_async_copy(own, total_out, local.at[1])
    total_copy.start()
    all_here(copies_x)
    gathered = in_x[...].reshape(mesh_x * 8, lanes)
    scaled = left(table("x_in"), gathered) * table("mu")
    lines = left(table("x_out"), scaled)
    y_out = table("y_out")
    by_row = []
    for q in range(ny // 7 + 1):
        line = lines[:8] * y_out[2 * q : 2 * q + 1] + lines[8:] * y_out[2 * q + 1 : 2 * q + 2]
        by_row.append(sum(line[:, 128 * b : 128 * b + 128] for b in range(lanes // 128)))
    nodes_out[...] = right(jnp.concatenate(by_row, axis=0), table("z_out"))
    total_copy.wait()
    left_here(copies_b)
    left_here(copies_d)
    for copy in copies_y + copies_x:
        copy.wait_send()


def finish(dims, spread, total, nodes, fine_out, coarse_out):
    nx, ny, nz, pitch, zl = dims["nx"], dims["ny"], dims["nz"], dims["pitch"], dims["zl"]
    ix, iy = lax.axis_index("gx"), lax.axis_index("gy")
    row = lax.broadcasted_iota(jnp.int32, (dims["own_rows"], 1), 0)
    keep = (ix * nx + row // pitch > 0) & (iy * ny + row % pitch > 0)
    values = nodes[...]
    for p in range(nx // 7):
        for q in range(ny // 7):
            line = values[8 * q + p : 8 * q + p + 1, zl : zl + nz // 7]
            coarse_out[p, q : q + 1, :] = line
    prolonged = left(spread[...], values[:, :zl])
    result = total[...] + prolonged * keep.astype(jnp.float32)
    for i in range(nx):
        fine_out[i] = result[i * pitch : i * pitch + ny, :nz]


def per_device(mesh_x, mesh_y, residual_in):
    t, dims, spread = tables(mesh_x, mesh_y, residual_in.shape)
    names = list(t)
    nx, ny, nz = residual_in.shape
    own_rows, zl, lanes = dims["own_rows"], dims["zl"], dims["lanes"]
    f32 = jnp.float32
    vmem = pl.BlockSpec(memory_space=pltpu.VMEM)
    total, nodes = pl.pallas_call(
        functools.partial(kernel, names, dims, mesh_x, mesh_y),
        out_shape=(
            jax.ShapeDtypeStruct((own_rows, zl), f32),
            jax.ShapeDtypeStruct((8 * (ny // 7 + 1), zl + 128), f32),
        ),
        in_specs=[pl.BlockSpec(memory_space=pl.ANY)] * (1 + len(names)),
        out_specs=(pl.BlockSpec(memory_space=pl.ANY), vmem),
        scratch_shapes=[
            pltpu.VMEM(t[name].shape[name in PER_DEVICE :], t[name].dtype) for name in names
        ]
        + [
            pltpu.VMEM((nx, ny, nz), f32),
            pltpu.VMEM((own_rows, zl), f32),
            pltpu.VMEM((dims["rows_b"], zl), f32),
            pltpu.VMEM((dims["rows_b"], zl), f32),
            pltpu.VMEM((dims["rows_d"], zl), f32),
            pltpu.VMEM((dims["rows_d"], zl), f32),
            pltpu.VMEM((8, 128), f32),
            pltpu.VMEM((mesh_y, 8, 128), f32),
            pltpu.VMEM((8, lanes), f32),
            pltpu.VMEM((mesh_x, 8, lanes), f32),
            pltpu.SemaphoreType.DMA((2,)),
            pltpu.SemaphoreType.DMA((len(names),)),
            pltpu.SemaphoreType.DMA((2, 8)),
            pltpu.SemaphoreType.DMA((2, 8)),
            pltpu.SemaphoreType.DMA((mesh_y,)),
            pltpu.SemaphoreType.DMA((mesh_y,)),
            pltpu.SemaphoreType.DMA((mesh_x,)),
            pltpu.SemaphoreType.DMA((mesh_x,)),
        ],
        compiler_params=pltpu.CompilerParams(
            collective_id=0, has_side_effects=True, vmem_limit_bytes=56 * 2**20
        ),
        cost_estimate=pl.CostEstimate(flops=10**9, bytes_accessed=10**7, transcendentals=0),
    )(residual_in, *[jnp.asarray(t[name]) for name in names])
    return pl.pallas_call(
        functools.partial(finish, dims),
        out_shape=(
            jax.ShapeDtypeStruct((nx, ny, nz), f32),
            jax.ShapeDtypeStruct((nx // 7, ny // 7, nz // 7), f32),
        ),
        in_specs=[vmem] * 3,
        out_specs=(vmem, vmem),
        compiler_params=pltpu.CompilerParams(vmem_limit_bytes=56 * 2**20),
        cost_estimate=pl.CostEstimate(flops=10**7, bytes_accessed=10**6, transcendentals=0),
    )(jnp.asarray(spread), total, nodes)


def solution(mesh):
    return jax.shard_map(
        functools.partial(per_device, mesh.shape["gx"], mesh.shape["gy"]),
        mesh=mesh,
        in_specs=(P("gx", "gy", None),),
        out_specs=(P("gx", "gy", None), P("gx", "gy", None)),
        check_vma=False,
    )
```

```python
import functools
import math

import jax
import jax.numpy as jnp
import ml_dtypes
import numpy as np
from jax import lax
from jax.experimental import pallas as pl
from jax.experimental.pallas import tpu as pltpu
from jax.sharding import PartitionSpec as P

theta_cheb = 1.125
delta_cheb = 0.875
start_points = [
    -0.8717401485096066,
    -0.5917001814331423,
    -0.2092992179024789,
    0.2092992179024789,
    0.5917001814331423,
    0.8717401485096066,
]


def legendre_pair(value):
    before, now = (1.0, value)
    for order in range(1, 7):
        before, now = (now, ((2 * order + 1) * value * now - order * before) / (order + 1))
    return (now, before)


def lobatto_tables():
    point_list = [-1.0]
    for guess in start_points:
        place = guess
        for newton in range(4):
            seventh, sixth = legendre_pair(place)
            slope = 7.0 * (place * seventh - sixth) / (place * place - 1.0)
            curve = (2.0 * place * slope - 56.0 * seventh) / (1.0 - place * place)
            place = place - slope / curve
        point_list.append(place)
    point_list.append(1.0)
    sample_nodes_list = np.array(point_list)
    values = np.array([legendre_pair(place)[0] for place in point_list])
    weights = 2.0 / (56.0 * values * values)
    derivative = np.zeros((8, 8))
    for i in range(8):
        for j in range(8):
            if i != j:
                derivative[i, j] = values[i] / (
                    values[j] * (sample_nodes_list[i] - sample_nodes_list[j])
                )
    derivative[0, 0] = -14.0
    derivative[7, 7] = 14.0
    stiffness = derivative.T @ (weights[:, None] * derivative)
    return (sample_nodes_list, weights, stiffness)


def assemble(elements, stiffness, weights):
    width = 7 * elements + 1
    assembled = np.zeros((width, width))
    masses = np.zeros(width)
    for e in range(elements):
        assembled[7 * e : 7 * e + 8, 7 * e : 7 * e + 8] += stiffness
        masses[7 * e : 7 * e + 8] += weights
    return (assembled, masses)


def jacobi_eigen(matrix):
    order = matrix.shape[0]
    work = [[float(matrix[i, j]) for j in range(order)] for i in range(order)]
    vectors = [[1.0 if i == j else 0.0 for j in range(order)] for i in range(order)]
    for sweep in range(12):
        for p in range(order):
            for q in range(p + 1, order):
                angle = 0.5 * math.atan2(2.0 * work[p][q], work[q][q] - work[p][p])
                cosine = math.cos(angle)
                sine = math.sin(angle)
                for k in range(order):
                    left, right = (work[k][p], work[k][q])
                    work[k][p] = cosine * left - sine * right
                    work[k][q] = sine * left + cosine * right
                for k in range(order):
                    left, right = (work[p][k], work[q][k])
                    work[p][k] = cosine * left - sine * right
                    work[q][k] = sine * left + cosine * right
                for k in range(order):
                    left, right = (vectors[k][p], vectors[k][q])
                    vectors[k][p] = cosine * left - sine * right
                    vectors[k][q] = sine * left + cosine * right
    return (np.array([work[i][i] for i in range(order)]), np.array(vectors))


def schwarz_basis():
    sample_nodes_list, weights, stiffness = lobatto_tables()
    assembled, masses = assemble(3, stiffness, weights)
    block_stiff = assembled[6:16, 6:16]
    inv_root = 1.0 / np.sqrt(masses[6:16])
    eigen_vals, eigen_vecs = jacobi_eigen(inv_root[:, None] * block_stiff * inv_root[None, :])
    return (inv_root[:, None] * eigen_vecs, eigen_vals)


def injection_coefficients(elements, sample_nodes_list):
    matrix = np.zeros((elements + 1, 7 * elements))
    for e in range(elements):
        for m in range(7):
            matrix[e, 7 * e + m] += (1.0 - sample_nodes_list[m]) / 2.0
            matrix[e + 1, 7 * e + m] += (1.0 + sample_nodes_list[m]) / 2.0
    return matrix


MESH = pl.DeviceIdType.MESH
LANES = 64
DIRECTIONS = [(-1, 0), (1, 0), (0, -1), (0, 1), (-1, -1), (-1, 1), (1, -1), (1, 1)]


def round_up(value, unit):
    return -(-value // unit) * unit


def sine_np(vertices, elements):
    modes = np.arange(elements)
    vertex = np.asarray(vertices)[:, None]
    entries = np.sqrt(2.0 / elements) * np.sin(np.pi * (vertex * modes % (2 * elements)) / elements)
    entries = entries / np.sqrt((4.0 + 2.0 * np.cos(np.pi * modes / elements)) / 3.0)
    inside = (modes > 0) & (vertex > 0) & (vertex < elements)
    return np.where(inside, entries, 0.0)


def eigen_np(elements):
    modes = np.arange(elements)
    cosine = np.cos(np.pi * modes / elements)
    return np.where(modes > 0, 3.0 * (1.0 - cosine) / (4.0 + 2.0 * cosine), 1.0)


def split_np(matrix, axis):
    high = matrix.astype(np.float32).astype(ml_dtypes.bfloat16)
    low = (matrix - high.astype(np.float64)).astype(np.float32).astype(ml_dtypes.bfloat16)
    return np.concatenate([high, high, low], axis=axis)


def lhs_np(matrix):
    return split_np(pad_np(matrix, round_up(matrix.shape[0], 16), matrix.shape[1]), 1)


def rhs_np(matrix):
    return split_np(matrix, 0)


def pad_np(matrix, rows, columns, value=0.0):
    out = np.full((rows, columns), value)
    out[: matrix.shape[0], : matrix.shape[1]] = matrix
    return out


class Line:
    def __init__(self, elements, stiffness, weights, eigen_basis, points):
        self.elements = elements
        self.nodes = 7 * elements
        around, masses = assemble(elements + 4, stiffness, weights)
        self.around, self.masses, self.shift = around, masses, 14
        self.forward = np.zeros((10 * elements, self.nodes + 3))
        self.backward = np.zeros((self.nodes, 10 * elements))
        for e in range(elements):
            self.forward[10 * e : 10 * e + 10, 7 * e : 7 * e + 10] = eigen_basis.T
            self.backward[7 * e : 7 * e + 7, 10 * e : 10 * e + 10] = eigen_basis[1:8]
        hats = injection_coefficients(elements + 4, points)
        kept = slice(self.shift, self.shift + self.nodes)
        rows = slice(1, 1 + elements + 2)
        full = np.zeros((hats.shape[0], self.around.shape[0]))
        full[:, : hats.shape[1]] = hats
        self.hats = hats[rows, kept]
        self.hats_stiff = (full @ around)[rows, kept]
        self.hats_mass = (full * masses)[rows, kept]

    def stiff(self, i, j):
        return self.around[i + self.shift, j + self.shift]

    def mass(self, i):
        return self.masses[i + self.shift]

    def values(self, side):
        n = self.nodes
        return {-1: [-1], 0: list(range(n)), 1: [n, n + 1]}[side]

    def sums(self, side):
        n = self.nodes
        return {-1: [-1, 0], 0: [], 1: [n, n + 1]}[side]


def segments(lines, with_sums):
    line_x, line_y = lines
    out, start = [], 0
    for dx, dy in DIRECTIONS:
        rows = [("v", i, j) for i in line_x.values(dx) for j in line_y.values(dy)]
        if with_sums:
            rows += [("x", i, j) for i in line_x.sums(dx) for j in line_y.values(dy)]
            rows += [("y", i, j) for i in line_x.values(dx) for j in line_y.sums(dy)]
        size = round_up(len(rows), 8)
        out.append((start, size, rows))
        start += size
    return out, start


def tables(mesh_x, mesh_y, shape):
    points, weights, stiffness = lobatto_tables()
    eigen_basis, eigen_vals = schwarz_basis()
    nx, ny, nz = shape
    ex, ey, ez = nx // 7, ny // 7, nz // 7
    line_x = Line(ex, stiffness, weights, eigen_basis, points)
    line_y = Line(ey, stiffness, weights, eigen_basis, points)
    lines = (line_x, line_y)
    pitch = round_up(ny, 8)
    own_rows = round_up(nx * pitch, 16)
    zl = round_up(nz, 128)
    half_z = ez // 2
    assert ez % 2 == 0 and 10 * half_z <= 256 and zl >= 256
    cl = 512
    windows = [0, zl - 256]
    coefs = 100 * ex * ey
    own = lambda i, j: i * pitch + j
    own_list = [(i, j) for i in range(nx) for j in range(ny)]
    t = {}
    dims = dict(nx=nx, ny=ny, nz=nz, pitch=pitch, own_rows=own_rows, zl=zl, windows=windows)

    forward = lambda i, j: np.kron(line_x.forward[:, i + 1], line_y.forward[:, j + 1])
    seg_b, rows_b = segments(lines, False)
    seg_d, rows_d = segments(lines, True)
    rows_d = round_up(rows_d, 16)
    dims.update(seg_b=[s[:2] for s in seg_b], rows_b=rows_b)
    dims.update(seg_d=[s[:2] for s in seg_d], rows_d=rows_d)

    pick = np.zeros((rows_b, own_rows))
    w_halo = np.zeros((coefs, rows_b))
    for (dx, dy), (start, size, rows) in zip(DIRECTIONS, seg_b):
        for r, (kind, i, j) in enumerate(rows):
            pick[start + r, own(i - nx * dx, j - ny * dy)] = 1.0
            w_halo[:, start + r] = forward(i, j)
    w_own = np.zeros((coefs, own_rows))
    back = np.zeros((own_rows, coefs))
    for i, j in own_list:
        w_own[:, own(i, j)] = forward(i, j)
        back[own(i, j)] = np.kron(line_x.backward[i], line_y.backward[j])
    z_fwd = np.zeros((zl, cl))
    z_back = np.zeros((cl, zl))
    l_z = np.ones(cl)
    for e in range(ez):
        lane = 256 * (e // half_z) + 10 * (e % half_z)
        l_z[lane : lane + 10] = eigen_vals
        for m in range(10):
            z = 7 * e - 1 + m
            if 0 < z < nz:
                z_fwd[z, lane : lane + 10] = eigen_basis[m]
                if 1 <= m <= 7:
                    z_back[lane : lane + 10, z] = eigen_basis[m]
    l_x, l_y = np.tile(eigen_vals, ex), np.tile(eigen_vals, ey)
    inverse = 1.0 / ((l_x[:, None] + l_y[None, :]).reshape(coefs, 1) + l_z)

    def window(matrix, c):
        kept = matrix[windows[c] : windows[c] + 256, 256 * c : 256 * c + 256]
        assert np.count_nonzero(kept) == np.count_nonzero(matrix[:, 256 * c : 256 * c + 256])
        return kept

    t["pick"] = pick.astype(ml_dtypes.bfloat16)
    t["z_fwd"] = np.stack([rhs_np(window(z_fwd, c)) for c in range(2)])
    t["w_own"] = lhs_np(w_own)
    t["coarse_b"] = None
    t["to_modes"] = None
    t["w_halo"] = lhs_np(w_halo)
    t["inverse"] = inverse.astype(np.float32)
    t["send_m"] = None
    t["z_back"] = np.stack([rhs_np(window(z_back.T, c).T) for c in range(2)])
    t["back"] = lhs_np(back)

    send = np.zeros((rows_d, own_rows))
    wide_y = ny + 3
    points_rows = round_up((nx + 3) * wide_y, 16)
    target = lambda i, j: (i + 1) * wide_y + (j + 1)
    inside_x = lambda i: -1 <= i <= nx + 1
    inside_y = lambda j: -1 <= j <= ny + 1
    lap_own = np.zeros((2 * points_rows, own_rows))
    lap_halo = np.zeros((2 * points_rows, rows_d))

    def value_column(column, i, j, dx, dy):
        for k in range(-1, nx + 2):
            if k not in line_x.sums(dx):
                column[target(k, j)] += line_x.stiff(k, i) * line_y.mass(j)
        for k in range(-1, ny + 2):
            if k not in line_y.sums(dy):
                column[target(i, k)] += line_y.stiff(k, j) * line_x.mass(i)
        column[points_rows + target(i, j)] += line_x.mass(i) * line_y.mass(j)

    for i, j in own_list:
        value_column(lap_own[:, own(i, j)], i, j, 0, 0)
    for (dx, dy), (start, size, rows) in zip(DIRECTIONS, seg_d):
        for r, (kind, i, j) in enumerate(rows):
            p, q = i - nx * dx, j - ny * dy
            if kind == "v":
                send[start + r, own(p, q)] = 1.0
                value_column(lap_halo[:, start + r], i, j, dx, dy)
            elif kind == "x":
                for k in range(nx):
                    send[start + r, own(k, q)] = line_x.stiff(p, k)
                lap_halo[target(i, j), start + r] += line_y.mass(j)
            else:
                for k in range(ny):
                    send[start + r, own(p, k)] = line_y.stiff(q, k)
                lap_halo[target(i, j), start + r] += line_x.mass(i)
    w_all = np.zeros((coefs, points_rows))
    for i in range(-1, nx + 2):
        for j in range(-1, ny + 2):
            w_all[:, target(i, j)] = forward(i, j)
    masked_backs = []
    for first_x in (0, 1):
        for first_y in (0, 1):
            masked = back.copy()
            for i, j in own_list:
                if (first_x and i == 0) or (first_y and j == 0):
                    masked[own(i, j)] = 0.0
            masked_backs.append(masked)
    t["send_m"] = np.stack([lhs_np(send @ masked / theta_cheb) for masked in masked_backs])
    stiff_z, mass_z = assemble(ez, stiffness, weights)
    stiff_z = pad_np(stiff_z[:nz, :nz], zl, zl)
    mass_z = np.diag(pad_np(mass_z[None, :nz], 1, zl)[0])
    both_z = [mass_z @ z_fwd, stiff_z @ z_fwd]
    t["z_lap"] = np.stack(
        [rhs_np(np.concatenate([window(matrix, c) for matrix in both_z], 1)) for c in range(2)]
    )
    t["lap_own"], t["lap_halo"] = [], []
    for place_x in range(3):
        for place_y in range(3):
            inner = np.zeros(points_rows)
            for i in range(-1, nx + 2):
                for j in range(-1, ny + 2):
                    out_x = (place_x == 0 and i <= 0) or (place_x == 2 and i >= nx)
                    out_y = (place_y == 0 and j <= 0) or (place_y == 2 and j >= ny)
                    inner[target(i, j)] = 0.0 if out_x or out_y else 1.0
            masked = w_all * inner
            for name, lap in (("lap_own", lap_own), ("lap_halo", lap_halo)):
                pair = [masked @ lap[:points_rows], masked @ lap[points_rows:]]
                pair = np.concatenate(pair, 1)
                t[name].append(lhs_np(pair)[:, pair.shape[1] :])
    t["lap_own"], t["lap_halo"] = np.stack(t["lap_own"]), np.stack(t["lap_halo"])

    count_x, count_y = mesh_x * ex, mesh_y * ey
    vx, vy = ex + 2, ey + 2
    assert vx == 4 and vy == 4 and count_y % 4 == 0
    half_y = count_y // 2
    dims.update(count_x=count_x, half_y=half_y, lanes=half_y * LANES)
    coarse = np.zeros((3, 16, own_rows))
    for i, j in own_list:
        for w in range(vy):
            for v in range(vx):
                row = 4 * w + v
                coarse[0, row, own(i, j)] = line_x.hats[v, i] * line_y.hats[w, j]
                coarse[1, row, own(i, j)] = (
                    line_x.hats_stiff[v, i] * line_y.hats_mass[w, j]
                    + line_x.hats_mass[v, i] * line_y.hats_stiff[w, j]
                )
                coarse[2, row, own(i, j)] = line_x.hats_mass[v, i] * line_y.hats_mass[w, j]
    t["coarse_b"] = lhs_np(coarse[0])
    coarse_m = [
        lhs_np(np.concatenate([coarse[1] @ masked, coarse[2] @ masked])) for masked in masked_backs
    ]
    t["coarse_m"] = np.stack(coarse_m)
    hats_z = injection_coefficients(ez, points)[:ez]
    phi_z = sine_np(np.arange(ez), ez)
    to_modes = pad_np(hats_z.T @ phi_z, zl, LANES)
    to_modes[0] = 0.0
    t["to_modes"] = rhs_np(np.tile(to_modes, (1, 2)))
    m_modes = np.concatenate([z_back @ mass_z @ to_modes, z_back @ stiff_z @ to_modes])
    t["m_modes"] = rhs_np(np.tile(m_modes, (1, 2)))
    y_in = np.zeros((mesh_y, count_y, 2, 4, 2, LANES))
    y_out = np.zeros((mesh_y, 8, half_y * LANES))
    for p in range(mesh_y):
        inward = sine_np(p * ey - 1 + np.arange(vy), count_y)
        outward = sine_np(p * ey + np.arange(ey + 1), count_y)
        for w in range(vy):
            y_in[p, :, w % 2, :, w // 2, :] = inward[w][:, None, None]
        for q in range(ey + 1):
            for h in range(2):
                y_out[p, 2 * q + h] = np.repeat(outward[q, h * half_y : (h + 1) * half_y], LANES)
    t["y_in"] = y_in.reshape(mesh_y * count_y * 8, 2 * LANES).astype(np.float32)
    x_in = np.zeros((2, count_x, mesh_x, 2, 4))
    x_out = np.zeros((mesh_x, 2, 8, 2, count_x))
    for p in range(mesh_x):
        for h in range(2):
            x_in[h, :, p, h] = sine_np(p * ex - 1 + np.arange(vx), count_x).T
            x_out[p, h, : ex + 1, h] = sine_np(p * ex + np.arange(ex + 1), count_x)
    t["x_in"] = lhs_np(x_in.reshape(2 * count_x, mesh_x * 8))
    mu = np.ones((count_x, count_y, LANES))
    mu[:, :, :ez] = (
        eigen_np(count_x)[:, None, None] + eigen_np(count_y)[None, :, None] + eigen_np(ez)
    )
    mu = mu.reshape(count_x, 2, half_y * LANES).transpose(1, 0, 2)
    t["mu"] = (1.0 / mu).reshape(2 * count_x, half_y * LANES).astype(np.float32)
    t["x_out"] = np.stack([lhs_np(x_out[p].reshape(16, 2 * count_x)) for p in range(mesh_x)])
    t["y_out"] = y_out.astype(np.float32)
    z_out = np.zeros((LANES, zl + 128))
    z_out[:ez, :nz] = phi_z.T @ hats_z
    z_out[:, 0] = 0.0
    z_out[:ez, zl : zl + ez] = phi_z.T
    t["z_out"] = rhs_np(np.tile(z_out, (2, 1)))
    spread = np.zeros((own_rows, 8 * (ey + 1)))
    hats_x, hats_y = line_x.hats[1:], line_y.hats[1:]
    for i, j in own_list:
        for q in range(ey + 1):
            for p in range(ex + 1):
                spread[own(i, j), 8 * q + p] = hats_x[p, i] * hats_y[q, j]
    return t, dims, lhs_np(spread)


def halves(value):
    high = value.astype(jnp.bfloat16)
    return high, (value - high.astype(jnp.float32)).astype(jnp.bfloat16)


def mm(a, b):
    return jnp.dot(a, b, preferred_element_type=jnp.float32)


def left(table, value):
    high, low = halves(value)
    return mm(table, jnp.concatenate([high, low, high], axis=0))


def left_two(table, value):
    high, low = halves(value)
    both = mm(table, jnp.concatenate([high, high], axis=0))
    return both + mm(table[:, : value.shape[0]], low)


def right(value, table):
    high, low = halves(value)
    return mm(jnp.concatenate([high, low, high], axis=1), table)


def to_coefs(value, table, windows):
    high, low = halves(value)
    out = []
    for c, start in enumerate(windows):
        near = slice(start, start + 256)
        out.append(mm(jnp.concatenate([high[:, near], low[:, near], high[:, near]], 1), table[c]))
    count = out[0].shape[1] // 256
    rows = [
        jnp.concatenate([part[:, 256 * n : 256 * n + 256] for part in out], 1) for n in range(count)
    ]
    return rows[0] if count == 1 else jnp.concatenate(rows, 0)


def from_coefs(value, table, windows, zl):
    total = None
    for c, start in enumerate(windows):
        part = right(value[:, 256 * c : 256 * c + 256], table[c])
        sides = [jnp.zeros((part.shape[0], n), part.dtype) for n in (start, zl - start - 256) if n]
        part = jnp.concatenate([part] + sides if start == 0 else sides + [part], axis=1)
        total = part if total is None else total + part
    return total


PER_DEVICE = ("send_m", "lap_own", "lap_halo", "coarse_m", "x_out", "y_out")


def kernel(names, dims, mesh_x, mesh_y, residual, *refs):
    count = len(names)
    far = dict(zip(names, refs[:count]))
    near = dict(zip(names, refs[count + 2 : 2 * count + 2]))
    total_out, nodes_out = refs[count : count + 2]
    (block, own, out_b, in_b, out_d, in_d, out_y, in_y, out_x, in_x,
     local, loaded, sent, got, sent_y, got_y, sent_x, got_x) = refs[2 * count + 2 :]
    nx, ny, nz, pitch = dims["nx"], dims["ny"], dims["nz"], dims["pitch"]
    own_rows, zl, windows = dims["own_rows"], dims["zl"], dims["windows"]
    ix, iy = lax.axis_index("gx"), lax.axis_index("gy")
    def exists(dx, dy):
        return (ix + dx >= 0) & (ix + dx < mesh_x) & (iy + dy >= 0) & (iy + dy < mesh_y)

    residual_in = pltpu.make_async_copy(residual, block, local.at[0])
    residual_in.start()
    in_b[...] = jnp.zeros_like(in_b)
    in_d[...] = jnp.zeros_like(in_d)
    barrier = pltpu.get_barrier_semaphore()
    for o in range(1, mesh_x):
        pl.semaphore_signal(
            barrier, inc=1, device_id=(lax.rem(ix + o, mesh_x), iy), device_id_type=MESH
        )
    for o in range(1, mesh_y):
        pl.semaphore_signal(
            barrier, inc=1, device_id=(ix, lax.rem(iy + o, mesh_y)), device_id_type=MESH
        )
    corners = DIRECTIONS[4:]
    for dx, dy in corners:
        @pl.when(exists(dx, dy))
        def _():
            pl.semaphore_signal(barrier, inc=1, device_id=(ix + dx, iy + dy), device_id_type=MESH)

    start_of_grid = 2 * (ix == 0).astype(jnp.int32) + (iy == 0).astype(jnp.int32)
    own[...] = jnp.zeros_like(own)
    place_x = 1 - (ix == 0).astype(jnp.int32) + (ix == mesh_x - 1).astype(jnp.int32)
    place_y = 1 - (iy == 0).astype(jnp.int32) + (iy == mesh_y - 1).astype(jnp.int32)
    in_grid = 3 * place_x + place_y
    place = dict(send_m=start_of_grid, lap_own=in_grid, lap_halo=in_grid)
    place.update(coarse_m=start_of_grid, x_out=ix, y_out=iy)
    loads = {}
    for n, name in enumerate(names):
        src = far[name].at[place[name]] if name in place else far[name]
        loads[name] = pltpu.make_async_copy(src, near[name], loaded.at[n])

    later = names.index("w_own")
    for name in names[:later]:
        loads[name].start()

    def table(name):
        if name in loads:
            loads.pop(name).wait()
        return near[name][...]

    row = lax.broadcasted_iota(jnp.int32, (own_rows, 1), 0)
    node_x, node_y = ix * nx + row // pitch, iy * ny + row % pitch
    keep = ((node_x > 0) & (node_y > 0) & (row % pitch < ny) & (row // pitch < nx)).astype(
        jnp.float32
    )
    residual_in.wait()
    for i in range(nx):
        own[i * pitch : i * pitch + ny, 0:nz] = block[i]
    source = own[...] * keep
    high, low = halves(source)
    pick = table("pick")
    out_b[...] = mm(pick, high) + mm(pick, low)

    greetings = mesh_x - 1 + mesh_y - 1
    for dx, dy in corners:
        greetings = greetings + exists(dx, dy).astype(jnp.int32)
    pl.semaphore_wait(barrier, greetings)

    def halo(phase, src, dst, places):
        copies = []
        for d, (dx, dy) in enumerate(DIRECTIONS):
            start, size = places[d]
            copies.append(
                pltpu.make_async_remote_copy(
                    src_ref=src.at[pl.ds(start, size)],
                    dst_ref=dst.at[pl.ds(start, size)],
                    send_sem=sent.at[phase, d],
                    recv_sem=got.at[phase, d],
                    device_id=(ix - dx, iy - dy),
                    device_id_type=MESH,
                )
            )
        for d in (2, 3, 4, 5, 6, 7, 0, 1):
            dx, dy = DIRECTIONS[d]
            pl.when(exists(-dx, -dy))(copies[d].start)
        return copies

    def arrived(copies):
        for d, (dx, dy) in enumerate(DIRECTIONS):
            pl.when(exists(dx, dy))(copies[d].wait_recv)

    def left_here(copies):
        for d, (dx, dy) in enumerate(DIRECTIONS):
            pl.when(exists(-dx, -dy))(copies[d].wait_send)

    copies_b = halo(0, out_b, in_b, dims["seg_b"])
    for name in names[later:]:
        loads[name].start()
    z_fwd = table("z_fwd")
    coefs = left(table("w_own"), to_coefs(source, z_fwd, windows))
    coarse_b = right(left(table("coarse_b"), source), table("to_modes"))
    arrived(copies_b)
    coefs = coefs + left(table("w_halo"), to_coefs(in_b[...], z_fwd, windows))
    modes_0 = coefs * table("inverse")
    z_back = table("z_back")
    out_d[...] = from_coefs(left(table("send_m"), modes_0), z_back, windows, zl)
    copies_d = halo(1, out_d, in_d, dims["seg_d"])
    first = from_coefs(left(table("back"), modes_0), z_back, windows, zl)
    first = first * (keep * (1.0 / theta_cheb))
    z_lap = table("z_lap")
    coefs = coefs - left_two(table("lap_own"), to_coefs(first, z_lap, windows))
    arrived(copies_d)
    coefs = coefs - left_two(table("lap_halo"), to_coefs(in_d[...], z_lap, windows))
    sigma = theta_cheb / delta_cheb
    rho_0 = 1.0 / sigma
    rho_1 = 1.0 / (2.0 * sigma - rho_0)
    weight_0, weight_1 = (1.0 + rho_1 * rho_0) / theta_cheb, 2.0 * rho_1 / delta_cheb
    modes = weight_0 * modes_0 + weight_1 * (coefs * table("inverse"))

    lanes = dims["lanes"]
    shares = left(table("coarse_m"), modes)
    shares = jnp.concatenate([shares[:16], shares[16:]], axis=1)
    share = coarse_b - right(shares, table("m_modes"))
    lower_lanes = lax.broadcasted_iota(jnp.int32, (8, 128), 1) < LANES
    lower_rows = lax.broadcasted_iota(jnp.int32, (8, 128), 0) < 4
    share = jnp.where(lower_lanes, share[:8], share[8:])

    def everyone(value, src, dst, count, me, send_sems, recv_sems, place):
        src[...] = value
        copies = []
        for o in range(1, count):
            to = lax.rem(me + o, count)
            copies.append(
                pltpu.make_async_remote_copy(
                    src_ref=src,
                    dst_ref=dst.at[me],
                    send_sem=send_sems.at[o],
                    recv_sem=recv_sems.at[o],
                    device_id=place(to),
                    device_id_type=MESH,
                )
            )
        for copy in copies:
            copy.start()
        dst[me] = value
        return copies

    def all_here(copies):
        for copy in copies:
            copy.wait_recv()

    copies_y = everyone(
        share, out_y, in_y, mesh_y, iy, sent_y, got_y, lambda to: (ix, to)
    )
    total = left(table("back"), modes)
    all_here(copies_y)
    half = dims["half_y"]
    y_in = table("y_in").reshape(mesh_y, 2 * half * 8, 128)
    tiles = []
    for b in range(2 * half):
        tile = sum(in_y[p] * y_in[p, 8 * b : 8 * b + 8] for p in range(mesh_y))
        tile = tile + pltpu.roll(tile, LANES, 1)
        tiles.append(tile + pltpu.roll(tile, 4, 0))
    blocks = []
    for b in range(0, half, 2):
        lower = jnp.where(lower_lanes, tiles[b], tiles[b + 1])
        upper = jnp.where(lower_lanes, tiles[half + b], tiles[half + b + 1])
        blocks.append(jnp.where(lower_rows, lower, upper))
    share = jnp.concatenate(blocks, axis=1)
    copies_x = everyone(
        share, out_x, in_x, mesh_x, ix, sent_x, got_x, lambda to: (to, iy)
    )
    own[...] = from_coefs(total, z_back, windows, zl) * keep
    total_copy = pltpu.make_async_copy(own, total_out, local.at[1])
    total_copy.start()
    all_here(copies_x)
    gathered = in_x[...].reshape(mesh_x * 8, lanes)
    scaled = left(table("x_in"), gathered) * table("mu")
    lines = left(table("x_out"), scaled)
    y_out = table("y_out")
    by_row = []
    for q in range(ny // 7 + 1):
        line = lines[:8] * y_out[2 * q : 2 * q + 1] + lines[8:] * y_out[2 * q + 1 : 2 * q + 2]
        by_row.append(sum(line[:, 128 * b : 128 * b + 128] for b in range(lanes // 128)))
    nodes_out[...] = right(jnp.concatenate(by_row, axis=0), table("z_out"))
    total_copy.wait()
    left_here(copies_b)
    left_here(copies_d)
    for copy in copies_y + copies_x:
        copy.wait_send()


def finish(dims, spread, total, nodes, fine_out, coarse_out):
    nx, ny, nz, pitch, zl = dims["nx"], dims["ny"], dims["nz"], dims["pitch"], dims["zl"]
    ix, iy = lax.axis_index("gx"), lax.axis_index("gy")
    row = lax.broadcasted_iota(jnp.int32, (dims["own_rows"], 1), 0)
    keep = (ix * nx + row // pitch > 0) & (iy * ny + row % pitch > 0)
    values = nodes[...]
    for p in range(nx // 7):
        for q in range(ny // 7):
            line = values[8 * q + p : 8 * q + p + 1, zl : zl + nz // 7]
            coarse_out[p, q : q + 1, :] = line
    prolonged = left(spread[...], values[:, :zl])
    result = total[...] + prolonged * keep.astype(jnp.float32)
    for i in range(nx):
        fine_out[i] = result[i * pitch : i * pitch + ny, :nz]


def per_device(mesh_x, mesh_y, residual_in):
    t, dims, spread = tables(mesh_x, mesh_y, residual_in.shape)
    names = list(t)
    nx, ny, nz = residual_in.shape
    own_rows, zl, lanes = dims["own_rows"], dims["zl"], dims["lanes"]
    f32 = jnp.float32
    vmem = pl.BlockSpec(memory_space=pltpu.VMEM)
    total, nodes = pl.pallas_call(
        functools.partial(kernel, names, dims, mesh_x, mesh_y),
        out_shape=(
            jax.ShapeDtypeStruct((own_rows, zl), f32),
            jax.ShapeDtypeStruct((8 * (ny // 7 + 1), zl + 128), f32),
        ),
        in_specs=[pl.BlockSpec(memory_space=pl.ANY)] * (1 + len(names)),
        out_specs=(pl.BlockSpec(memory_space=pl.ANY), vmem),
        scratch_shapes=[
            pltpu.VMEM(t[name].shape[name in PER_DEVICE :], t[name].dtype) for name in names
        ]
        + [
            pltpu.VMEM((nx, ny, nz), f32),
            pltpu.VMEM((own_rows, zl), f32),
            pltpu.VMEM((dims["rows_b"], zl), f32),
            pltpu.VMEM((dims["rows_b"], zl), f32),
            pltpu.VMEM((dims["rows_d"], zl), f32),
            pltpu.VMEM((dims["rows_d"], zl), f32),
            pltpu.VMEM((8, 128), f32),
            pltpu.VMEM((mesh_y, 8, 128), f32),
            pltpu.VMEM((8, lanes), f32),
            pltpu.VMEM((mesh_x, 8, lanes), f32),
            pltpu.SemaphoreType.DMA((2,)),
            pltpu.SemaphoreType.DMA((len(names),)),
            pltpu.SemaphoreType.DMA((2, 8)),
            pltpu.SemaphoreType.DMA((2, 8)),
            pltpu.SemaphoreType.DMA((mesh_y,)),
            pltpu.SemaphoreType.DMA((mesh_y,)),
            pltpu.SemaphoreType.DMA((mesh_x,)),
            pltpu.SemaphoreType.DMA((mesh_x,)),
        ],
        compiler_params=pltpu.CompilerParams(
            collective_id=0, has_side_effects=True, vmem_limit_bytes=56 * 2**20
        ),
        cost_estimate=pl.CostEstimate(flops=10**9, bytes_accessed=10**7, transcendentals=0),
    )(residual_in, *[jnp.asarray(t[name]) for name in names])
    return pl.pallas_call(
        functools.partial(finish, dims),
        out_shape=(
            jax.ShapeDtypeStruct((nx, ny, nz), f32),
            jax.ShapeDtypeStruct((nx // 7, ny // 7, nz // 7), f32),
        ),
        in_specs=[vmem] * 3,
        out_specs=(vmem, vmem),
        compiler_params=pltpu.CompilerParams(vmem_limit_bytes=56 * 2**20),
        cost_estimate=pl.CostEstimate(flops=10**7, bytes_accessed=10**6, transcendentals=0),
    )(jnp.asarray(spread), total, nodes)


def solution(mesh):
    return jax.shard_map(
        functools.partial(per_device, mesh.shape["gx"], mesh.shape["gy"]),
        mesh=mesh,
        in_specs=(P("gx", "gy", None),),
        out_specs=(P("gx", "gy", None), P("gx", "gy", None)),
        check_vma=False,
    )
```
